32 devices in a mesh: leaf: 32 (over z, y, x, core).
Axes of the slice: x: 2, y: 2, z: 4, core: 2. Of those that a mesh axis runs over, the one named last changes fastest.
Arguments:
- solution: float32 [32, 98304], P(None, 'leaf'), may hold values from -6 to 6
- residual: float32 [32, 98304], P(None, 'leaf')
- direction: float32 [32, 98304], P(None, 'leaf')
- coordinates: float32 [3, 98304], P(None, 'leaf'), may hold values from 0 to 1
- cluster_order: int32 [98304], P('leaf'), may hold values from 0 to 3071, as said below
- leaf_sizes: int32 [32, 4], P('leaf'), may hold values from 1 to 1024, 3072 in all within a row
- leaf_basis: bfloat16 [128, 98304], P(None, 'leaf'), may hold values from -0.1875 to 0.1875
- node_transfer: bfloat16 [32, 7, 128, 128], P('leaf'), may hold values from -0.375 to 0.375
- node_coupling: bfloat16 [32, 7, 128, 128], P('leaf')
- upper_transfer: bfloat16 [32, 3, 128, 128], P('leaf'), as said below
- upper_coupling: bfloat16 [32, 4, 128, 128], P('leaf'), as said below
- lengthscale: float32 [1], replicated, may hold values from 0.15 to 0.4
- outputscale: float32 [1], replicated, may hold values from 0.05 to 0.2
- noise_variance: float32 [1], replicated, may hold values from 0.5 to 2
Outputs:
- new_solution: float32 [32, 98304], P(None, 'leaf')
- new_residual: float32 [32, 98304], P(None, 'leaf')
- new_direction: float32 [32, 98304], P(None, 'leaf')
The draws below stay inside these ranges and needn't reach their ends.
Inputs may be any that keep to these rules, and one draw needn't show every extreme that they name: `cluster_order`: each device's block of 3072 entries holds every number of 0 to 3071 once. `leaf_sizes`: each row sums to 3072 and its largest entry is 1024. `upper_transfer`: entry (d, j - 1) is the same for all devices d whose index divided by 2 to the power j is the same. `upper_coupling`: entry (d, j - 1) is the same for all devices d whose index divided by 2 to the power j is the same.
All inputs are finite; a program needn't handle non-finite values.
Results may differ from the reference program's by a relative error of at most 0.0003.
Values sent between devices are 32-bit elements; how exact they have to be, the bound alone decides.
No kernel may reach another device: no remote copies, remote signals or barrier semaphores. Data moves between devices by JAX's collectives and lax.ppermute only.
A program may use at most 64 MiB of HBM per device.

```python
import math
import jax
import jax.numpy as jnp
import numpy as np
from jax import lax

LEAF = 1024
R = 128
PROBES = 32
LEAF_DEV = 4
LOCAL = 2
LEVELS = 5
PTS_DEV = 3072
SUBTREES = 32
POINTS = 98304


def shared_scales(key, ratio_value):
    sub_keys = jax.random.split(key, 2)
    log_range = math.log(10.0)
    probe_scale = jnp.exp(jax.random.uniform(sub_keys[0], (PROBES, 1), jnp.float32, 0.0, log_range)) / math.sqrt(10.0)
    point_scale = jnp.exp(jax.random.uniform(sub_keys[1], (1, POINTS), jnp.float32, 0.0, log_range)) / math.sqrt(10.0)
    owner_index = (jnp.arange(POINTS) // PTS_DEV).astype(jnp.float32)
    ramp = jnp.sqrt((1.0 + (ratio_value - 1.0) * owner_index / (SUBTREES - 1)) * 2.0 / (1.0 + ratio_value))
    return probe_scale * point_scale * ramp[None, :]


def draw_residual(key, part):
    ratio_value = 3.0
    scales = shared_scales(key, ratio_value)
    key = jax.random.fold_in(key, 21)
    values = jax.random.normal(key, (PROBES, POINTS), jnp.float32)
    return values * scales


def draw_direction(key, part):
    ratio_value = 3.0
    scales = shared_scales(key, ratio_value)
    key = jax.random.fold_in(key, 22)
    values = jax.random.normal(key, (PROBES, POINTS), jnp.float32)
    return values * scales


def draw_cluster_order(key, part):
    key = jax.random.fold_in(key, 5)
    device_keys = jax.random.split(key, SUBTREES)
    blocks = jax.vmap(lambda one_key: jax.random.permutation(one_key, PTS_DEV))(device_keys)
    return blocks.reshape(POINTS).astype(jnp.int32)


def draw_node_coupling(key, part):
    key = jax.random.fold_in(key, 7)
    values = jax.random.normal(key, (SUBTREES, 2 * LEAF_DEV - 1, R, R), jnp.float32)
    heap_index = jnp.arange(2 * LEAF_DEV - 1) + 1
    depth_value = jnp.zeros((2 * LEAF_DEV - 1,), jnp.float32)
    for shift_index in range(1, LOCAL + 1):
        depth_value = depth_value + (heap_index >= 2 ** shift_index).astype(jnp.float32)
    height = LOCAL - depth_value
    scale_row = 0.5 * jnp.exp2(0.25 * height) / math.sqrt(R)
    return (values * scale_row[None, :, None, None]).astype(jnp.bfloat16)


def level_copies(key, level_count, base_scale, growth):
    tables = []
    for level_index in range(1, level_count + 1):
        groups = SUBTREES // 2 ** level_index
        values = jax.random.normal(jax.random.fold_in(key, level_index), (groups, R, R), jnp.float32)
        values = values * (base_scale * 2.0 ** (growth * (LOCAL + level_index)))
        tables.append(jnp.repeat(values, 2 ** level_index, axis=0))
    return jnp.stack(tables, axis=1)


def draw_upper_transfer(key, part):
    key = jax.random.fold_in(key, 9)
    return level_copies(key, LEVELS - 2, 1.0 / math.sqrt(2 * R), 0.0).astype(jnp.bfloat16)


def draw_upper_coupling(key, part):
    key = jax.random.fold_in(key, 13)
    return level_copies(key, LEVELS - 1, 0.5 / math.sqrt(R), 0.25).astype(jnp.bfloat16)


def level_of(key, dims, cuts, least, high):
    loudness = 1.0
    for axis_at, shards_of in cuts:
        heights = jax.random.uniform(jax.random.fold_in(jax.random.fold_in(key, 6), axis_at), (shards_of,), jnp.float32, least / len(cuts), high / len(cuts))
        loudness = loudness * jnp.repeat(jnp.exp(heights), dims[axis_at] // shards_of).reshape((-1,) + (1,) * (len(dims) - 1 - axis_at))
    return loudness


def length_profile(number_of, total, bound, slope):
    loads = [(1 << 20) // math.isqrt(rank ** slope) + 1 for rank in range(2, number_of + 1)]
    spare, holding = total - bound - (number_of - 1), [1] * (number_of - 1)
    while spare > 0:
        candidates = [i for i in range(number_of - 1) if holding[i] < bound]
        whole, remaining = sum([loads[i] for i in candidates]), spare
        for i in candidates:
            extra = min(bound - holding[i], max(1, remaining * loads[i] // whole), spare)
            holding[i] = holding[i] + extra
            spare = spare - extra
    return np.array([bound] + holding)


def ragged_sizes(own_key, amount, total, limit, slope):
    if amount == 2:
        one = jax.random.randint(own_key, (), max(1, total - limit), min(limit, total - 1) + 1)
        return jnp.stack([one, total - one])
    lengths = jnp.asarray(length_profile(amount, total, limit, slope), jnp.int32)
    couples = (amount - 1) // 2
    source_of, receiver = lengths[1:1 + 2 * couples:2], lengths[2:2 + 2 * couples:2]
    room = jnp.minimum(source_of - 1, limit - receiver)
    moved = jax.random.randint(jax.random.fold_in(own_key, 1), (couples,), 0, 1 << 20) % (room + 1)
    lengths = lengths.at[1:1 + 2 * couples:2].set(source_of - moved).at[2:2 + 2 * couples:2].set(receiver + moved)
    return lengths[jax.random.permutation(jax.random.fold_in(own_key, 2), amount)]


def gaussian(stream_key, dims, spread, limit, cuts=(), kind=jnp.bfloat16):
    loudness = level_of(stream_key, dims, cuts, -0.22, 0.18) if cuts else 1.0
    result = jax.random.normal(stream_key, dims, jnp.float32) * spread * loudness
    return jnp.minimum(jnp.maximum(result, -limit), limit).astype(kind)


def setup_inputs(seed: int = 0) -> dict:
    key_list = jax.random.split(jax.random.key(seed), 15)
    solution = gaussian(key_list[0], (PROBES, POINTS), 1.0, 6.0, ((1, 32),), jnp.float32)
    residual = draw_residual(jax.random.fold_in(key_list[14], 71), 0)
    direction = draw_direction(jax.random.fold_in(key_list[14], 71), 0)
    coordinates = jnp.clip(1.0 * jax.random.uniform(key_list[3], (3, POINTS), jnp.float32) ** level_of(key_list[3], (3, POINTS), ((1, 32),), -0.2, 0.2), 0.0, 1.0)
    cluster_order = draw_cluster_order(jax.random.fold_in(key_list[14], 71), 0)
    leaf_sizes = jax.vmap(lambda own: ragged_sizes(own, LEAF_DEV, PTS_DEV, LEAF, 1))(jax.random.split(key_list[5], SUBTREES)).reshape((SUBTREES, LEAF_DEV)).astype(jnp.int32)
    leaf_basis = gaussian(key_list[6], (R, POINTS), LEAF ** -0.5, 0.1875, ((1, 32),))
    node_transfer = gaussian(key_list[7], (SUBTREES, 2 * LEAF_DEV - 1, R, R), (2 * R) ** -0.5, 0.375, ((0, 32),))
    node_coupling = draw_node_coupling(jax.random.fold_in(key_list[14], 71), 0)
    upper_transfer = draw_upper_transfer(jax.random.fold_in(key_list[14], 71), 0)
    upper_coupling = draw_upper_coupling(jax.random.fold_in(key_list[14], 71), 0)
    lengthscale = jnp.clip(jnp.exp(jax.random.uniform(key_list[11], (1,), jnp.float32, math.log(0.15), math.log(0.4))), 0.15, 0.4)
    outputscale = jnp.clip(jnp.exp(jax.random.uniform(key_list[12], (1,), jnp.float32, math.log(0.05), math.log(0.2))), 0.05, 0.2)
    noise_variance = jnp.clip(jnp.exp(jax.random.uniform(key_list[13], (1,), jnp.float32, math.log(0.5), math.log(2.0))), 0.5, 2.0)
    return dict(solution=solution, residual=residual, direction=direction, coordinates=coordinates, cluster_order=cluster_order, leaf_sizes=leaf_sizes, leaf_basis=leaf_basis, node_transfer=node_transfer, node_coupling=node_coupling, upper_transfer=upper_transfer, upper_coupling=upper_coupling, lengthscale=lengthscale, outputscale=outputscale, noise_variance=noise_variance)


def exact_product(form, left, right):
    return jnp.einsum(form, left, right, precision=lax.Precision.HIGHEST)

def matern_block(points, lengthscale, outputscale):
    point_count = points.shape[1]
    squared = jnp.zeros((point_count, point_count), jnp.float32)
    for axis_index in range(3):
        gap_row = points[axis_index][:, None] - points[axis_index][None, :]
        squared = squared + gap_row * gap_row
    scaled = jnp.sqrt(5.0) * jnp.sqrt(squared) / lengthscale
    return outputscale * (1.0 + scaled + scaled * scaled / 3.0) * jnp.exp(-scaled)

def leaf_layout(sizes_row, points_dev):
    leaf_ends = jnp.cumsum(sizes_row).astype(jnp.int32)
    starts = (leaf_ends - sizes_row).astype(jnp.int32)
    first_rows = jnp.clip(starts, 0, points_dev - LEAF).astype(jnp.int32)
    positions = jnp.arange(points_dev, dtype=jnp.int32)
    leaf_of = lax.optimization_barrier(jnp.sum((positions[None, :] >= leaf_ends[:, None]).astype(jnp.int32), axis=0))
    return (first_rows, leaf_of)

def near_pass(direction, ordered, basis, first_rows, leaf_of, lengthscale, outputscale):
    leaf_count = first_rows.shape[0]

    def one_leaf(leaf_index, carry):
        near_sum, coeffs = carry
        first_row = first_rows[leaf_index]
        member = (lax.dynamic_slice_in_dim(leaf_of, first_row, LEAF, 0) == leaf_index).astype(jnp.float32)
        masked = lax.dynamic_slice_in_dim(direction, first_row, LEAF, 1) * member[None, :]
        kernel = matern_block(lax.dynamic_slice_in_dim(ordered, first_row, LEAF, 1), lengthscale, outputscale)
        applied = exact_product('pa,ab->pb', masked, kernel) * member[None, :]
        current = lax.dynamic_slice_in_dim(near_sum, first_row, LEAF, 1)
        near_sum = lax.dynamic_update_slice_in_dim(near_sum, current + applied, first_row, 1)
        window = lax.dynamic_slice_in_dim(basis, first_row, LEAF, 1).astype(jnp.float32)
        coeffs = coeffs.at[leaf_index].set(exact_product('pa,ra->pr', masked, window))
        return (near_sum, coeffs)
    initial = (jnp.zeros_like(direction), jnp.zeros((leaf_count, direction.shape[0], basis.shape[0]), jnp.float32))
    return lax.fori_loop(0, leaf_count, one_leaf, initial)

def far_pass(leaf_terms, basis, first_rows, leaf_of, template):

    def one_leaf(leaf_index, far_sum):
        first_row = first_rows[leaf_index]
        member = (lax.dynamic_slice_in_dim(leaf_of, first_row, LEAF, 0) == leaf_index).astype(jnp.float32)
        window = lax.dynamic_slice_in_dim(basis, first_row, LEAF, 1).astype(jnp.float32)
        added = exact_product('pr,ra->pa', leaf_terms[leaf_index], window) * member[None, :]
        current = lax.dynamic_slice_in_dim(far_sum, first_row, LEAF, 1)
        return lax.dynamic_update_slice_in_dim(far_sum, current + added, first_row, 1)
    return lax.fori_loop(0, leaf_terms.shape[0], one_leaf, jnp.zeros_like(template))

def climb_local(leaf_coeffs, transfers, couplings):
    current = leaf_coeffs
    parent_sums = []
    for depth_index in range(leaf_coeffs.shape[0].bit_length() - 1, 0, -1):
        first_node = 2 ** depth_index - 1
        node_count = 2 ** depth_index
        raised = exact_product('npa,nab->npb', current, transfers[first_node:first_node + node_count])
        sided = exact_product('npa,nab->npb', current, couplings[first_node:first_node + node_count])
        current = raised[0::2] + raised[1::2]
        parent_sums.insert(0, sided[0::2] + sided[1::2])
    return (current[0], parent_sums)

def descend_local(device_term, parent_sums, transfers, couplings):
    current = device_term[None]
    for depth_index in range(1, len(parent_sums) + 1):
        first_node = 2 ** depth_index - 1
        node_count = 2 ** depth_index
        inherited = jnp.repeat(current, 2, axis=0)
        sums_here = jnp.repeat(parent_sums[depth_index - 1], 2, axis=0)
        current = exact_product('npb,nab->npa', inherited, transfers[first_node:first_node + node_count]) + exact_product('npb,nab->npa', sums_here, couplings[first_node:first_node + node_count])
    return current

def reference(solution, residual, direction, coordinates, cluster_order, leaf_sizes, leaf_basis, node_transfer, node_coupling, upper_transfer, upper_coupling, lengthscale, outputscale, noise_variance):
    noise_level = noise_variance[0]
    direction_dev = direction.reshape(PROBES, SUBTREES, PTS_DEV).transpose(1, 0, 2)
    coords_dev = coordinates.reshape(3, SUBTREES, PTS_DEV).transpose(1, 0, 2)
    order_dev = cluster_order.reshape(SUBTREES, PTS_DEV)
    basis_dev = leaf_basis.reshape(R, SUBTREES, PTS_DEV).transpose(1, 0, 2)

    def lower_part(pieces):
        direction_one, coords_one, order_one, sizes_one, basis_one, transfer_one, coupling_one = pieces
        ordered = jnp.take(coords_one, order_one, axis=1)
        first_rows, leaf_of = leaf_layout(sizes_one, PTS_DEV)
        near_sum, leaf_coeffs = near_pass(direction_one, ordered, basis_one, first_rows, leaf_of, lengthscale[0], outputscale[0])
        device_coeff, local_sums = climb_local(leaf_coeffs, transfer_one.astype(jnp.float32), coupling_one.astype(jnp.float32))
        return (near_sum, device_coeff, tuple(local_sums))
    near_all, device_coeffs, local_sums_all = lax.map(lower_part, (direction_dev, coords_dev, order_dev, leaf_sizes, basis_dev, node_transfer, node_coupling))

    def level_generators(level_index):
        if level_index == 0:
            return (node_transfer[:, 0].astype(jnp.float32), node_coupling[:, 0].astype(jnp.float32))
        stride = 2 ** level_index
        coupling_level = upper_coupling[::stride, level_index - 1].astype(jnp.float32)
        transfer_level = None
        if level_index <= LEVELS - 2:
            transfer_level = upper_transfer[::stride, level_index - 1].astype(jnp.float32)
        return (transfer_level, coupling_level)
    level_coeffs = device_coeffs
    upper_sums = []
    for level_index in range(LEVELS):
        transfer_level, coupling_level = level_generators(level_index)
        sided = exact_product('gpa,gab->gpb', level_coeffs, coupling_level)
        upper_sums.append(sided[0::2] + sided[1::2])
        if level_index + 1 < LEVELS:
            raised = exact_product('gpa,gab->gpb', level_coeffs, transfer_level)
            level_coeffs = raised[0::2] + raised[1::2]
    downward = None
    for level_index in range(LEVELS - 1, -1, -1):
        transfer_level, coupling_level = level_generators(level_index)
        coupled = exact_product('gpb,gab->gpa', jnp.repeat(upper_sums[level_index], 2, axis=0), coupling_level)
        if level_index == LEVELS - 1:
            downward = coupled
        else:
            downward = exact_product('gpb,gab->gpa', jnp.repeat(downward, 2, axis=0), transfer_level) + coupled

    def upper_part(pieces):
        direction_one, sizes_one, basis_one, transfer_one, coupling_one, device_term, local_sums = pieces
        first_rows, leaf_of = leaf_layout(sizes_one, PTS_DEV)
        leaf_terms = descend_local(device_term, list(local_sums), transfer_one.astype(jnp.float32), coupling_one.astype(jnp.float32))
        return far_pass(leaf_terms, basis_one, first_rows, leaf_of, direction_one)
    far_all = lax.map(upper_part, (direction_dev, leaf_sizes, basis_dev, node_transfer, node_coupling, downward, local_sums_all))
    near = near_all.transpose(1, 0, 2).reshape(PROBES, POINTS)
    far = far_all.transpose(1, 0, 2).reshape(PROBES, POINTS)
    applied = noise_level * direction + near + far
    curvature = lax.optimization_barrier(jnp.sum(direction * applied, axis=1))
    norm_old = lax.optimization_barrier(jnp.sum(residual * residual, axis=1))
    step_size = norm_old / curvature
    new_solution = solution + step_size[:, None] * direction
    new_residual = residual - step_size[:, None] * applied
    norm_new = lax.optimization_barrier(jnp.sum(new_residual * new_residual, axis=1))
    new_direction = new_residual + (norm_new / norm_old)[:, None] * direction
    return (new_solution, new_residual, new_direction)
```

```python
import functools
import math

import jax
import jax.numpy as jnp
from jax import lax
from jax.experimental import pallas as pl
from jax.experimental.pallas import tpu as pltpu
from jax.sharding import PartitionSpec as P

F32 = jnp.float32
BF16 = jnp.bfloat16
TILE = 256
FAR_AWAY = 32768.0
LOG2E = 1.0 / math.log(2.0)
POLY = math.log(2.0) ** 2 / 3.0
LINEAR = 3.0 * LOG2E
CONSTANT = 3.0 * LOG2E * LOG2E

VMEM = pl.BlockSpec(memory_space=pltpu.VMEM)
SMEM = pl.BlockSpec(memory_space=pltpu.SMEM)
ANY = pl.BlockSpec(memory_space=pl.ANY)
PARAMS = pltpu.CompilerParams(vmem_limit_bytes=48 * 1024 * 1024)


def halves(x):
    high = x.astype(BF16)
    low = (x - high.astype(F32)).astype(BF16)
    return jnp.concatenate([high, low], axis=0)


def folded(x):
    rows = x.shape[0] // 2
    return x[:rows] + x[rows:]


def times(x, generator):
    return folded(jnp.dot(halves(x), generator, preferred_element_type=F32))


def times_transposed(x, generator):
    return folded(
        lax.dot_general(
            halves(x), generator, (((1,), (1,)), ((), ())), preferred_element_type=F32
        )
    )


def leaf_ends(sizes_ref, leaf_count):
    ends = []
    total = 0
    for leaf in range(leaf_count):
        total = total + sizes_ref[0, leaf]
        ends.append(total)
    return ends


def leaf_row(ends, first, shape):
    positions = lax.broadcasted_iota(jnp.int32, shape, 1) + first
    leaf = jnp.zeros(shape, jnp.int32)
    for end in ends[:-1]:
        leaf = leaf + (positions >= end).astype(jnp.int32)
    return leaf


def up_kernel(
    leaf_count,
    levels,
    sizes_ref,
    d_ref,
    basis_ref,
    nt_ref,
    nc_ref,
    ut_ref,
    uc_ref,
    up_ref,
    local_ref,
):
    probes, points = d_ref.shape
    ends = leaf_ends(sizes_ref, leaf_count)
    split = halves(d_ref[...])
    leaf = leaf_row(ends, 0, (2 * probes, points))
    zero = jnp.zeros_like(split)
    masked = jnp.concatenate(
        [jnp.where(leaf == index, split, zero) for index in range(leaf_count)], axis=0
    )
    raw = lax.dot_general(
        masked, basis_ref[...], (((1,), (1,)), ((), ())), preferred_element_type=F32
    )
    current = [
        folded(raw[2 * probes * index : 2 * probes * (index + 1)]) for index in range(leaf_count)
    ]
    rank = basis_ref.shape[0]
    while len(current) > 1:
        count = len(current)
        raised, sided = [], []
        for index in range(count):
            node = count - 1 + index
            both = jnp.concatenate([nt_ref[0, node], nc_ref[0, node]], axis=1)
            image = times(current[index], both)
            raised.append(image[:, :rank])
            sided.append(image[:, rank:])
        current = [raised[2 * i] + raised[2 * i + 1] for i in range(count // 2)]
        for i in range(count // 2):
            local_ref[count // 2 - 1 + i] = sided[2 * i] + sided[2 * i + 1]
    coefficient = current[0]
    for level in range(levels):
        coupling = nc_ref[0, 0] if level == 0 else uc_ref[0, level - 1]
        if level + 1 < levels:
            transfer = nt_ref[0, 0] if level == 0 else ut_ref[0, level - 1]
            image = times(coefficient, jnp.concatenate([transfer, coupling], axis=1))
            coefficient = image[:, :rank]
            up_ref[level] = image[:, rank:]
        else:
            up_ref[level] = times(coefficient, coupling)


def climb(sizes, direction, basis, node_transfer, node_coupling, upper_transfer, upper_coupling, levels):
    leaf_count = sizes.shape[1]
    probes, rank = direction.shape[0], basis.shape[0]
    return pl.pallas_call(
        functools.partial(up_kernel, leaf_count, levels),
        out_shape=(
            jax.ShapeDtypeStruct((levels, probes, rank), F32),
            jax.ShapeDtypeStruct((leaf_count - 1, probes, rank), F32),
        ),
        in_specs=[SMEM] + [VMEM] * 6,
        out_specs=(VMEM, VMEM),
        compiler_params=PARAMS,
        name="climb",
    )(sizes, direction, basis, node_transfer, node_coupling, upper_transfer, upper_coupling)


def features_kernel(
    leaf_count,
    sizes_ref,
    length_ref,
    coords_ref,
    order_ref,
    d_ref,
    after_ref,
    left_ref,
    right_ref,
    dd_ref,
    ordered_ref,
):
    points = coords_ref.shape[1]
    chunks = points // 128
    ordered_ref[...] = jnp.zeros_like(ordered_ref)
    for group in range(chunks // 8):
        order = order_ref[8 * group : 8 * group + 8, :]
        chunk_of = lax.shift_right_logical(order, 7)
        lane_of = lax.bitwise_and(order, 127)
        for axis in range(3):
            found = jnp.zeros((8, 128), F32)
            for chunk in range(chunks):
                source = jnp.broadcast_to(
                    coords_ref[axis : axis + 1, 128 * chunk : 128 * chunk + 128], (8, 128)
                )
                picked = jnp.take_along_axis(source, lane_of, axis=1)
                found = jnp.where(chunk_of == chunk, picked, found)
            for row in range(8):
                place = 128 * (8 * group + row)
                ordered_ref[axis : axis + 1, place : place + 128] = found[row : row + 1, :]
    row8 = lax.broadcasted_iota(jnp.int32, (8, points), 0)
    scale = jnp.full((1, 1), math.sqrt(5.0) * LOG2E, F32) / length_ref[0]
    scaled = jnp.where(row8 < 3, (ordered_ref[...] - 0.5) * scale, 0.0)
    z1 = scaled.astype(BF16).astype(F32)
    z2 = (scaled - z1).astype(BF16).astype(F32)
    kept = z1 + z2
    norm = jnp.broadcast_to(jnp.sum(kept * kept, axis=0, keepdims=True), (8, points))
    n1 = norm.astype(BF16).astype(F32)
    n2 = (norm - n1).astype(BF16).astype(F32)
    n3 = norm - n1 - n2
    ends = leaf_ends(sizes_ref, leaf_count)
    leaf = leaf_row(ends, 0, (8, points))
    parts = jnp.where(row8 % 3 == 0, n1, jnp.where(row8 % 3 == 1, n2, n3))
    norm_left = jnp.where(row8 < 3, parts, jnp.where(row8 < 6, 1.0, 0.0))
    norm_right = jnp.where(row8 < 3, 1.0, jnp.where(row8 < 6, parts, 0.0))
    same = leaf == row8
    leaf_left = jnp.where(same, 1.0, 0.0)
    leaf_right = jnp.where(same, 0.0, FAR_AWAY)
    left = jnp.concatenate(
        [-2.0 * z1, -2.0 * z1, -2.0 * z2, -2.0 * z2, norm_left, leaf_left]
        + [jnp.zeros((80, points), F32)],
        axis=0,
    )
    right = jnp.concatenate(
        [z1, z2, z1, z2, norm_right, leaf_right] + [jnp.zeros((80, points), F32)], axis=0
    )
    right_ref[...] = right.astype(BF16)
    left_ref[...] = left.T.astype(BF16)
    split = halves(d_ref[...]).astype(F32)
    split = jnp.concatenate([split, jnp.zeros((128 - split.shape[0], points), F32)], axis=0)
    dd_ref[...] = split.T.astype(BF16)


def features(sizes, lengthscale, coordinates, order, direction, after):
    leaf_count = sizes.shape[1]
    points = direction.shape[1]
    return pl.pallas_call(
        functools.partial(features_kernel, leaf_count),
        out_shape=(
            jax.ShapeDtypeStruct((points, 128), BF16),
            jax.ShapeDtypeStruct((128, points), BF16),
            jax.ShapeDtypeStruct((points, 128), BF16),
        ),
        in_specs=[SMEM, SMEM, VMEM, VMEM, VMEM, ANY],
        out_specs=(VMEM, VMEM, VMEM),
        scratch_shapes=[pltpu.VMEM((8, points), F32)],
        compiler_params=PARAMS,
        name="features",
    )(sizes, lengthscale, coordinates, order.reshape(-1, 128), direction, after)


def near_kernel(leaf_count, probes, first, sizes_ref, left_ref, right_ref, dd_ref, after_ref, out_ref):
    ends = leaf_ends(sizes_ref, leaf_count)
    count = out_ref.shape[1] // TILE

    def one_tile(step, carry):
        row = first + step
        begin = row * TILE
        last = begin + TILE - 1
        low = 0
        high = ends[-1]
        for end in ends:
            low = jnp.where(end <= begin, end, low)
        for end in ends[::-1]:
            high = jnp.where(end > last, end, high)
        left = left_ref[pl.ds(pl.multiple_of(begin, TILE), TILE), :]

        def one_block(block, total):
            place = pl.multiple_of(block * TILE, TILE)
            squared = jnp.dot(left, right_ref[:, pl.ds(place, TILE)], preferred_element_type=F32)
            squared = jnp.maximum(squared, 1e-12)
            root = squared * lax.rsqrt(squared)
            kernel = (squared + LINEAR * root + CONSTANT) * jnp.exp2(-root)
            high_part = kernel.astype(BF16)
            low_part = (kernel - high_part.astype(F32)).astype(BF16)
            weights = dd_ref[pl.ds(place, TILE), :]
            return (
                total
                + jnp.dot(high_part, weights, preferred_element_type=F32)
                + jnp.dot(low_part, weights, preferred_element_type=F32)
            )

        total = lax.fori_loop(
            lax.shift_right_logical(low, 8),
            lax.shift_right_logical(high - 1, 8) + 1,
            one_block,
            jnp.zeros((TILE, 128), F32),
        )
        flipped = total.T
        out_ref[:, pl.ds(pl.multiple_of(step * TILE, TILE), TILE)] = (
            flipped[:probes] + flipped[probes : 2 * probes]
        )
        return carry

    lax.fori_loop(0, count, one_tile, 0)


def near_part(sizes, left, right, dd, after, probes, first, count):
    leaf_count = sizes.shape[1]
    return pl.pallas_call(
        functools.partial(near_kernel, leaf_count, probes, first),
        out_shape=jax.ShapeDtypeStruct((probes, count * TILE), F32),
        in_specs=[SMEM, VMEM, VMEM, VMEM, ANY],
        out_specs=VMEM,
        compiler_params=PARAMS,
        name="near_part",
    )(sizes, left, right, dd, after)


def down_kernel(
    leaf_count,
    levels,
    parts,
    sizes_ref,
    noise_ref,
    scale_ref,
    d_ref,
    r_ref,
    basis_ref,
    nt_ref,
    nc_ref,
    ut_ref,
    uc_ref,
    local_ref,
    *rest,
):
    side_refs = rest[:levels]
    near_refs = rest[levels : levels + parts]
    a_ref, sums_ref = rest[levels + parts :]
    probes, points = d_ref.shape
    down = None
    for level in range(levels - 1, -1, -1):
        coupling = nc_ref[0, 0] if level == 0 else uc_ref[0, level - 1]
        side = side_refs[level][...]
        if down is None:
            down = times_transposed(side, coupling)
        else:
            transfer = nt_ref[0, 0] if level == 0 else ut_ref[0, level - 1]
            down = times_transposed(
                jnp.concatenate([down, side], axis=1),
                jnp.concatenate([transfer, coupling], axis=1),
            )
    current = [down]
    while len(current) < leaf_count:
        count = len(current)
        following = []
        for index in range(2 * count):
            node = 2 * count - 1 + index
            parent = index // 2
            following.append(
                times_transposed(
                    jnp.concatenate([current[parent], local_ref[count - 1 + parent]], axis=1),
                    jnp.concatenate([nt_ref[0, node], nc_ref[0, node]], axis=1),
                )
            )
        current = following
    stacked = jnp.concatenate([halves(term) for term in current], axis=0)
    ends = leaf_ends(sizes_ref, leaf_count)
    noise = noise_ref[0]
    near_scale = scale_ref[0] * POLY
    width = 512
    peak = jnp.zeros((probes, 128), F32)
    old = jnp.zeros((probes, 128), F32)
    curve = jnp.zeros((probes, 128), F32)
    per_part = near_refs[0].shape[1]

    def lanes(x):
        return sum(x[:, 128 * i : 128 * i + 128] for i in range(width // 128))

    for first in range(0, points, width):
        far_all = jnp.dot(
            stacked, basis_ref[:, first : first + width], preferred_element_type=F32
        )
        leaf = leaf_row(ends, first, (probes, width))
        far = folded(far_all[: 2 * probes])
        for index in range(1, leaf_count):
            term = folded(far_all[2 * probes * index : 2 * probes * (index + 1)])
            far = jnp.where(leaf == index, term, far)
        d = d_ref[:, first : first + width]
        r = r_ref[:, first : first + width]
        at = first % per_part
        near = near_refs[first // per_part][:, at : at + width]
        applied = noise * d + near_scale * near + far
        a_ref[:, first : first + width] = applied
        size = jnp.abs(applied)
        for i in range(width // 128):
            peak = jnp.maximum(peak, size[:, 128 * i : 128 * i + 128])
        old = old + lanes(r * r)
        curve = curve + lanes(d * applied)
    top = jnp.maximum(jnp.max(peak, axis=1, keepdims=True), 1e-30)
    inverse = 1.0 / top
    cross = jnp.zeros((probes, 128), F32)
    square = jnp.zeros((probes, 128), F32)
    for first in range(0, points, width):
        unit = a_ref[:, first : first + width] * inverse
        cross = cross + lanes(r_ref[:, first : first + width] * unit)
        square = square + lanes(unit * unit)
    lane = lax.broadcasted_iota(jnp.int32, (probes, 128), 1)
    sums = jnp.where(lane == 0, jnp.sum(old, axis=1, keepdims=True), 0.0)
    sums = jnp.where(lane == 1, jnp.sum(curve, axis=1, keepdims=True), sums)
    sums = jnp.where(lane == 2, jnp.sum(cross, axis=1, keepdims=True), sums)
    sums = jnp.where(lane == 3, jnp.sum(square, axis=1, keepdims=True), sums)
    sums_ref[...] = jnp.where(lane == 4, top, sums)


def descend(
    sizes, noise, scale, direction, residual, basis, node_transfer, node_coupling,
    upper_transfer, upper_coupling, local, sides, nears,
):
    leaf_count = sizes.shape[1]
    probes, points = direction.shape
    return pl.pallas_call(
        functools.partial(down_kernel, leaf_count, len(sides), len(nears)),
        out_shape=(
            jax.ShapeDtypeStruct((probes, points), F32),
            jax.ShapeDtypeStruct((probes, 128), F32),
        ),
        in_specs=[SMEM, SMEM, SMEM] + [VMEM] * (8 + len(sides) + len(nears)),
        out_specs=(VMEM, VMEM),
        compiler_params=PARAMS,
        name="descend",
    )(
        sizes, noise, scale, direction, residual, basis, node_transfer, node_coupling,
        upper_transfer, upper_coupling, local, *sides, *nears,
    )


def merged(pieces):
    tops = [piece[:, 4:5] for piece in pieces]
    top = functools.reduce(jnp.maximum, tops)
    lane = lax.broadcasted_iota(jnp.int32, pieces[0].shape, 1)
    total = jnp.zeros_like(pieces[0])
    for piece, own in zip(pieces, tops):
        ratio = own / top
        factor = jnp.where(lane < 2, 1.0, jnp.where(lane == 2, ratio, ratio * ratio))
        total = total + piece * factor
    return jnp.where(lane == 4, top, total)


def merge_kernel(*refs):
    refs[-1][...] = merged([ref[...] for ref in refs[:-1]])


def merge(pieces):
    return pl.pallas_call(
        merge_kernel,
        out_shape=jax.ShapeDtypeStruct(pieces[0].shape, F32),
        in_specs=[VMEM] * len(pieces),
        out_specs=VMEM,
        name="merge",
    )(*pieces)


def step_kernel(pieces, *refs):
    sums = merged([ref[...] for ref in refs[:pieces]])
    x_ref, r_ref, d_ref, a_ref, nx_ref, nr_ref, nd_ref = refs[pieces:]
    old, curve, cross, square, top = (sums[:, i : i + 1] for i in range(5))
    step = old / curve
    reach = step * top
    fresh = old - 2.0 * (reach * cross) + (reach * reach) * square
    beta = fresh / old
    d = d_ref[...]
    nx_ref[...] = x_ref[...] + step * d
    remaining = r_ref[...] - step * a_ref[...]
    nr_ref[...] = remaining
    nd_ref[...] = remaining + beta * d


def finish(pieces, solution_block, residual, direction, applied):
    shape = jax.ShapeDtypeStruct(direction.shape, F32)
    return pl.pallas_call(
        functools.partial(step_kernel, len(pieces)),
        out_shape=(shape, shape, shape),
        in_specs=[VMEM] * (len(pieces) + 4),
        out_specs=(VMEM, VMEM, VMEM),
        compiler_params=PARAMS,
        name="finish",
    )(*pieces, solution_block, residual, direction, applied)


def from_partner(array, stride):
    count = lax.axis_size("leaf")
    return lax.ppermute(array, "leaf", [(i, i ^ stride) for i in range(count)])


def level_groups(levels):
    groups = [[0]]
    level = 1
    while level < levels:
        groups.append(list(range(level, min(level + 2, levels))))
        level += 2
    return groups


def shards(
    solution,
    residual,
    direction,
    coordinates,
    cluster_order,
    leaf_sizes,
    leaf_basis,
    node_transfer,
    node_coupling,
    upper_transfer,
    upper_coupling,
    lengthscale,
    outputscale,
    noise_variance,
):
    levels = lax.axis_size("leaf").bit_length() - 1
    probes, points = direction.shape
    up, local = climb(
        leaf_sizes, direction, leaf_basis, node_transfer, node_coupling,
        upper_transfer, upper_coupling, levels,
    )
    left, right, dd = features(leaf_sizes, lengthscale, coordinates, cluster_order, direction, up)
    tiles = points // TILE
    groups = level_groups(levels)
    parts = 3
    per_part = tiles // parts
    sides = [None] * levels
    nears = []
    current = up
    for number, group in enumerate(groups):
        base = group[0]
        strides = [2**level for level in group]
        incoming = {}
        for pick in range(1, 2 ** len(group)):
            stride = sum(s for bit, s in enumerate(strides) if pick >> bit & 1)
            top = pick.bit_length() - 1
            incoming[pick] = from_partner(current[top:], stride)
        if number < parts:
            nears.append(
                near_part(leaf_sizes, left, right, dd, current, probes, number * per_part, per_part)
            )
        for position in range(len(group)):
            total = current[position]
            for pick in range(1, 2 ** (position + 1)):
                top = pick.bit_length() - 1
                total = total + incoming[pick][position - top]
            sides[base + position] = total
        following = current[len(group) :]
        if following.shape[0]:
            for pick in range(1, 2 ** len(group)):
                top = pick.bit_length() - 1
                following = following + incoming[pick][len(group) - top :]
        current = following
    for number in range(len(groups), parts):
        nears.append(
            near_part(leaf_sizes, left, right, dd, up, probes, number * per_part, per_part)
        )
    applied, sums = descend(
        leaf_sizes, noise_variance, outputscale, direction, residual, leaf_basis,
        node_transfer, node_coupling, upper_transfer, upper_coupling, local, sides, nears,
    )
    pieces = [sums]
    for group in groups:
        own = merge(pieces) if len(pieces) > 1 else pieces[0]
        pieces = [own]
        for pick in range(1, 2 ** len(group)):
            stride = sum(2**level for bit, level in enumerate(group) if pick >> bit & 1)
            pieces.append(from_partner(own, stride))
    return finish(pieces, solution, residual, direction, applied)


def solution(mesh):
    in_specs = (
        P(None, "leaf"),
        P(None, "leaf"),
        P(None, "leaf"),
        P(None, "leaf"),
        P("leaf"),
        P("leaf", None),
        P(None, "leaf"),
        P("leaf", None, None, None),
        P("leaf", None, None, None),
        P("leaf", None, None, None),
        P("leaf", None, None, None),
        P(),
        P(),
        P(),
    )
    out_specs = (P(None, "leaf"), P(None, "leaf"), P(None, "leaf"))
    return jax.shard_map(shards, mesh=mesh, in_specs=in_specs, out_specs=out_specs, check_vma=False)
```

```python
import functools
import math

import jax
import jax.numpy as jnp
from jax import lax
from jax.experimental import pallas as pl
from jax.experimental.pallas import tpu as pltpu
from jax.sharding import PartitionSpec as P

F32 = jnp.float32
BF16 = jnp.bfloat16
TILE = 256
FAR_AWAY = 32768.0
LOG2E = 1.0 / math.log(2.0)
POLY = math.log(2.0) ** 2 / 3.0
LINEAR = 3.0 * LOG2E
CONSTANT = 3.0 * LOG2E * LOG2E

VMEM = pl.BlockSpec(memory_space=pltpu.VMEM)
SMEM = pl.BlockSpec(memory_space=pltpu.SMEM)
ANY = pl.BlockSpec(memory_space=pl.ANY)
HBM = pl.BlockSpec(memory_space=pltpu.HBM)
GROUP = 4
PARAMS = pltpu.CompilerParams(vmem_limit_bytes=48 * 1024 * 1024)


def halves(x):
    high = x.astype(BF16)
    low = (x - high.astype(F32)).astype(BF16)
    return jnp.concatenate([high, low], axis=0)


def folded(x):
    rows = x.shape[0] // 2
    return x[:rows] + x[rows:]


def times(x, generator):
    return folded(jnp.dot(halves(x), generator, preferred_element_type=F32))


def times_transposed(x, generator):
    return folded(
        lax.dot_general(
            halves(x), generator, (((1,), (1,)), ((), ())), preferred_element_type=F32
        )
    )


def leaf_ends(sizes_ref, leaf_count):
    ends = []
    total = 0
    for leaf in range(leaf_count):
        total = total + sizes_ref[0, leaf]
        ends.append(total)
    return ends


def leaf_row(ends, first, shape):
    positions = lax.broadcasted_iota(jnp.int32, shape, 1) + first
    leaf = jnp.zeros(shape, jnp.int32)
    for end in ends[:-1]:
        leaf = leaf + (positions >= end).astype(jnp.int32)
    return leaf


def up_kernel(leaf_count, levels, *refs):
    sources, (up_ref, local_ref) = refs[:7], refs[7:9]
    held, semaphores = refs[9:16], refs[16]
    copies = [
        pltpu.make_async_copy(source, target, semaphores.at[index])
        for index, (source, target) in enumerate(zip(sources, held))
    ]
    for copy in copies:
        copy.start()
    for copy in copies:
        copy.wait()
    sizes_ref, d_ref, basis_ref, nt_ref, nc_ref, ut_ref, uc_ref = held
    probes, points = d_ref.shape
    ends = leaf_ends(sizes_ref, leaf_count)
    split = halves(d_ref[...])
    leaf = leaf_row(ends, 0, (2 * probes, points))
    zero = jnp.zeros_like(split)
    masked = jnp.concatenate(
        [jnp.where(leaf == index, split, zero) for index in range(leaf_count)], axis=0
    )
    raw = lax.dot_general(
        masked, basis_ref[...], (((1,), (1,)), ((), ())), preferred_element_type=F32
    )
    current = [
        folded(raw[2 * probes * index : 2 * probes * (index + 1)]) for index in range(leaf_count)
    ]
    rank = basis_ref.shape[0]
    while len(current) > 1:
        count = len(current)
        raised, sided = [], []
        for index in range(count):
            node = count - 1 + index
            both = jnp.concatenate([nt_ref[0, node], nc_ref[0, node]], axis=1)
            image = times(current[index], both)
            raised.append(image[:, :rank])
            sided.append(image[:, rank:])
        current = [raised[2 * i] + raised[2 * i + 1] for i in range(count // 2)]
        for i in range(count // 2):
            local_ref[count // 2 - 1 + i] = sided[2 * i] + sided[2 * i + 1]
    coefficient = current[0]
    for level in range(levels):
        coupling = nc_ref[0, 0] if level == 0 else uc_ref[0, level - 1]
        if level + 1 < levels:
            transfer = nt_ref[0, 0] if level == 0 else ut_ref[0, level - 1]
            image = times(coefficient, jnp.concatenate([transfer, coupling], axis=1))
            coefficient = image[:, :rank]
            up_ref[level] = image[:, rank:]
        else:
            up_ref[level] = times(coefficient, coupling)


def climb(sizes, direction, basis, node_transfer, node_coupling, upper_transfer, upper_coupling, levels):
    leaf_count = sizes.shape[1]
    probes, rank = direction.shape[0], basis.shape[0]
    return pl.pallas_call(
        functools.partial(up_kernel, leaf_count, levels),
        out_shape=(
            jax.ShapeDtypeStruct((levels, probes, rank), F32),
            jax.ShapeDtypeStruct((leaf_count - 1, probes, rank), F32),
        ),
        in_specs=[HBM] * 7,
        out_specs=(VMEM, VMEM),
        scratch_shapes=[pltpu.SMEM(sizes.shape, jnp.int32)]
        + [
            pltpu.VMEM(array.shape, array.dtype)
            for array in (
                direction, basis, node_transfer, node_coupling, upper_transfer, upper_coupling
            )
        ]
        + [pltpu.SemaphoreType.DMA((7,))],
        compiler_params=PARAMS,
        name="climb",
    )(sizes, direction, basis, node_transfer, node_coupling, upper_transfer, upper_coupling)


def features_kernel(
    leaf_count,
    sizes_ref,
    length_ref,
    coords_ref,
    order_ref,
    d_ref,
    after_ref,
    left_ref,
    right_ref,
    dd_ref,
    ordered_ref,
):
    points = coords_ref.shape[1]
    chunks = points // 128
    ordered_ref[...] = jnp.zeros_like(ordered_ref)
    for group in range(chunks // 8):
        order = order_ref[8 * group : 8 * group + 8, :]
        chunk_of = lax.shift_right_logical(order, 7)
        lane_of = lax.bitwise_and(order, 127)
        for axis in range(3):
            found = jnp.zeros((8, 128), F32)
            for chunk in range(chunks):
                source = jnp.broadcast_to(
                    coords_ref[axis : axis + 1, 128 * chunk : 128 * chunk + 128], (8, 128)
                )
                picked = jnp.take_along_axis(source, lane_of, axis=1)
                found = jnp.where(chunk_of == chunk, picked, found)
            for row in range(8):
                place = 128 * (8 * group + row)
                ordered_ref[axis : axis + 1, place : place + 128] = found[row : row + 1, :]
    row8 = lax.broadcasted_iota(jnp.int32, (8, points), 0)
    scale = (math.sqrt(5.0) * LOG2E) / length_ref[...]
    scaled = jnp.where(row8 < 3, (ordered_ref[...] - 0.5) * scale, 0.0)
    z1 = scaled.astype(BF16).astype(F32)
    z2 = (scaled - z1).astype(BF16).astype(F32)
    kept = z1 + z2
    norm = jnp.broadcast_to(jnp.sum(kept * kept, axis=0, keepdims=True), (8, points))
    n1 = norm.astype(BF16).astype(F32)
    n2 = (norm - n1).astype(BF16).astype(F32)
    n3 = norm - n1 - n2
    ends = leaf_ends(sizes_ref, leaf_count)
    leaf = leaf_row(ends, 0, (8, points))
    parts = jnp.where(row8 % 3 == 0, n1, jnp.where(row8 % 3 == 1, n2, n3))
    norm_left = jnp.where(row8 < 3, parts, jnp.where(row8 < 6, 1.0, 0.0))
    norm_right = jnp.where(row8 < 3, 1.0, jnp.where(row8 < 6, parts, 0.0))
    same = leaf == row8
    leaf_left = jnp.where(same, 1.0, 0.0)
    leaf_right = jnp.where(same, 0.0, FAR_AWAY)
    left = jnp.concatenate(
        [-2.0 * z1, -2.0 * z1, -2.0 * z2, -2.0 * z2, norm_left, leaf_left]
        + [jnp.zeros((80, points), F32)],
        axis=0,
    )
    right = jnp.concatenate(
        [z1, z2, z1, z2, norm_right, leaf_right] + [jnp.zeros((80, points), F32)], axis=0
    )
    right_ref[...] = right.astype(BF16)
    left_ref[:points, :] = left.T.astype(BF16)
    left_ref[points:, :] = jnp.zeros((TILE, 128), BF16)
    split = halves(d_ref[...]).astype(F32)
    split = jnp.concatenate([split, jnp.zeros((128 - split.shape[0], points), F32)], axis=0)
    dd_ref[...] = split.T.astype(BF16)


def features(sizes, lengthscale, coordinates, order, direction, after):
    leaf_count = sizes.shape[1]
    points = direction.shape[1]
    return pl.pallas_call(
        functools.partial(features_kernel, leaf_count),
        out_shape=(
            jax.ShapeDtypeStruct((points + TILE, 128), BF16),
            jax.ShapeDtypeStruct((128, points), BF16),
            jax.ShapeDtypeStruct((points, 128), BF16),
        ),
        in_specs=[SMEM, VMEM, VMEM, VMEM, VMEM, ANY],
        out_specs=(VMEM, VMEM, VMEM),
        scratch_shapes=[pltpu.VMEM((8, points), F32)],
        compiler_params=PARAMS,
        name="features",
    )(sizes, lengthscale.reshape(1, 1), coordinates, order.reshape(-1, 128), direction, after)


def tile_spans(ends, tiles):
    lows, counts = [], []
    for tile in range(tiles):
        begin, last = tile * TILE, tile * TILE + TILE - 1
        low = 0
        high = ends[-1]
        for end in ends:
            low = jnp.where(end <= begin, end, low)
        for end in ends[::-1]:
            high = jnp.where(end > last, end, high)
        low = lax.div(low, TILE)
        lows.append(low)
        counts.append(lax.div(high - 1, TILE) + 1 - low)
    return lows, counts


def near_kernel(leaf_count, part, parts, sizes_ref, left_ref, right_ref, dd_ref, before_ref, after_ref, out_ref):
    ends = leaf_ends(sizes_ref, leaf_count)
    tiles = right_ref.shape[1] // TILE
    lows, counts = tile_spans(ends, tiles)
    firsts = [0]
    for count in counts:
        firsts.append(firsts[-1] + count)
    groups = lax.div(firsts[-1] + (GROUP - 1), GROUP)
    offsets = [low - first for low, first in zip(lows, firsts)]
    if part == 0:
        out_ref[...] = jnp.zeros_like(out_ref)

    def one_group(group, carry):
        for unit in range(GROUP):
            item = group * GROUP + unit
            row = 0
            offset = offsets[0]
            for tile in range(1, tiles):
                inside = item >= firsts[tile]
                row = jnp.where(inside, tile, row)
                offset = jnp.where(inside, offsets[tile], offset)
            spare = item >= firsts[-1]
            row = jnp.where(spare, tiles, row)
            column = jnp.where(spare, 0, item + offset)
            begin = pl.multiple_of(row * TILE, TILE)
            place = pl.multiple_of(column * TILE, TILE)
            squared = jnp.dot(
                left_ref[pl.ds(begin, TILE), :],
                right_ref[:, pl.ds(place, TILE)],
                preferred_element_type=F32,
            )
            squared = jnp.maximum(squared, 1e-12)
            root = squared * lax.rsqrt(squared)
            kernel = (squared + LINEAR * root + CONSTANT) * jnp.exp2(-root)
            high_part = kernel.astype(BF16)
            low_part = (kernel - high_part.astype(F32)).astype(BF16)
            weights = dd_ref[pl.ds(place, TILE), :]
            out_ref[pl.ds(begin, TILE), :] += jnp.dot(
                jnp.concatenate([high_part, low_part], axis=1),
                jnp.concatenate([weights, weights], axis=0),
                preferred_element_type=F32,
            )
        return carry

    lax.fori_loop(
        lax.div(groups * part, parts), lax.div(groups * (part + 1), parts), one_group, 0
    )


def near_part(sizes, left, right, dd, before, after, part, parts):
    leaf_count = sizes.shape[1]
    return pl.pallas_call(
        functools.partial(near_kernel, leaf_count, part, parts),
        out_shape=jax.ShapeDtypeStruct(left.shape, F32),
        in_specs=[SMEM, VMEM, VMEM, VMEM, ANY if part == 0 else VMEM, ANY],
        out_specs=VMEM,
        input_output_aliases={} if part == 0 else {4: 0},
        compiler_params=PARAMS,
        name="near_part",
    )(sizes, left, right, dd, before, after)


def down_kernel(
    leaf_count,
    levels,
    sizes_ref,
    noise_ref,
    scale_ref,
    d_ref,
    r_ref,
    basis_ref,
    nt_ref,
    nc_ref,
    ut_ref,
    uc_ref,
    local_ref,
    *rest,
):
    side_refs = rest[:levels]
    near_ref, a_ref, sums_ref = rest[levels:]
    probes, points = d_ref.shape
    down = None
    for level in range(levels - 1, -1, -1):
        coupling = nc_ref[0, 0] if level == 0 else uc_ref[0, level - 1]
        side = side_refs[level][...]
        if down is None:
            down = times_transposed(side, coupling)
        else:
            transfer = nt_ref[0, 0] if level == 0 else ut_ref[0, level - 1]
            down = times_transposed(
                jnp.concatenate([down, side], axis=1),
                jnp.concatenate([transfer, coupling], axis=1),
            )
    current = [down]
    while len(current) < leaf_count:
        count = len(current)
        following = []
        for index in range(2 * count):
            node = 2 * count - 1 + index
            parent = index // 2
            following.append(
                times_transposed(
                    jnp.concatenate([current[parent], local_ref[count - 1 + parent]], axis=1),
                    jnp.concatenate([nt_ref[0, node], nc_ref[0, node]], axis=1),
                )
            )
        current = following
    stacked = jnp.concatenate([halves(term) for term in current], axis=0)
    ends = leaf_ends(sizes_ref, leaf_count)
    noise = noise_ref[...]
    near_scale = scale_ref[...] * POLY
    width = 512
    peak = jnp.zeros((probes, 128), F32)
    old = jnp.zeros((probes, 128), F32)
    curve = jnp.zeros((probes, 128), F32)

    def lanes(x):
        return sum(x[:, 128 * i : 128 * i + 128] for i in range(width // 128))

    for first in range(0, points, width):
        far_all = jnp.dot(
            stacked, basis_ref[:, first : first + width], preferred_element_type=F32
        )
        leaf = leaf_row(ends, first, (probes, width))
        far = folded(far_all[: 2 * probes])
        for index in range(1, leaf_count):
            term = folded(far_all[2 * probes * index : 2 * probes * (index + 1)])
            far = jnp.where(leaf == index, term, far)
        d = d_ref[:, first : first + width]
        r = r_ref[:, first : first + width]
        near = near_ref[first : first + width, :].T
        near = near[:probes] + near[probes : 2 * probes]
        applied = noise * d + near_scale * near + far
        a_ref[:, first : first + width] = applied
        size = jnp.abs(applied)
        for i in range(width // 128):
            peak = jnp.maximum(peak, size[:, 128 * i : 128 * i + 128])
        old = old + lanes(r * r)
        curve = curve + lanes(d * applied)
    top = jnp.maximum(jnp.max(peak, axis=1, keepdims=True), 1e-30)
    inverse = 1.0 / top
    cross = jnp.zeros((probes, 128), F32)
    square = jnp.zeros((probes, 128), F32)
    for first in range(0, points, width):
        unit = a_ref[:, first : first + width] * inverse
        cross = cross + lanes(r_ref[:, first : first + width] * unit)
        square = square + lanes(unit * unit)
    lane = lax.broadcasted_iota(jnp.int32, (probes, 128), 1)
    sums = jnp.where(lane == 0, jnp.sum(old, axis=1, keepdims=True), 0.0)
    sums = jnp.where(lane == 1, jnp.sum(curve, axis=1, keepdims=True), sums)
    sums = jnp.where(lane == 2, jnp.sum(cross, axis=1, keepdims=True), sums)
    sums = jnp.where(lane == 3, jnp.sum(square, axis=1, keepdims=True), sums)
    sums_ref[...] = jnp.where(lane == 4, top, sums).T[:8]


def descend(
    sizes, noise, scale, direction, residual, basis, node_transfer, node_coupling,
    upper_transfer, upper_coupling, local, sides, near,
):
    leaf_count = sizes.shape[1]
    probes, points = direction.shape
    return pl.pallas_call(
        functools.partial(down_kernel, leaf_count, len(sides)),
        out_shape=(
            jax.ShapeDtypeStruct((probes, points), F32),
            jax.ShapeDtypeStruct((8, probes), F32),
        ),
        in_specs=[SMEM] + [VMEM] * (11 + len(sides)),
        out_specs=(VMEM, VMEM),
        compiler_params=PARAMS,
        name="descend",
    )(
        sizes, noise.reshape(1, 1), scale.reshape(1, 1), direction, residual, basis,
        node_transfer, node_coupling, upper_transfer, upper_coupling, local, *sides, near,
    )


def step_kernel(sums_ref, x_ref, r_ref, d_ref, a_ref, nx_ref, nr_ref, nd_ref):
    sums = sums_ref[...]
    probes = d_ref.shape[0]
    tops = sums[:, 4:5, :]
    top = jnp.max(tops, axis=0)
    ratio = tops / top
    old, curve = jnp.sum(sums[:, 0:1, :], axis=0), jnp.sum(sums[:, 1:2, :], axis=0)
    cross = jnp.sum(sums[:, 2:3, :] * ratio, axis=0)
    square = jnp.sum(sums[:, 3:4, :] * (ratio * ratio), axis=0)
    step = old / curve
    reach = step * top
    fresh = old - 2.0 * (reach * cross) + (reach * reach) * square
    beta = fresh / old
    own = lax.broadcasted_iota(jnp.int32, (probes, probes), 0) == lax.broadcasted_iota(
        jnp.int32, (probes, probes), 1
    )
    step = jnp.sum(jnp.where(own, step, 0.0), axis=1, keepdims=True)
    beta = jnp.sum(jnp.where(own, beta, 0.0), axis=1, keepdims=True)
    d = d_ref[...]
    nx_ref[...] = x_ref[...] + step * d
    remaining = r_ref[...] - step * a_ref[...]
    nr_ref[...] = remaining
    nd_ref[...] = remaining + beta * d


def finish(sums, solution_block, residual, direction, applied):
    shape = jax.ShapeDtypeStruct(direction.shape, F32)
    return pl.pallas_call(
        step_kernel,
        out_shape=(shape, shape, shape),
        in_specs=[VMEM] * 5,
        out_specs=(VMEM, VMEM, VMEM),
        compiler_params=PARAMS,
        name="finish",
    )(sums, solution_block, residual, direction, applied)


def from_partner(array, stride):
    count = lax.axis_size("leaf")
    return lax.ppermute(array, "leaf", [(i, i ^ stride) for i in range(count)])


def level_groups(levels):
    groups = [[0]]
    level = 1
    while level < levels:
        groups.append(list(range(level, min(level + 2, levels))))
        level += 2
    return groups


def shards(
    solution,
    residual,
    direction,
    coordinates,
    cluster_order,
    leaf_sizes,
    leaf_basis,
    node_transfer,
    node_coupling,
    upper_transfer,
    upper_coupling,
    lengthscale,
    outputscale,
    noise_variance,
):
    levels = lax.axis_size("leaf").bit_length() - 1
    probes, points = direction.shape
    up, local = climb(
        leaf_sizes, direction, leaf_basis, node_transfer, node_coupling,
        upper_transfer, upper_coupling, levels,
    )
    left, right, dd = features(leaf_sizes, lengthscale, coordinates, cluster_order, direction, up)
    groups = level_groups(levels)
    parts = 3
    sides = [None] * levels
    near = up
    current = up
    for number, group in enumerate(groups):
        base = group[0]
        strides = [2**level for level in group]
        incoming = {}
        for pick in range(1, 2 ** len(group)):
            stride = sum(s for bit, s in enumerate(strides) if pick >> bit & 1)
            top = pick.bit_length() - 1
            incoming[pick] = from_partner(current[top:], stride)
        if number < parts:
            near = near_part(leaf_sizes, left, right, dd, near, current, number, parts)
        for position in range(len(group)):
            total = current[position]
            for pick in range(1, 2 ** (position + 1)):
                top = pick.bit_length() - 1
                total = total + incoming[pick][position - top]
            sides[base + position] = total
        following = current[len(group) :]
        if following.shape[0]:
            for pick in range(1, 2 ** len(group)):
                top = pick.bit_length() - 1
                following = following + incoming[pick][len(group) - top :]
        current = following
    for number in range(len(groups), parts):
        near = near_part(leaf_sizes, left, right, dd, near, up, number, parts)
    applied, sums = descend(
        leaf_sizes, noise_variance, outputscale, direction, residual, leaf_basis,
        node_transfer, node_coupling, upper_transfer, upper_coupling, local, sides, near,
    )
    gathered = lax.all_gather(sums, "leaf")
    return finish(gathered, solution, residual, direction, applied)


def solution(mesh):
    in_specs = (
        P(None, "leaf"),
        P(None, "leaf"),
        P(None, "leaf"),
        P(None, "leaf"),
        P("leaf"),
        P("leaf", None),
        P(None, "leaf"),
        P("leaf", None, None, None),
        P("leaf", None, None, None),
        P("leaf", None, None, None),
        P("leaf", None, None, None),
        P(),
        P(),
        P(),
    )
    out_specs = (P(None, "leaf"), P(None, "leaf"), P(None, "leaf"))
    return jax.shard_map(shards, mesh=mesh, in_specs=in_specs, out_specs=out_specs, check_vma=False)
```

```python
import functools
import math

import jax
import jax.numpy as jnp
from jax import lax
from jax.experimental import pallas as pl
from jax.experimental.pallas import tpu as pltpu
from jax.sharding import PartitionSpec as P

F32 = jnp.float32
BF16 = jnp.bfloat16
TILE = 256
FAR_AWAY = 32768.0
LOG2E = 1.0 / math.log(2.0)
POLY = math.log(2.0) ** 2 / 3.0
LINEAR = 3.0 * LOG2E
CONSTANT = 3.0 * LOG2E * LOG2E

VMEM = pl.BlockSpec(memory_space=pltpu.VMEM)
SMEM = pl.BlockSpec(memory_space=pltpu.SMEM)
ANY = pl.BlockSpec(memory_space=pl.ANY)
HBM = pl.BlockSpec(memory_space=pltpu.HBM)
GROUP = 4
PARAMS = pltpu.CompilerParams(vmem_limit_bytes=48 * 1024 * 1024)


def halves(x):
    high = x.astype(BF16)
    low = (x - high.astype(F32)).astype(BF16)
    return jnp.concatenate([high, low], axis=0)


def folded(x):
    rows = x.shape[0] // 2
    return x[:rows] + x[rows:]


def times(x, generator):
    return folded(jnp.dot(halves(x), generator, preferred_element_type=F32))


def times_transposed(x, generator):
    return folded(
        lax.dot_general(
            halves(x), generator, (((1,), (1,)), ((), ())), preferred_element_type=F32
        )
    )


def leaf_ends(sizes_ref, leaf_count):
    ends = []
    total = 0
    for leaf in range(leaf_count):
        total = total + sizes_ref[0, leaf]
        ends.append(total)
    return ends


def leaf_row(ends, first, shape):
    positions = lax.broadcasted_iota(jnp.int32, shape, 1) + first
    leaf = jnp.zeros(shape, jnp.int32)
    for end in ends[:-1]:
        leaf = leaf + (positions >= end).astype(jnp.int32)
    return leaf


def up_kernel(leaf_count, levels, *refs):
    sources, (up_ref, local_ref) = refs[:7], refs[7:9]
    held, semaphores = refs[9:16], refs[16]
    copies = [
        pltpu.make_async_copy(source, target, semaphores.at[index])
        for index, (source, target) in enumerate(zip(sources, held))
    ]
    for copy in copies:
        copy.start()
    for copy in copies:
        copy.wait()
    sizes_ref, d_ref, basis_ref, nt_ref, nc_ref, ut_ref, uc_ref = held
    probes, points = d_ref.shape
    ends = leaf_ends(sizes_ref, leaf_count)
    split = halves(d_ref[...])
    leaf = leaf_row(ends, 0, (2 * probes, points))
    zero = jnp.zeros_like(split)
    masked = jnp.concatenate(
        [jnp.where(leaf == index, split, zero) for index in range(leaf_count)], axis=0
    )
    raw = lax.dot_general(
        masked, basis_ref[...], (((1,), (1,)), ((), ())), preferred_element_type=F32
    )
    current = [
        folded(raw[2 * probes * index : 2 * probes * (index + 1)]) for index in range(leaf_count)
    ]
    rank = basis_ref.shape[0]
    while len(current) > 1:
        count = len(current)
        raised, sided = [], []
        for index in range(count):
            node = count - 1 + index
            both = jnp.concatenate([nt_ref[0, node], nc_ref[0, node]], axis=1)
            image = times(current[index], both)
            raised.append(image[:, :rank])
            sided.append(image[:, rank:])
        current = [raised[2 * i] + raised[2 * i + 1] for i in range(count // 2)]
        for i in range(count // 2):
            local_ref[count // 2 - 1 + i] = sided[2 * i] + sided[2 * i + 1]
    coefficient = current[0]
    for level in range(levels):
        coupling = nc_ref[0, 0] if level == 0 else uc_ref[0, level - 1]
        if level + 1 < levels:
            transfer = nt_ref[0, 0] if level == 0 else ut_ref[0, level - 1]
            image = times(coefficient, jnp.concatenate([transfer, coupling], axis=1))
            coefficient = image[:, :rank]
            up_ref[level] = image[:, rank:]
        else:
            up_ref[level] = times(coefficient, coupling)


def climb(sizes, vectors, levels):
    leaf_count = sizes.shape[1]
    probes, rank = vectors[0].shape[0], vectors[1].shape[0]
    arrays = (sizes, *vectors)
    return pl.pallas_call(
        functools.partial(up_kernel, leaf_count, levels),
        out_shape=(
            jax.ShapeDtypeStruct((levels, probes, rank), F32),
            jax.ShapeDtypeStruct((leaf_count - 1, probes, rank), F32),
        ),
        in_specs=[HBM] * len(arrays),
        out_specs=(VMEM, VMEM),
        scratch_shapes=[pltpu.SMEM(sizes.shape, sizes.dtype)]
        + [pltpu.VMEM(array.shape, array.dtype) for array in vectors]
        + [pltpu.SemaphoreType.DMA((len(arrays),))],
        compiler_params=PARAMS,
        name="climb",
    )(*(pltpu.with_memory_space_constraint(array, pltpu.HBM) for array in arrays))


def features_kernel(
    leaf_count,
    sizes_ref,
    length_ref,
    coords_ref,
    order_ref,
    d_ref,
    after_ref,
    left_ref,
    right_ref,
    dd_ref,
    ds_ref,
    ordered_ref,
):
    points = coords_ref.shape[1]
    chunks = points // 128
    ordered_ref[...] = jnp.zeros_like(ordered_ref)
    for group in range(chunks // 8):
        order = order_ref[8 * group : 8 * group + 8, :]
        chunk_of = lax.shift_right_logical(order, 7)
        lane_of = lax.bitwise_and(order, 127)
        for axis in range(3):
            found = jnp.zeros((8, 128), F32)
            for chunk in range(chunks):
                source = jnp.broadcast_to(
                    coords_ref[axis : axis + 1, 128 * chunk : 128 * chunk + 128], (8, 128)
                )
                picked = jnp.take_along_axis(source, lane_of, axis=1)
                found = jnp.where(chunk_of == chunk, picked, found)
            for row in range(8):
                place = 128 * (8 * group + row)
                ordered_ref[axis : axis + 1, place : place + 128] = found[row : row + 1, :]
    row8 = lax.broadcasted_iota(jnp.int32, (8, points), 0)
    scale = (math.sqrt(5.0) * LOG2E) / length_ref[...].reshape(1, 1)
    scaled = jnp.where(row8 < 3, (ordered_ref[...] - 0.5) * scale, 0.0)
    z1 = scaled.astype(BF16).astype(F32)
    z2 = (scaled - z1).astype(BF16).astype(F32)
    kept = z1 + z2
    norm = jnp.broadcast_to(jnp.sum(kept * kept, axis=0, keepdims=True), (8, points))
    n1 = norm.astype(BF16).astype(F32)
    n2 = (norm - n1).astype(BF16).astype(F32)
    n3 = norm - n1 - n2
    ends = leaf_ends(sizes_ref, leaf_count)
    leaf = leaf_row(ends, 0, (8, points))
    parts = jnp.where(row8 % 3 == 0, n1, jnp.where(row8 % 3 == 1, n2, n3))
    norm_left = jnp.where(row8 < 3, parts, jnp.where(row8 < 6, 1.0, 0.0))
    norm_right = jnp.where(row8 < 3, 1.0, jnp.where(row8 < 6, parts, 0.0))
    same = leaf == row8
    leaf_left = jnp.where(same, 1.0, 0.0)
    leaf_right = jnp.where(same, 0.0, FAR_AWAY)
    left = jnp.concatenate(
        [-2.0 * z1, -2.0 * z1, -2.0 * z2, -2.0 * z2, norm_left, leaf_left]
        + [jnp.zeros((80, points), F32)],
        axis=0,
    )
    right = jnp.concatenate(
        [z1, z2, z1, z2, norm_right, leaf_right] + [jnp.zeros((80, points), F32)], axis=0
    )
    right_ref[...] = right.astype(BF16)
    left_ref[...] = left.T.astype(BF16)
    split = halves(d_ref[...])
    ds_ref[...] = split
    split = split.astype(F32)
    split = jnp.concatenate([split, jnp.zeros((128 - split.shape[0], points), F32)], axis=0)
    dd_ref[...] = split.T.astype(BF16)


def features(sizes, lengthscale, coordinates, order, direction, after):
    leaf_count = sizes.shape[1]
    points = direction.shape[1]
    return pl.pallas_call(
        functools.partial(features_kernel, leaf_count),
        out_shape=(
            jax.ShapeDtypeStruct((points, 128), BF16),
            jax.ShapeDtypeStruct((128, points), BF16),
            jax.ShapeDtypeStruct((points, 128), BF16),
            jax.ShapeDtypeStruct((2 * direction.shape[0], points), BF16),
        ),
        in_specs=[SMEM, VMEM, VMEM, VMEM, VMEM, ANY],
        out_specs=(VMEM,) * 4,
        scratch_shapes=[pltpu.VMEM((8, points), F32)],
        compiler_params=PARAMS,
        name="features",
    )(sizes, lengthscale, coordinates, order.reshape(-1, 128), direction, after)


def tile_counts(ends, tiles):
    counts = []
    for tile in range(tiles):
        last = tile * TILE + TILE - 1
        high = ends[-1]
        for end in ends[::-1]:
            high = jnp.where(end > last, end, high)
        counts.append(lax.div(high - 1, TILE) + 1 - tile)
    return counts


def near_kernel(
    leaf_count, part, parts, sizes_ref, left_ref, right_ref, dd_ref, ds_ref, *refs
):
    tall_ref, wide_ref = refs[-2:]
    ends = leaf_ends(sizes_ref, leaf_count)
    tiles = right_ref.shape[1] // TILE
    firsts = [0]
    for count in tile_counts(ends, tiles):
        firsts.append(firsts[-1] + count)
    groups = lax.div(firsts[-1] + (GROUP - 1), GROUP)
    offsets = [tile - first for tile, first in zip(range(tiles), firsts)]
    if part == 0:
        tall_ref[...] = jnp.zeros_like(tall_ref)
        wide_ref[...] = jnp.zeros_like(wide_ref)

    def one_group(group, carry):
        for unit in range(GROUP):
            item = group * GROUP + unit
            row = 0
            offset = offsets[0]
            for tile in range(1, tiles):
                inside = item >= firsts[tile]
                row = jnp.where(inside, tile, row)
                offset = jnp.where(inside, offsets[tile], offset)
            spare = item >= firsts[-1]
            column = item + offset
            tall = pl.multiple_of(jnp.where(spare, tiles, row) * TILE, TILE)
            wide = pl.multiple_of(jnp.where(spare | (row == column), tiles, column) * TILE, TILE)
            rows = pl.ds(pl.multiple_of(jnp.where(spare, 0, row) * TILE, TILE), TILE)
            columns = pl.ds(pl.multiple_of(jnp.where(spare, 0, column) * TILE, TILE), TILE)
            squared = jnp.dot(
                left_ref[rows, :], right_ref[:, columns], preferred_element_type=F32
            )
            squared = jnp.maximum(squared, 1e-12)
            root = squared * lax.rsqrt(squared)
            kernel = (squared + LINEAR * root + CONSTANT) * jnp.exp2(-root)
            high_part = kernel.astype(BF16)
            low_part = (kernel - high_part.astype(F32)).astype(BF16)
            weights = dd_ref[columns, :]
            tall_ref[pl.ds(tall, TILE), :] += jnp.dot(
                jnp.concatenate([high_part, low_part], axis=1),
                jnp.concatenate([weights, weights], axis=0),
                preferred_element_type=F32,
            )
            vectors = ds_ref[:, rows]
            wide_ref[:, pl.ds(wide, TILE)] += jnp.dot(
                jnp.concatenate([vectors, vectors], axis=1),
                jnp.concatenate([high_part, low_part], axis=0),
                preferred_element_type=F32,
            )
        return carry

    lax.fori_loop(
        lax.div(groups * part, parts), lax.div(groups * (part + 1), parts), one_group, 0
    )


def near_part(sizes, prepared, before, after, part, parts):
    leaf_count = sizes.shape[1]
    left, right, dd, ds = prepared
    points = right.shape[1]
    return pl.pallas_call(
        functools.partial(near_kernel, leaf_count, part, parts),
        out_shape=(
            jax.ShapeDtypeStruct((points + TILE, 128), F32),
            jax.ShapeDtypeStruct((ds.shape[0], points + TILE), F32),
        ),
        in_specs=[SMEM] + [VMEM] * (4 + len(before)) + [ANY],
        out_specs=(VMEM, VMEM),
        input_output_aliases={5 + index: index for index in range(len(before))},
        compiler_params=PARAMS,
        name="near_part",
    )(sizes, left, right, dd, ds, *before, after)


def down_kernel(
    leaf_count,
    levels,
    sizes_ref,
    noise_ref,
    scale_ref,
    d_ref,
    r_ref,
    basis_ref,
    nt_ref,
    nc_ref,
    ut_ref,
    uc_ref,
    local_ref,
    *rest,
):
    side_refs = rest[:levels]
    tall_ref, wide_ref, a_ref, sums_ref = rest[levels:]
    probes, points = d_ref.shape
    down = None
    for level in range(levels - 1, -1, -1):
        coupling = nc_ref[0, 0] if level == 0 else uc_ref[0, level - 1]
        side = side_refs[level][...]
        if down is None:
            down = times_transposed(side, coupling)
        else:
            transfer = nt_ref[0, 0] if level == 0 else ut_ref[0, level - 1]
            down = times_transposed(
                jnp.concatenate([down, side], axis=1),
                jnp.concatenate([transfer, coupling], axis=1),
            )
    current = [down]
    while len(current) < leaf_count:
        count = len(current)
        following = []
        for index in range(2 * count):
            node = 2 * count - 1 + index
            parent = index // 2
            following.append(
                times_transposed(
                    jnp.concatenate([current[parent], local_ref[count - 1 + parent]], axis=1),
                    jnp.concatenate([nt_ref[0, node], nc_ref[0, node]], axis=1),
                )
            )
        current = following
    stacked = jnp.concatenate([halves(term) for term in current], axis=0)
    ends = leaf_ends(sizes_ref, leaf_count)
    noise = noise_ref[...].reshape(1, 1)
    near_scale = scale_ref[...].reshape(1, 1) * POLY
    width = 512
    peak = jnp.zeros((probes, 128), F32)
    old = jnp.zeros((probes, 128), F32)
    curve = jnp.zeros((probes, 128), F32)

    def lanes(x):
        return sum(x[:, 128 * i : 128 * i + 128] for i in range(width // 128))

    for first in range(0, points, width):
        far_all = jnp.dot(
            stacked, basis_ref[:, first : first + width], preferred_element_type=F32
        )
        leaf = leaf_row(ends, first, (probes, width))
        far = folded(far_all[: 2 * probes])
        for index in range(1, leaf_count):
            term = folded(far_all[2 * probes * index : 2 * probes * (index + 1)])
            far = jnp.where(leaf == index, term, far)
        d = d_ref[:, first : first + width]
        r = r_ref[:, first : first + width]
        near = tall_ref[first : first + width, :].T[: 2 * probes]
        near = folded(near + wide_ref[:, first : first + width])
        applied = noise * d + near_scale * near + far
        a_ref[:, first : first + width] = applied
        size = jnp.abs(applied)
        for i in range(width // 128):
            peak = jnp.maximum(peak, size[:, 128 * i : 128 * i + 128])
        old = old + lanes(r * r)
        curve = curve + lanes(d * applied)
    top = jnp.maximum(jnp.max(peak, axis=1, keepdims=True), 1e-30)
    inverse = 1.0 / top
    cross = jnp.zeros((probes, 128), F32)
    square = jnp.zeros((probes, 128), F32)
    for first in range(0, points, width):
        unit = a_ref[:, first : first + width] * inverse
        cross = cross + lanes(r_ref[:, first : first + width] * unit)
        square = square + lanes(unit * unit)
    lane = lax.broadcasted_iota(jnp.int32, (probes, 128), 1)
    sums = jnp.where(lane == 0, jnp.sum(old, axis=1, keepdims=True), 0.0)
    sums = jnp.where(lane == 1, jnp.sum(curve, axis=1, keepdims=True), sums)
    sums = jnp.where(lane == 2, jnp.sum(cross, axis=1, keepdims=True), sums)
    sums = jnp.where(lane == 3, jnp.sum(square, axis=1, keepdims=True), sums)
    sums = jnp.where(lane == 4, top, sums).T[:8]
    sums_ref[...] = jnp.broadcast_to(sums[None], sums_ref.shape)


def descend(
    sizes, noise, scale, direction, residual, basis, node_transfer, node_coupling,
    upper_transfer, upper_coupling, local, sides, near,
):
    leaf_count = sizes.shape[1]
    probes, points = direction.shape
    return pl.pallas_call(
        functools.partial(down_kernel, leaf_count, len(sides)),
        out_shape=(
            jax.ShapeDtypeStruct((probes, points), F32),
            jax.ShapeDtypeStruct((2 ** len(sides), 8, probes), F32),
        ),
        in_specs=[SMEM] + [VMEM] * (12 + len(sides)),
        out_specs=(VMEM, VMEM),
        compiler_params=PARAMS,
        name="descend",
    )(
        sizes, noise, scale, direction, residual, basis,
        node_transfer, node_coupling, upper_transfer, upper_coupling, local, *sides, *near,
    )


def step_kernel(sums_ref, x_ref, r_ref, d_ref, a_ref, nx_ref, nr_ref, nd_ref):
    sums = sums_ref[...]
    probes = d_ref.shape[0]
    tops = sums[:, 4:5, :]
    top = jnp.max(tops, axis=0)
    ratio = tops / top
    old, curve = jnp.sum(sums[:, 0:1, :], axis=0), jnp.sum(sums[:, 1:2, :], axis=0)
    cross = jnp.sum(sums[:, 2:3, :] * ratio, axis=0)
    square = jnp.sum(sums[:, 3:4, :] * (ratio * ratio), axis=0)
    step = old / curve
    reach = step * top
    fresh = old - 2.0 * (reach * cross) + (reach * reach) * square
    beta = fresh / old
    own = lax.broadcasted_iota(jnp.int32, (probes, probes), 0) == lax.broadcasted_iota(
        jnp.int32, (probes, probes), 1
    )
    step = jnp.sum(jnp.where(own, step, 0.0), axis=1, keepdims=True)
    beta = jnp.sum(jnp.where(own, beta, 0.0), axis=1, keepdims=True)
    d = d_ref[...]
    nx_ref[...] = x_ref[...] + step * d
    remaining = r_ref[...] - step * a_ref[...]
    nr_ref[...] = remaining
    nd_ref[...] = remaining + beta * d


def finish(sums, solution_block, residual, direction, applied):
    shape = jax.ShapeDtypeStruct(direction.shape, F32)
    return pl.pallas_call(
        step_kernel,
        out_shape=(shape, shape, shape),
        in_specs=[VMEM] * 5,
        out_specs=(VMEM, VMEM, VMEM),
        compiler_params=PARAMS,
        name="finish",
    )(sums, solution_block, residual, direction, applied)


def from_partner(array, stride):
    count = lax.axis_size("leaf")
    return lax.ppermute(array, "leaf", [(i, i ^ stride) for i in range(count)])


def level_groups(levels):
    groups = [[0]]
    level = 1
    while level < levels:
        groups.append(list(range(level, min(level + 2, levels))))
        level += 2
    return groups


def shards(
    solution,
    residual,
    direction,
    coordinates,
    cluster_order,
    leaf_sizes,
    leaf_basis,
    node_transfer,
    node_coupling,
    upper_transfer,
    upper_coupling,
    lengthscale,
    outputscale,
    noise_variance,
):
    levels = lax.axis_size("leaf").bit_length() - 1
    probes, points = direction.shape
    up, local = climb(
        leaf_sizes,
        (direction, leaf_basis, node_transfer, node_coupling, upper_transfer, upper_coupling),
        levels,
    )
    prepared = features(leaf_sizes, lengthscale, coordinates, cluster_order, direction, up)
    groups = level_groups(levels)
    parts = 3
    sides = [None] * levels
    near = ()
    current = up
    for number, group in enumerate(groups):
        base = group[0]
        strides = [2**level for level in group]
        incoming = {}
        for pick in range(1, 2 ** len(group)):
            stride = sum(s for bit, s in enumerate(strides) if pick >> bit & 1)
            top = pick.bit_length() - 1
            incoming[pick] = from_partner(current[top:], stride)
        if number < parts:
            near = near_part(leaf_sizes, prepared, near, current, number, parts)
        for position in range(len(group)):
            total = current[position]
            for pick in range(1, 2 ** (position + 1)):
                top = pick.bit_length() - 1
                total = total + incoming[pick][position - top]
            sides[base + position] = total
        following = current[len(group) :]
        if following.shape[0]:
            for pick in range(1, 2 ** len(group)):
                top = pick.bit_length() - 1
                following = following + incoming[pick][len(group) - top :]
        current = following
    for number in range(len(groups), parts):
        near = near_part(leaf_sizes, prepared, near, up, number, parts)
    applied, sums = descend(
        leaf_sizes, noise_variance, outputscale, direction, residual, leaf_basis,
        node_transfer, node_coupling, upper_transfer, upper_coupling, local, sides, near,
    )
    gathered = lax.all_to_all(sums, "leaf", 0, 0)
    return finish(gathered, solution, residual, direction, applied)


def solution(mesh):
    in_specs = (
        P(None, "leaf"),
        P(None, "leaf"),
        P(None, "leaf"),
        P(None, "leaf"),
        P("leaf"),
        P("leaf", None),
        P(None, "leaf"),
        P("leaf", None, None, None),
        P("leaf", None, None, None),
        P("leaf", None, None, None),
        P("leaf", None, None, None),
        P(),
        P(),
        P(),
    )
    out_specs = (P(None, "leaf"), P(None, "leaf"), P(None, "leaf"))
    return jax.shard_map(shards, mesh=mesh, in_specs=in_specs, out_specs=out_specs, check_vma=False)
```

```python
import functools
import math

import jax
import jax.numpy as jnp
from jax import lax
from jax.experimental import pallas as pl
from jax.experimental.pallas import tpu as pltpu
from jax.sharding import PartitionSpec as P

F32 = jnp.float32
BF16 = jnp.bfloat16
TILE = 256
FAR_AWAY = 32768.0
LOG2E = 1.0 / math.log(2.0)
POLY = math.log(2.0) ** 2 / 3.0
LINEAR = 3.0 * LOG2E
CONSTANT = 3.0 * LOG2E * LOG2E

VMEM = pl.BlockSpec(memory_space=pltpu.VMEM)
SMEM = pl.BlockSpec(memory_space=pltpu.SMEM)
ANY = pl.BlockSpec(memory_space=pl.ANY)
HBM = pl.BlockSpec(memory_space=pltpu.HBM)
STRIP = 512
GROUP = 2
PARTS = 5
PARAMS = pltpu.CompilerParams(vmem_limit_bytes=48 * 1024 * 1024)


def halves(x):
    high = x.astype(BF16)
    low = (x - high.astype(F32)).astype(BF16)
    return jnp.concatenate([high, low], axis=0)


def folded(x):
    rows = x.shape[0] // 2
    return x[:rows] + x[rows:]


def times(x, generator):
    return folded(jnp.dot(halves(x), generator, preferred_element_type=F32))


def times_transposed(x, generator):
    return folded(
        lax.dot_general(
            halves(x), generator, (((1,), (1,)), ((), ())), preferred_element_type=F32
        )
    )


def leaf_ends(sizes_ref, leaf_count):
    ends = []
    total = 0
    for leaf in range(leaf_count):
        total = total + sizes_ref[0, leaf]
        ends.append(total)
    return ends


def leaf_row(ends, first, shape):
    positions = lax.broadcasted_iota(jnp.int32, shape, 1) + first
    leaf = jnp.zeros(shape, jnp.int32)
    for end in ends[:-1]:
        leaf = leaf + (positions >= end).astype(jnp.int32)
    return leaf


def up_kernel(leaf_count, levels, *refs):
    sources, (up_ref, local_ref) = refs[:7], refs[7:9]
    held, semaphores = refs[9:16], refs[16]
    copies = [
        pltpu.make_async_copy(source, target, semaphores.at[index])
        for index, (source, target) in enumerate(zip(sources, held))
    ]
    for copy in copies:
        copy.start()
    for copy in copies:
        copy.wait()
    sizes_ref, d_ref, basis_ref, nt_ref, nc_ref, ut_ref, uc_ref = held
    probes, points = d_ref.shape
    ends = leaf_ends(sizes_ref, leaf_count)
    split = halves(d_ref[...])
    leaf = leaf_row(ends, 0, (2 * probes, points))
    zero = jnp.zeros_like(split)
    masked = jnp.concatenate(
        [jnp.where(leaf == index, split, zero) for index in range(leaf_count)], axis=0
    )
    raw = lax.dot_general(
        masked, basis_ref[...], (((1,), (1,)), ((), ())), preferred_element_type=F32
    )
    current = [
        folded(raw[2 * probes * index : 2 * probes * (index + 1)]) for index in range(leaf_count)
    ]
    rank = basis_ref.shape[0]
    while len(current) > 1:
        count = len(current)
        raised, sided = [], []
        for index in range(count):
            node = count - 1 + index
            both = jnp.concatenate([nt_ref[0, node], nc_ref[0, node]], axis=1)
            image = times(current[index], both)
            raised.append(image[:, :rank])
            sided.append(image[:, rank:])
        current = [raised[2 * i] + raised[2 * i + 1] for i in range(count // 2)]
        for i in range(count // 2):
            local_ref[count // 2 - 1 + i] = sided[2 * i] + sided[2 * i + 1]
    coefficient = current[0]
    for level in range(levels):
        coupling = nc_ref[0, 0] if level == 0 else uc_ref[0, level - 1]
        if level + 1 < levels:
            transfer = nt_ref[0, 0] if level == 0 else ut_ref[0, level - 1]
            image = times(coefficient, jnp.concatenate([transfer, coupling], axis=1))
            coefficient = image[:, :rank]
            up_ref[level] = image[:, rank:]
        else:
            up_ref[level] = times(coefficient, coupling)


def climb(sizes, vectors, levels):
    leaf_count = sizes.shape[1]
    probes, rank = vectors[0].shape[0], vectors[1].shape[0]
    arrays = (sizes, *vectors)
    return pl.pallas_call(
        functools.partial(up_kernel, leaf_count, levels),
        out_shape=(
            jax.ShapeDtypeStruct((levels, probes, rank), F32),
            jax.ShapeDtypeStruct((leaf_count - 1, probes, rank), F32),
        ),
        in_specs=[HBM] * len(arrays),
        out_specs=(VMEM, VMEM),
        scratch_shapes=[pltpu.SMEM(sizes.shape, sizes.dtype)]
        + [pltpu.VMEM(array.shape, array.dtype) for array in vectors]
        + [pltpu.SemaphoreType.DMA((len(arrays),))],
        compiler_params=PARAMS,
        name="climb",
    )(*(pltpu.with_memory_space_constraint(array, pltpu.HBM) for array in arrays))


def features_kernel(
    leaf_count,
    sizes_ref,
    length_ref,
    coords_ref,
    order_ref,
    d_ref,
    after_ref,
    left_ref,
    right_ref,
    dd_ref,
    ordered_ref,
):
    points = coords_ref.shape[1]
    chunks = points // 128
    ordered_ref[...] = jnp.zeros_like(ordered_ref)
    for group in range(chunks // 8):
        order = order_ref[8 * group : 8 * group + 8, :]
        chunk_of = lax.shift_right_logical(order, 7)
        lane_of = lax.bitwise_and(order, 127)
        for axis in range(3):
            found = jnp.zeros((8, 128), F32)
            for chunk in range(chunks):
                source = jnp.broadcast_to(
                    coords_ref[axis : axis + 1, 128 * chunk : 128 * chunk + 128], (8, 128)
                )
                picked = jnp.take_along_axis(source, lane_of, axis=1)
                found = jnp.where(chunk_of == chunk, picked, found)
            for row in range(8):
                place = 128 * (8 * group + row)
                ordered_ref[axis : axis + 1, place : place + 128] = found[row : row + 1, :]
    row8 = lax.broadcasted_iota(jnp.int32, (8, points), 0)
    scale = (math.sqrt(5.0) * LOG2E) / length_ref[...].reshape(1, 1)
    scaled = jnp.where(row8 < 3, (ordered_ref[...] - 0.5) * scale, 0.0)
    z1 = scaled.astype(BF16).astype(F32)
    z2 = (scaled - z1).astype(BF16).astype(F32)
    kept = z1 + z2
    norm = jnp.broadcast_to(jnp.sum(kept * kept, axis=0, keepdims=True), (8, points))
    n1 = norm.astype(BF16).astype(F32)
    n2 = (norm - n1).astype(BF16).astype(F32)
    n3 = norm - n1 - n2
    ends = leaf_ends(sizes_ref, leaf_count)
    leaf = leaf_row(ends, 0, (8, points))
    parts = jnp.where(row8 % 3 == 0, n1, jnp.where(row8 % 3 == 1, n2, n3))
    norm_left = jnp.where(row8 < 3, parts, jnp.where(row8 < 6, 1.0, 0.0))
    norm_right = jnp.where(row8 < 3, 1.0, jnp.where(row8 < 6, parts, 0.0))
    same = leaf == row8
    leaf_left = jnp.where(same, 1.0, 0.0)
    leaf_right = jnp.where(same, 0.0, FAR_AWAY)
    left = jnp.concatenate(
        [-2.0 * z1, -2.0 * z1, -2.0 * z2, -2.0 * z2, norm_left, leaf_left]
        + [jnp.zeros((80, points), F32)],
        axis=0,
    )
    right = jnp.concatenate(
        [z1, z2, z1, z2, norm_right, leaf_right], axis=0
    )
    right_ref[...] = right.astype(BF16)
    left_ref[:points, :] = left.T.astype(BF16)
    left_ref[points:, :] = jnp.zeros((STRIP, 128), BF16)
    split = halves(d_ref[...]).astype(F32)
    split = jnp.concatenate([split, jnp.zeros((128 - split.shape[0], points), F32)], axis=0)
    dd_ref[:points, :] = split.T.astype(BF16)
    dd_ref[points:, :] = jnp.zeros((TILE, 128), BF16)


def features(sizes, lengthscale, coordinates, order, direction, after):
    leaf_count = sizes.shape[1]
    points = direction.shape[1]
    return pl.pallas_call(
        functools.partial(features_kernel, leaf_count),
        out_shape=(
            jax.ShapeDtypeStruct((points + STRIP, 128), BF16),
            jax.ShapeDtypeStruct((48, points), BF16),
            jax.ShapeDtypeStruct((points + TILE, 128), BF16),
        ),
        in_specs=[SMEM, VMEM, VMEM, VMEM, VMEM, ANY],
        out_specs=(VMEM,) * 3,
        scratch_shapes=[pltpu.VMEM((8, points), F32)],
        compiler_params=PARAMS,
        name="features",
    )(sizes, lengthscale, coordinates, order.reshape(-1, 128), direction, after)


def strip_spans(ends, tiles):
    begins, counts = [], []
    for tile in range(tiles):
        first = tile * TILE
        last = first + TILE - 1
        low = 0
        high = ends[-1]
        for end in ends:
            low = jnp.where(end <= first, end, low)
        for end in ends[::-1]:
            high = jnp.where(end > last, end, high)
        low = lax.div(low, 128) * 128
        begins.append(low)
        counts.append(lax.div(high - low + (STRIP - 1), STRIP))
    return begins, counts


def near_kernel(leaf_count, part, sizes_ref, left_ref, right_ref, dd_ref, *refs):
    out_ref = refs[-1]
    ends = leaf_ends(sizes_ref, leaf_count)
    tiles = right_ref.shape[1] // TILE
    depth = right_ref.shape[0]
    begins, counts = strip_spans(ends, tiles)
    firsts = [0]
    for count in counts:
        firsts.append(firsts[-1] + count)
    groups = lax.div(firsts[-1] + (GROUP - 1), GROUP)
    offsets = [begin - first * STRIP for begin, first in zip(begins, firsts)]
    if part == 0:
        out_ref[...] = jnp.zeros_like(out_ref)

    def one_group(group, carry):
        for unit in range(GROUP):
            item = group * GROUP + unit
            tile_at = 0
            offset = offsets[0]
            for tile in range(1, tiles):
                inside = item >= firsts[tile]
                tile_at = jnp.where(inside, tile, tile_at)
                offset = jnp.where(inside, offsets[tile], offset)
            spare = item >= firsts[-1]
            begin = jnp.where(spare, 0, item * STRIP + offset)
            rows = pl.ds(pl.multiple_of(begin, 128), STRIP)
            columns = pl.ds(pl.multiple_of(tile_at * TILE, TILE), TILE)
            source = pl.ds(pl.multiple_of(jnp.where(spare, tiles, tile_at) * TILE, TILE), TILE)
            squared = jnp.dot(
                left_ref[rows, :depth], right_ref[:, columns], preferred_element_type=F32
            )
            squared = jnp.maximum(squared, 1e-12)
            root = squared * lax.rsqrt(squared)
            kernel = (squared + LINEAR * root + CONSTANT) * jnp.exp2(-root)
            high_part = kernel.astype(BF16)
            low_part = (kernel - high_part.astype(F32)).astype(BF16)
            both = jnp.dot(
                jnp.concatenate([high_part, low_part], axis=0),
                dd_ref[source, :],
                preferred_element_type=F32,
            )
            out_ref[rows, :] += folded(both)
        return carry

    lax.fori_loop(
        lax.div(groups * part, PARTS), lax.div(groups * (part + 1), PARTS), one_group, 0
    )


def near_part(sizes, prepared, before, after, part):
    leaf_count = sizes.shape[1]
    left, right, dd = prepared
    return pl.pallas_call(
        functools.partial(near_kernel, leaf_count, part),
        out_shape=jax.ShapeDtypeStruct(left.shape, F32),
        in_specs=[SMEM] + [VMEM] * (3 + len(before)) + [ANY],
        out_specs=VMEM,
        input_output_aliases={4: 0} if before else {},
        compiler_params=PARAMS,
        name="near_part",
    )(sizes, left, right, dd, *before, after)


def down_kernel(
    leaf_count,
    levels,
    sizes_ref,
    noise_ref,
    scale_ref,
    d_ref,
    r_ref,
    basis_ref,
    nt_ref,
    nc_ref,
    ut_ref,
    uc_ref,
    local_ref,
    *rest,
):
    side_refs = rest[:levels]
    near_ref, a_ref, sums_ref = rest[levels:]
    probes, points = d_ref.shape
    down = None
    for level in range(levels - 1, -1, -1):
        coupling = nc_ref[0, 0] if level == 0 else uc_ref[0, level - 1]
        side = side_refs[level][...]
        if down is None:
            down = times_transposed(side, coupling)
        else:
            transfer = nt_ref[0, 0] if level == 0 else ut_ref[0, level - 1]
            down = times_transposed(
                jnp.concatenate([down, side], axis=1),
                jnp.concatenate([transfer, coupling], axis=1),
            )
    current = [down]
    while len(current) < leaf_count:
        count = len(current)
        following = []
        for index in range(2 * count):
            node = 2 * count - 1 + index
            parent = index // 2
            following.append(
                times_transposed(
                    jnp.concatenate([current[parent], local_ref[count - 1 + parent]], axis=1),
                    jnp.concatenate([nt_ref[0, node], nc_ref[0, node]], axis=1),
                )
            )
        current = following
    stacked = jnp.concatenate([halves(term) for term in current], axis=0)
    ends = leaf_ends(sizes_ref, leaf_count)
    noise = noise_ref[...].reshape(1, 1)
    near_scale = scale_ref[...].reshape(1, 1) * POLY
    width = 512
    peak = jnp.zeros((probes, 128), F32)
    old = jnp.zeros((probes, 128), F32)
    curve = jnp.zeros((probes, 128), F32)

    def lanes(x):
        return sum(x[:, 128 * i : 128 * i + 128] for i in range(width // 128))

    for first in range(0, points, width):
        far_all = jnp.dot(
            stacked, basis_ref[:, first : first + width], preferred_element_type=F32
        )
        leaf = leaf_row(ends, first, (probes, width))
        far = folded(far_all[: 2 * probes])
        for index in range(1, leaf_count):
            term = folded(far_all[2 * probes * index : 2 * probes * (index + 1)])
            far = jnp.where(leaf == index, term, far)
        d = d_ref[:, first : first + width]
        r = r_ref[:, first : first + width]
        near = folded(near_ref[first : first + width, :].T[: 2 * probes])
        applied = noise * d + near_scale * near + far
        a_ref[:, first : first + width] = applied
        size = jnp.abs(applied)
        for i in range(width // 128):
            peak = jnp.maximum(peak, size[:, 128 * i : 128 * i + 128])
        old = old + lanes(r * r)
        curve = curve + lanes(d * applied)
    top = jnp.maximum(jnp.max(peak, axis=1, keepdims=True), 1e-30)
    inverse = 1.0 / top
    cross = jnp.zeros((probes, 128), F32)
    square = jnp.zeros((probes, 128), F32)
    for first in range(0, points, width):
        unit = a_ref[:, first : first + width] * inverse
        cross = cross + lanes(r_ref[:, first : first + width] * unit)
        square = square + lanes(unit * unit)
    columns = [jnp.sum(x, axis=1, keepdims=True) for x in (old, curve, cross, square)]
    lane = lax.broadcasted_iota(jnp.int32, (probes, 128), 1)
    quantity = lax.div(lane, probes)
    own = lax.rem(lane, probes) == lax.broadcasted_iota(jnp.int32, (probes, 128), 0)
    picked = columns[0]
    for index in range(1, 4):
        picked = jnp.where(quantity == index, columns[index], picked)
    row = jnp.concatenate(
        [
            jnp.sum(jnp.where(own, picked, 0.0), axis=0, keepdims=True),
            jnp.sum(jnp.where(own, top, 0.0), axis=0, keepdims=True),
        ],
        axis=1,
    )
    sums_ref[...] = jnp.broadcast_to(row[None], sums_ref.shape)


def descend(
    sizes, noise, scale, direction, residual, basis, node_transfer, node_coupling,
    upper_transfer, upper_coupling, local, sides, near,
):
    leaf_count = sizes.shape[1]
    probes, points = direction.shape
    return pl.pallas_call(
        functools.partial(down_kernel, leaf_count, len(sides)),
        out_shape=(
            jax.ShapeDtypeStruct((probes, points), F32),
            jax.ShapeDtypeStruct((2 ** len(sides), 1, 256), F32),
        ),
        in_specs=[SMEM] + [VMEM] * (11 + len(sides)),
        out_specs=(VMEM, VMEM),
        compiler_params=PARAMS,
        name="descend",
    )(
        sizes, noise, scale, direction, residual, basis,
        node_transfer, node_coupling, upper_transfer, upper_coupling, local, *sides, near,
    )


def step_kernel(sums_ref, x_ref, r_ref, d_ref, a_ref, nx_ref, nr_ref, nd_ref):
    probes = d_ref.shape[0]
    sums, tops = sums_ref[:, :, :128], sums_ref[:, :, 128:]
    top = jnp.max(tops, axis=0)
    ratio = tops / top
    quantity = lax.div(lax.broadcasted_iota(jnp.int32, (1, 1, 128), 2), probes)
    factor = jnp.where(quantity < 2, 1.0, jnp.where(quantity == 2, ratio, ratio * ratio))
    total = jnp.sum(sums * factor, axis=0)
    lane = lax.broadcasted_iota(jnp.int32, (probes, 128), 1)
    probe = lax.broadcasted_iota(jnp.int32, (probes, 128), 0)

    def column(row, index):
        return jnp.sum(
            jnp.where(lane == index * probes + probe, row, 0.0), axis=1, keepdims=True
        )

    old, curve, cross, square = (column(total, index) for index in range(4))
    step = old / curve
    reach = step * column(top, 0)
    fresh = old - 2.0 * (reach * cross) + (reach * reach) * square
    beta = fresh / old
    d = d_ref[...]
    nx_ref[...] = x_ref[...] + step * d
    remaining = r_ref[...] - step * a_ref[...]
    nr_ref[...] = remaining
    nd_ref[...] = remaining + beta * d


def finish(sums, solution_block, residual, direction, applied):
    shape = jax.ShapeDtypeStruct(direction.shape, F32)
    return pl.pallas_call(
        step_kernel,
        out_shape=(shape, shape, shape),
        in_specs=[VMEM] * 5,
        out_specs=(VMEM, VMEM, VMEM),
        compiler_params=PARAMS,
        name="finish",
    )(sums, solution_block, residual, direction, applied)


def from_partner(array, stride):
    count = lax.axis_size("leaf")
    return lax.ppermute(array, "leaf", [(i, i ^ stride) for i in range(count)])


def shards(
    solution,
    residual,
    direction,
    coordinates,
    cluster_order,
    leaf_sizes,
    leaf_basis,
    node_transfer,
    node_coupling,
    upper_transfer,
    upper_coupling,
    lengthscale,
    outputscale,
    noise_variance,
):
    levels = lax.axis_size("leaf").bit_length() - 1
    probes, points = direction.shape
    up, local = climb(
        leaf_sizes,
        (direction, leaf_basis, node_transfer, node_coupling, upper_transfer, upper_coupling),
        levels,
    )
    prepared = features(leaf_sizes, lengthscale, coordinates, cluster_order, direction, up)
    sides = []
    near = ()
    current = up
    for level in range(max(levels, PARTS)):
        if level < levels:
            incoming = from_partner(current, 2**level)
        if level < PARTS:
            near = (near_part(leaf_sizes, prepared, near, current, level),)
        if level < levels:
            current = current + incoming
            sides.append(current[0])
            current = current[1:] if level + 1 < levels else current
    near = near[0]
    applied, sums = descend(
        leaf_sizes, noise_variance, outputscale, direction, residual, leaf_basis,
        node_transfer, node_coupling, upper_transfer, upper_coupling, local, sides, near,
    )
    gathered = lax.all_to_all(sums, "leaf", 0, 0, tiled=True)
    return finish(gathered, solution, residual, direction, applied)


def solution(mesh):
    in_specs = (
        P(None, "leaf"),
        P(None, "leaf"),
        P(None, "leaf"),
        P(None, "leaf"),
        P("leaf"),
        P("leaf", None),
        P(None, "leaf"),
        P("leaf", None, None, None),
        P("leaf", None, None, None),
        P("leaf", None, None, None),
        P("leaf", None, None, None),
        P(),
        P(),
        P(),
    )
    out_specs = (P(None, "leaf"), P(None, "leaf"), P(None, "leaf"))
    return jax.shard_map(shards, mesh=mesh, in_specs=in_specs, out_specs=out_specs, check_vma=False)
```

```python
import functools
import math

import jax
import jax.numpy as jnp
from jax import lax
from jax.experimental import pallas as pl
from jax.experimental.pallas import tpu as pltpu
from jax.sharding import PartitionSpec as P

F32 = jnp.float32
BF16 = jnp.bfloat16
TILE = 128
FAR_AWAY = 32768.0
LOG2E = 1.0 / math.log(2.0)
POLY = math.log(2.0) ** 2 / 3.0
LINEAR = 3.0 * LOG2E
CONSTANT = 3.0 * LOG2E * LOG2E

VMEM = pl.BlockSpec(memory_space=pltpu.VMEM)
SMEM = pl.BlockSpec(memory_space=pltpu.SMEM)
ANY = pl.BlockSpec(memory_space=pl.ANY)
HBM = pl.BlockSpec(memory_space=pltpu.HBM)
STRIP = 384
GROUP = 4
PARTS = 5
PARAMS = pltpu.CompilerParams(vmem_limit_bytes=48 * 1024 * 1024)


def halves(x):
    high = x.astype(BF16)
    low = (x - high.astype(F32)).astype(BF16)
    return jnp.concatenate([high, low], axis=0)


def folded(x):
    rows = x.shape[0] // 2
    return x[:rows] + x[rows:]


def times(x, generator):
    return folded(jnp.dot(halves(x), generator, preferred_element_type=F32))


def times_transposed(x, generator):
    return folded(
        lax.dot_general(
            halves(x), generator, (((1,), (1,)), ((), ())), preferred_element_type=F32
        )
    )


def leaf_ends(sizes_ref, leaf_count):
    ends = []
    total = 0
    for leaf in range(leaf_count):
        total = total + sizes_ref[0, leaf]
        ends.append(total)
    return ends


def leaf_row(ends, first, shape):
    positions = lax.broadcasted_iota(jnp.int32, shape, 1) + first
    leaf = jnp.zeros(shape, jnp.int32)
    for end in ends[:-1]:
        leaf = leaf + (positions >= end).astype(jnp.int32)
    return leaf


def up_kernel(leaf_count, levels, *refs):
    sources, (up_ref, local_ref) = refs[:7], refs[7:9]
    held, semaphores = refs[9:16], refs[16]
    copies = [
        pltpu.make_async_copy(source, target, semaphores.at[index])
        for index, (source, target) in enumerate(zip(sources, held))
    ]
    for copy in copies:
        copy.start()
    for copy in copies:
        copy.wait()
    sizes_ref, d_ref, basis_ref, nt_ref, nc_ref, ut_ref, uc_ref = held
    probes, points = d_ref.shape
    ends = leaf_ends(sizes_ref, leaf_count)
    split = halves(d_ref[...])
    leaf = leaf_row(ends, 0, (2 * probes, points))
    zero = jnp.zeros_like(split)
    masked = jnp.concatenate(
        [jnp.where(leaf == index, split, zero) for index in range(leaf_count)], axis=0
    )
    raw = lax.dot_general(
        masked, basis_ref[...], (((1,), (1,)), ((), ())), preferred_element_type=F32
    )
    current = [
        folded(raw[2 * probes * index : 2 * probes * (index + 1)]) for index in range(leaf_count)
    ]
    rank = basis_ref.shape[0]
    while len(current) > 1:
        count = len(current)
        raised, sided = [], []
        for index in range(count):
            node = count - 1 + index
            both = jnp.concatenate([nt_ref[0, node], nc_ref[0, node]], axis=1)
            image = times(current[index], both)
            raised.append(image[:, :rank])
            sided.append(image[:, rank:])
        current = [raised[2 * i] + raised[2 * i + 1] for i in range(count // 2)]
        for i in range(count // 2):
            local_ref[count // 2 - 1 + i] = sided[2 * i] + sided[2 * i + 1]
    coefficient = current[0]
    for level in range(levels):
        coupling = nc_ref[0, 0] if level == 0 else uc_ref[0, level - 1]
        if level + 1 < levels:
            transfer = nt_ref[0, 0] if level == 0 else ut_ref[0, level - 1]
            image = times(coefficient, jnp.concatenate([transfer, coupling], axis=1))
            coefficient = image[:, :rank]
            up_ref[level] = image[:, rank:]
        else:
            up_ref[level] = times(coefficient, coupling)


def climb(sizes, vectors, levels):
    leaf_count = sizes.shape[1]
    probes, rank = vectors[0].shape[0], vectors[1].shape[0]
    arrays = (sizes, *vectors)
    return pl.pallas_call(
        functools.partial(up_kernel, leaf_count, levels),
        out_shape=(
            jax.ShapeDtypeStruct((levels, probes, rank), F32),
            jax.ShapeDtypeStruct((leaf_count - 1, probes, rank), F32),
        ),
        in_specs=[HBM] * len(arrays),
        out_specs=(VMEM, VMEM),
        scratch_shapes=[pltpu.SMEM(sizes.shape, sizes.dtype)]
        + [pltpu.VMEM(array.shape, array.dtype) for array in vectors]
        + [pltpu.SemaphoreType.DMA((len(arrays),))],
        compiler_params=PARAMS,
        name="climb",
    )(*(pltpu.with_memory_space_constraint(array, pltpu.HBM) for array in arrays))


def features_kernel(
    leaf_count,
    sizes_ref,
    length_ref,
    coords_ref,
    order_ref,
    d_ref,
    after_ref,
    left_ref,
    right_ref,
    dd_ref,
    ordered_ref,
):
    points = coords_ref.shape[1]
    chunks = points // 128
    ordered_ref[...] = jnp.zeros_like(ordered_ref)
    for group in range(chunks // 8):
        order = order_ref[8 * group : 8 * group + 8, :]
        chunk_of = lax.shift_right_logical(order, 7)
        lane_of = lax.bitwise_and(order, 127)
        for axis in range(3):
            found = jnp.zeros((8, 128), F32)
            for chunk in range(chunks):
                source = jnp.broadcast_to(
                    coords_ref[axis : axis + 1, 128 * chunk : 128 * chunk + 128], (8, 128)
                )
                picked = jnp.take_along_axis(source, lane_of, axis=1)
                found = jnp.where(chunk_of == chunk, picked, found)
            for row in range(8):
                place = 128 * (8 * group + row)
                ordered_ref[axis : axis + 1, place : place + 128] = found[row : row + 1, :]
    row8 = lax.broadcasted_iota(jnp.int32, (8, points), 0)
    scale = (math.sqrt(5.0) * LOG2E) / length_ref[...].reshape(1, 1)
    scaled = jnp.where(row8 < 3, (ordered_ref[...] - 0.5) * scale, 0.0)
    z1 = scaled.astype(BF16).astype(F32)
    z2 = (scaled - z1).astype(BF16).astype(F32)
    kept = z1 + z2
    norm = jnp.broadcast_to(jnp.sum(kept * kept, axis=0, keepdims=True), (8, points))
    n1 = norm.astype(BF16).astype(F32)
    n2 = (norm - n1).astype(BF16).astype(F32)
    n3 = norm - n1 - n2
    ends = leaf_ends(sizes_ref, leaf_count)
    leaf = leaf_row(ends, 0, (8, points))
    parts = jnp.where(row8 % 3 == 0, n1, jnp.where(row8 % 3 == 1, n2, n3))
    norm_left = jnp.where(row8 < 3, parts, jnp.where(row8 < 6, 1.0, 0.0))
    norm_right = jnp.where(row8 < 3, 1.0, jnp.where(row8 < 6, parts, 0.0))
    same = leaf == row8
    leaf_left = jnp.where(same, 1.0, 0.0)
    leaf_right = jnp.where(same, 0.0, FAR_AWAY)
    left = jnp.concatenate(
        [-2.0 * z1, -2.0 * z1, -2.0 * z2, -2.0 * z2, norm_left, leaf_left]
        + [jnp.zeros((80, points), F32)],
        axis=0,
    )
    right = jnp.concatenate(
        [z1, z2, z1, z2, norm_right, leaf_right], axis=0
    )
    right_ref[...] = right.astype(BF16)
    left_ref[:points, :] = left.T.astype(BF16)
    left_ref[points:, :] = jnp.zeros((STRIP, 128), BF16)
    split = halves(d_ref[...]).astype(F32)
    split = jnp.concatenate([split, jnp.zeros((128 - split.shape[0], points), F32)], axis=0)
    dd_ref[:points, :] = split.T.astype(BF16)
    dd_ref[points:, :] = jnp.zeros((TILE, 128), BF16)


def features(sizes, lengthscale, coordinates, order, direction, after):
    leaf_count = sizes.shape[1]
    points = direction.shape[1]
    return pl.pallas_call(
        functools.partial(features_kernel, leaf_count),
        out_shape=(
            jax.ShapeDtypeStruct((points + STRIP, 128), BF16),
            jax.ShapeDtypeStruct((48, points), BF16),
            jax.ShapeDtypeStruct((points + TILE, 128), BF16),
        ),
        in_specs=[SMEM, VMEM, VMEM, VMEM, VMEM, ANY],
        out_specs=(VMEM,) * 3,
        scratch_shapes=[pltpu.VMEM((8, points), F32)],
        compiler_params=PARAMS,
        name="features",
    )(sizes, lengthscale, coordinates, order.reshape(-1, 128), direction, after)


def strip_spans(ends, tiles):
    begins, counts = [], []
    for tile in range(tiles):
        first = tile * TILE
        last = first + TILE - 1
        low = 0
        high = ends[-1]
        for end in ends:
            low = jnp.where(end <= first, end, low)
        for end in ends[::-1]:
            high = jnp.where(end > last, end, high)
        low = lax.div(low, 128) * 128
        begins.append(low)
        counts.append(lax.div(high - low + (STRIP - 1), STRIP))
    return begins, counts


def near_kernel(leaf_count, part, sizes_ref, left_ref, right_ref, dd_ref, *refs):
    out_ref = refs[-1]
    ends = leaf_ends(sizes_ref, leaf_count)
    tiles = right_ref.shape[1] // TILE
    depth = right_ref.shape[0]
    begins, counts = strip_spans(ends, tiles)
    firsts = [0]
    for count in counts:
        firsts.append(firsts[-1] + count)
    groups = lax.div(firsts[-1] + (GROUP - 1), GROUP)
    offsets = [begin - first * STRIP for begin, first in zip(begins, firsts)]
    if part == 0:
        out_ref[...] = jnp.zeros_like(out_ref)

    def one_group(group, carry):
        for unit in range(GROUP):
            item = group * GROUP + unit
            tile_at = 0
            offset = offsets[0]
            for tile in range(1, tiles):
                inside = item >= firsts[tile]
                tile_at = jnp.where(inside, tile, tile_at)
                offset = jnp.where(inside, offsets[tile], offset)
            spare = item >= firsts[-1]
            begin = jnp.where(spare, 0, item * STRIP + offset)
            rows = pl.ds(pl.multiple_of(begin, 128), STRIP)
            columns = pl.ds(pl.multiple_of(tile_at * TILE, TILE), TILE)
            source = pl.ds(pl.multiple_of(jnp.where(spare, tiles, tile_at) * TILE, TILE), TILE)
            squared = jnp.dot(
                left_ref[rows, :depth], right_ref[:, columns], preferred_element_type=F32
            )
            squared = jnp.maximum(squared, 1e-12)
            root = squared * lax.rsqrt(squared)
            kernel = (squared + LINEAR * root + CONSTANT) * jnp.exp2(-root)
            high_part = kernel.astype(BF16)
            low_part = (kernel - high_part.astype(F32)).astype(BF16)
            weights = dd_ref[source, :]
            out_ref[rows, :] += jnp.dot(
                jnp.concatenate([high_part, low_part], axis=1),
                jnp.concatenate([weights, weights], axis=0),
                preferred_element_type=F32,
            )
        return carry

    lax.fori_loop(
        lax.div(groups * part, PARTS), lax.div(groups * (part + 1), PARTS), one_group, 0
    )


def near_part(sizes, prepared, before, after, part):
    leaf_count = sizes.shape[1]
    left, right, dd = prepared
    return pl.pallas_call(
        functools.partial(near_kernel, leaf_count, part),
        out_shape=jax.ShapeDtypeStruct(left.shape, F32),
        in_specs=[SMEM] + [VMEM] * (3 + len(before)) + [ANY],
        out_specs=VMEM,
        input_output_aliases={4: 0} if before else {},
        compiler_params=PARAMS,
        name="near_part",
    )(sizes, left, right, dd, *before, after)


def down_kernel(
    leaf_count,
    levels,
    sizes_ref,
    noise_ref,
    scale_ref,
    d_ref,
    r_ref,
    basis_ref,
    nt_ref,
    nc_ref,
    ut_ref,
    uc_ref,
    local_ref,
    *rest,
):
    side_refs = rest[:levels]
    near_ref, a_ref, sums_ref = rest[levels:]
    probes, points = d_ref.shape
    down = None
    for level in range(levels - 1, -1, -1):
        coupling = nc_ref[0, 0] if level == 0 else uc_ref[0, level - 1]
        side = side_refs[level][...]
        if down is None:
            down = times_transposed(side, coupling)
        else:
            transfer = nt_ref[0, 0] if level == 0 else ut_ref[0, level - 1]
            down = times_transposed(
                jnp.concatenate([down, side], axis=1),
                jnp.concatenate([transfer, coupling], axis=1),
            )
    current = [down]
    while len(current) < leaf_count:
        count = len(current)
        following = []
        for index in range(2 * count):
            node = 2 * count - 1 + index
            parent = index // 2
            following.append(
                times_transposed(
                    jnp.concatenate([current[parent], local_ref[count - 1 + parent]], axis=1),
                    jnp.concatenate([nt_ref[0, node], nc_ref[0, node]], axis=1),
                )
            )
        current = following
    stacked = jnp.concatenate([halves(term) for term in current], axis=0)
    ends = leaf_ends(sizes_ref, leaf_count)
    noise = noise_ref[...].reshape(1, 1)
    near_scale = scale_ref[...].reshape(1, 1) * POLY
    width = 512
    peak = jnp.zeros((probes, 128), F32)
    old = jnp.zeros((probes, 128), F32)
    curve = jnp.zeros((probes, 128), F32)

    def lanes(x):
        return sum(x[:, 128 * i : 128 * i + 128] for i in range(width // 128))

    for first in range(0, points, width):
        far_all = jnp.dot(
            stacked, basis_ref[:, first : first + width], preferred_element_type=F32
        )
        leaf = leaf_row(ends, first, (probes, width))
        far = folded(far_all[: 2 * probes])
        for index in range(1, leaf_count):
            term = folded(far_all[2 * probes * index : 2 * probes * (index + 1)])
            far = jnp.where(leaf == index, term, far)
        d = d_ref[:, first : first + width]
        r = r_ref[:, first : first + width]
        near = folded(near_ref[first : first + width, :].T[: 2 * probes])
        applied = noise * d + near_scale * near + far
        a_ref[:, first : first + width] = applied
        size = jnp.abs(applied)
        for i in range(width // 128):
            peak = jnp.maximum(peak, size[:, 128 * i : 128 * i + 128])
        old = old + lanes(r * r)
        curve = curve + lanes(d * applied)
    top = jnp.maximum(jnp.max(peak, axis=1, keepdims=True), 1e-30)
    inverse = 1.0 / top
    cross = jnp.zeros((probes, 128), F32)
    square = jnp.zeros((probes, 128), F32)
    for first in range(0, points, width):
        unit = a_ref[:, first : first + width] * inverse
        cross = cross + lanes(r_ref[:, first : first + width] * unit)
        square = square + lanes(unit * unit)
    columns = [jnp.sum(x, axis=1, keepdims=True) for x in (old, curve, cross, square)]
    lane = lax.broadcasted_iota(jnp.int32, (probes, 128), 1)
    quantity = lax.div(lane, probes)
    own = lax.rem(lane, probes) == lax.broadcasted_iota(jnp.int32, (probes, 128), 0)
    picked = columns[0]
    for index in range(1, 4):
        picked = jnp.where(quantity == index, columns[index], picked)
    row = jnp.concatenate(
        [
            jnp.sum(jnp.where(own, picked, 0.0), axis=0, keepdims=True),
            jnp.sum(jnp.where(own, top, 0.0), axis=0, keepdims=True),
        ],
        axis=1,
    )
    sums_ref[...] = row[None]


def descend(
    sizes, noise, scale, direction, residual, basis, node_transfer, node_coupling,
    upper_transfer, upper_coupling, local, sides, near,
):
    leaf_count = sizes.shape[1]
    probes, points = direction.shape
    return pl.pallas_call(
        functools.partial(down_kernel, leaf_count, len(sides)),
        out_shape=(
            jax.ShapeDtypeStruct((probes, points), F32),
            jax.ShapeDtypeStruct((1, 1, 256), F32),
        ),
        in_specs=[SMEM] + [VMEM] * (11 + len(sides)),
        out_specs=(VMEM, VMEM),
        compiler_params=PARAMS,
        name="descend",
    )(
        sizes, noise, scale, direction, residual, basis,
        node_transfer, node_coupling, upper_transfer, upper_coupling, local, *sides, near,
    )


def merged(sums, probes):
    values, tops = sums[:, :, :128], sums[:, :, 128:]
    top = jnp.max(tops, axis=0)
    ratio = tops / top
    quantity = lax.div(lax.broadcasted_iota(jnp.int32, (1, 1, 128), 2), probes)
    factor = jnp.where(quantity < 2, 1.0, jnp.where(quantity == 2, ratio, ratio * ratio))
    return jnp.sum(values * factor, axis=0), top


def pair_kernel(probes, own_ref, other_ref, out_ref):
    total, top = merged(jnp.concatenate([own_ref[...], other_ref[...]], axis=0), probes)
    out_ref[...] = jnp.broadcast_to(jnp.concatenate([total, top], axis=1)[None], out_ref.shape)


def merge_pair(own, other, probes, copies):
    return pl.pallas_call(
        functools.partial(pair_kernel, probes),
        out_shape=jax.ShapeDtypeStruct((copies, 1, 256), F32),
        in_specs=[VMEM, VMEM],
        out_specs=VMEM,
        compiler_params=PARAMS,
        name="merge_pair",
    )(own, other)


def step_kernel(sums_ref, x_ref, r_ref, d_ref, a_ref, nx_ref, nr_ref, nd_ref):
    probes = d_ref.shape[0]
    total, top = merged(sums_ref[...], probes)
    lane = lax.broadcasted_iota(jnp.int32, (probes, 128), 1)
    probe = lax.broadcasted_iota(jnp.int32, (probes, 128), 0)

    def column(row, index):
        return jnp.sum(
            jnp.where(lane == index * probes + probe, row, 0.0), axis=1, keepdims=True
        )

    old, curve, cross, square = (column(total, index) for index in range(4))
    step = old / curve
    reach = step * column(top, 0)
    fresh = old - 2.0 * (reach * cross) + (reach * reach) * square
    beta = fresh / old
    d = d_ref[...]
    nx_ref[...] = x_ref[...] + step * d
    remaining = r_ref[...] - step * a_ref[...]
    nr_ref[...] = remaining
    nd_ref[...] = remaining + beta * d


def finish(sums, solution_block, residual, direction, applied):
    shape = jax.ShapeDtypeStruct(direction.shape, F32)
    return pl.pallas_call(
        step_kernel,
        out_shape=(shape, shape, shape),
        in_specs=[VMEM] * 5,
        out_specs=(VMEM, VMEM, VMEM),
        compiler_params=PARAMS,
        name="finish",
    )(sums, solution_block, residual, direction, applied)


def from_partner(array, stride):
    count = lax.axis_size("leaf")
    return lax.ppermute(array, "leaf", [(i, i ^ stride) for i in range(count)])


def shards(
    solution,
    residual,
    direction,
    coordinates,
    cluster_order,
    leaf_sizes,
    leaf_basis,
    node_transfer,
    node_coupling,
    upper_transfer,
    upper_coupling,
    lengthscale,
    outputscale,
    noise_variance,
):
    levels = lax.axis_size("leaf").bit_length() - 1
    probes, points = direction.shape
    up, local = climb(
        leaf_sizes,
        (direction, leaf_basis, node_transfer, node_coupling, upper_transfer, upper_coupling),
        levels,
    )
    prepared = features(leaf_sizes, lengthscale, coordinates, cluster_order, direction, up)
    sides = []
    near = ()
    current = up
    for level in range(max(levels, PARTS)):
        if level < levels:
            incoming = from_partner(current, 2**level)
        if level < PARTS:
            near = (near_part(leaf_sizes, prepared, near, current, level),)
        if level < levels:
            current = current + incoming
            sides.append(current[0])
            current = current[1:] if level + 1 < levels else current
    near = near[0]
    applied, sums = descend(
        leaf_sizes, noise_variance, outputscale, direction, residual, leaf_basis,
        node_transfer, node_coupling, upper_transfer, upper_coupling, local, sides, near,
    )
    chips = lax.axis_size("leaf") // 2
    copies = merge_pair(sums, from_partner(sums, 1), probes, chips)
    gathered = lax.all_to_all(
        copies,
        "leaf",
        0,
        0,
        axis_index_groups=[[2 * chip + core for chip in range(chips)] for core in range(2)],
        tiled=True,
    )
    return finish(gathered, solution, residual, direction, applied)


def solution(mesh):
    in_specs = (
        P(None, "leaf"),
        P(None, "leaf"),
        P(None, "leaf"),
        P(None, "leaf"),
        P("leaf"),
        P("leaf", None),
        P(None, "leaf"),
        P("leaf", None, None, None),
        P("leaf", None, None, None),
        P("leaf", None, None, None),
        P("leaf", None, None, None),
        P(),
        P(),
        P(),
    )
    out_specs = (P(None, "leaf"), P(None, "leaf"), P(None, "leaf"))
    return jax.shard_map(shards, mesh=mesh, in_specs=in_specs, out_specs=out_specs, check_vma=False)
```

```python
import functools
import math

import jax
import jax.numpy as jnp
from jax import lax
from jax.experimental import pallas as pl
from jax.experimental.pallas import tpu as pltpu
from jax.sharding import PartitionSpec as P

F32 = jnp.float32
BF16 = jnp.bfloat16
TILE = 128
FAR_AWAY = 32768.0
LOG2E = 1.0 / math.log(2.0)
POLY = math.log(2.0) ** 2 / 3.0
LINEAR = 3.0 * LOG2E
CONSTANT = 3.0 * LOG2E * LOG2E

VMEM = pl.BlockSpec(memory_space=pltpu.VMEM)
SMEM = pl.BlockSpec(memory_space=pltpu.SMEM)
ANY = pl.BlockSpec(memory_space=pl.ANY)
HBM = pl.BlockSpec(memory_space=pltpu.HBM)
STRIP = 384
GROUP = 8
PARTS = 3
PARAMS = pltpu.CompilerParams(vmem_limit_bytes=48 * 1024 * 1024)


def halves(x):
    high = x.astype(BF16)
    low = (x - high.astype(F32)).astype(BF16)
    return jnp.concatenate([high, low], axis=0)


def folded(x):
    rows = x.shape[0] // 2
    return x[:rows] + x[rows:]


def times(x, generator):
    return folded(jnp.dot(halves(x), generator, preferred_element_type=F32))


def times_transposed(x, generator):
    return folded(
        lax.dot_general(
            halves(x), generator, (((1,), (1,)), ((), ())), preferred_element_type=F32
        )
    )


def leaf_ends(sizes_ref, leaf_count):
    ends = []
    total = 0
    for leaf in range(leaf_count):
        total = total + sizes_ref[0, leaf]
        ends.append(total)
    return ends


def leaf_row(ends, first, shape):
    positions = lax.broadcasted_iota(jnp.int32, shape, 1) + first
    leaf = jnp.zeros(shape, jnp.int32)
    for end in ends[:-1]:
        leaf = leaf + (positions >= end).astype(jnp.int32)
    return leaf


def up_kernel(leaf_count, levels, *refs):
    sources, (up_ref, local_ref) = refs[:7], refs[7:9]
    held, semaphores = refs[9:16], refs[16]
    copies = [
        pltpu.make_async_copy(source, target, semaphores.at[index])
        for index, (source, target) in enumerate(zip(sources, held))
    ]
    for copy in copies:
        copy.start()
    for copy in copies:
        copy.wait()
    sizes_ref, d_ref, basis_ref, nt_ref, nc_ref, ut_ref, uc_ref = held
    probes, points = d_ref.shape
    ends = leaf_ends(sizes_ref, leaf_count)
    split = halves(d_ref[...])
    leaf = leaf_row(ends, 0, (2 * probes, points))
    zero = jnp.zeros_like(split)
    masked = jnp.concatenate(
        [jnp.where(leaf == index, split, zero) for index in range(leaf_count)], axis=0
    )
    raw = lax.dot_general(
        masked, basis_ref[...], (((1,), (1,)), ((), ())), preferred_element_type=F32
    )
    current = [
        folded(raw[2 * probes * index : 2 * probes * (index + 1)]) for index in range(leaf_count)
    ]
    rank = basis_ref.shape[0]
    while len(current) > 1:
        count = len(current)
        raised, sided = [], []
        for index in range(count):
            node = count - 1 + index
            both = jnp.concatenate([nt_ref[0, node], nc_ref[0, node]], axis=1)
            image = times(current[index], both)
            raised.append(image[:, :rank])
            sided.append(image[:, rank:])
        current = [raised[2 * i] + raised[2 * i + 1] for i in range(count // 2)]
        for i in range(count // 2):
            local_ref[count // 2 - 1 + i] = sided[2 * i] + sided[2 * i + 1]
    coefficient = current[0]
    for level in range(levels):
        coupling = nc_ref[0, 0] if level == 0 else uc_ref[0, level - 1]
        if level + 1 < levels:
            transfer = nt_ref[0, 0] if level == 0 else ut_ref[0, level - 1]
            image = times(coefficient, jnp.concatenate([transfer, coupling], axis=1))
            coefficient = image[:, :rank]
            up_ref[level] = image[:, rank:]
        else:
            up_ref[level] = times(coefficient, coupling)


def climb(sizes, vectors, levels):
    leaf_count = sizes.shape[1]
    probes, rank = vectors[0].shape[0], vectors[1].shape[0]
    arrays = (sizes, *vectors)
    return pl.pallas_call(
        functools.partial(up_kernel, leaf_count, levels),
        out_shape=(
            jax.ShapeDtypeStruct((levels, probes, rank), F32),
            jax.ShapeDtypeStruct((leaf_count - 1, probes, rank), F32),
        ),
        in_specs=[HBM] * len(arrays),
        out_specs=(VMEM, VMEM),
        scratch_shapes=[pltpu.SMEM(sizes.shape, sizes.dtype)]
        + [pltpu.VMEM(array.shape, array.dtype) for array in vectors]
        + [pltpu.SemaphoreType.DMA((len(arrays),))],
        compiler_params=PARAMS,
        name="climb",
    )(*(pltpu.with_memory_space_constraint(array, pltpu.HBM) for array in arrays))


def features_kernel(
    leaf_count,
    sizes_ref,
    length_ref,
    coords_ref,
    order_ref,
    d_ref,
    after_ref,
    left_ref,
    right_ref,
    dd_ref,
    plan_ref,
    ordered_ref,
):
    points = coords_ref.shape[1]
    chunks = points // 128
    ordered_ref[...] = jnp.zeros_like(ordered_ref)
    for group in range(chunks // 8):
        order = order_ref[8 * group : 8 * group + 8, :]
        chunk_of = lax.shift_right_logical(order, 7)
        lane_of = lax.bitwise_and(order, 127)
        for axis in range(3):
            found = jnp.zeros((8, 128), F32)
            for chunk in range(chunks):
                source = jnp.broadcast_to(
                    coords_ref[axis : axis + 1, 128 * chunk : 128 * chunk + 128], (8, 128)
                )
                picked = jnp.take_along_axis(source, lane_of, axis=1)
                found = jnp.where(chunk_of == chunk, picked, found)
            for row in range(8):
                place = 128 * (8 * group + row)
                ordered_ref[axis : axis + 1, place : place + 128] = found[row : row + 1, :]
    row8 = lax.broadcasted_iota(jnp.int32, (8, points), 0)
    scale = (math.sqrt(5.0) * LOG2E) / length_ref[...].reshape(1, 1)
    scaled = jnp.where(row8 < 3, (ordered_ref[...] - 0.5) * scale, 0.0)
    z1 = scaled.astype(BF16).astype(F32)
    z2 = (scaled - z1).astype(BF16).astype(F32)
    kept = z1 + z2
    norm = jnp.broadcast_to(jnp.sum(kept * kept, axis=0, keepdims=True), (8, points))
    n1 = norm.astype(BF16).astype(F32)
    n2 = (norm - n1).astype(BF16).astype(F32)
    n3 = norm - n1 - n2
    ends = leaf_ends(sizes_ref, leaf_count)
    plan_ref[...] = near_plan(ends, points // TILE)
    leaf = leaf_row(ends, 0, (8, points))
    parts = jnp.where(row8 % 3 == 0, n1, jnp.where(row8 % 3 == 1, n2, n3))
    norm_left = jnp.where(row8 < 3, parts, jnp.where(row8 < 6, 1.0, 0.0))
    norm_right = jnp.where(row8 < 3, 1.0, jnp.where(row8 < 6, parts, 0.0))
    same = leaf == row8
    leaf_left = jnp.where(same, 1.0, 0.0)
    leaf_right = jnp.where(same, 0.0, FAR_AWAY)
    left = jnp.concatenate(
        [-2.0 * z1, -2.0 * z1, -2.0 * z2, -2.0 * z2, norm_left, leaf_left]
        + [jnp.zeros((80, points), F32)],
        axis=0,
    )
    right = jnp.concatenate(
        [z1, z2, z1, z2, norm_right, leaf_right], axis=0
    )
    right_ref[...] = right.astype(BF16)
    left_ref[:points, :] = left.T.astype(BF16)
    left_ref[points:, :] = jnp.zeros((STRIP, 128), BF16)
    split = halves(d_ref[...]).astype(F32)
    split = jnp.concatenate([split, jnp.zeros((128 - split.shape[0], points), F32)], axis=0)
    dd_ref[:points, :] = split.T.astype(BF16)
    dd_ref[points:, :] = jnp.zeros((TILE, 128), BF16)


def features(sizes, lengthscale, coordinates, order, direction, after):
    leaf_count = sizes.shape[1]
    points = direction.shape[1]
    return pl.pallas_call(
        functools.partial(features_kernel, leaf_count),
        out_shape=(
            jax.ShapeDtypeStruct((points + STRIP, 128), BF16),
            jax.ShapeDtypeStruct((48, points), BF16),
            jax.ShapeDtypeStruct((points + TILE, 128), BF16),
            jax.ShapeDtypeStruct((8, 128), jnp.int32),
        ),
        in_specs=[SMEM, VMEM, VMEM, VMEM, VMEM, ANY],
        out_specs=(VMEM,) * 4,
        scratch_shapes=[pltpu.VMEM((8, points), F32)],
        compiler_params=PARAMS,
        name="features",
    )(sizes, lengthscale, coordinates, order.reshape(-1, 128), direction, after)


def strip_spans(ends, tiles):
    begins, counts = [], []
    for tile in range(tiles):
        first = tile * TILE
        last = first + TILE - 1
        low = 0
        high = ends[-1]
        for end in ends:
            low = jnp.where(end <= first, end, low)
        for end in ends[::-1]:
            high = jnp.where(end > last, end, high)
        low = lax.div(low, 128) * 128
        begins.append(low)
        counts.append(lax.div(high - low + (STRIP - 1), STRIP))
    return begins, counts


def near_plan(ends, tiles):
    begins, counts = strip_spans(ends, tiles)
    item = lax.broadcasted_iota(jnp.int32, (8, 128), 1)
    first = 0
    begin = jnp.zeros((8, 128), jnp.int32)
    column = jnp.full((8, 128), tiles * TILE, jnp.int32)
    for tile, (low, count) in enumerate(zip(begins, counts)):
        inside = (item >= first) & (item < first + count)
        begin = jnp.where(inside, low + (item - first) * STRIP, begin)
        column = jnp.where(inside, tile * TILE, column)
        first = first + count
    groups = jnp.full((8, 128), lax.div(first + (GROUP - 1), GROUP), jnp.int32)
    row = lax.broadcasted_iota(jnp.int32, (8, 128), 0)
    return jnp.where(row == 0, begin, jnp.where(row == 1, column, groups))


def near_kernel(part, plan_ref, left_ref, right_ref, dd_ref, *refs):
    out_ref = refs[-1]
    depth, points = right_ref.shape
    groups = plan_ref[2, 0]
    if part == 0:
        out_ref[...] = jnp.zeros_like(out_ref)

    def one_group(group, carry):
        for unit in range(GROUP):
            item = group * GROUP + unit
            begin = plan_ref[0, item]
            column = plan_ref[1, item]
            rows = pl.ds(pl.multiple_of(begin, 128), STRIP)
            source = pl.ds(pl.multiple_of(column, TILE), TILE)
            columns = pl.ds(pl.multiple_of(jnp.minimum(column, points - TILE), TILE), TILE)
            squared = jnp.dot(
                left_ref[rows, :depth], right_ref[:, columns], preferred_element_type=F32
            )
            squared = jnp.maximum(squared, 1e-12)
            root = squared * lax.rsqrt(squared)
            kernel = (squared + LINEAR * root + CONSTANT) * jnp.exp2(-root)
            high_part = kernel.astype(BF16)
            low_part = (kernel - high_part.astype(F32)).astype(BF16)
            weights = dd_ref[source, :]
            out_ref[rows, :] += jnp.dot(
                jnp.concatenate([high_part, low_part], axis=1),
                jnp.concatenate([weights, weights], axis=0),
                preferred_element_type=F32,
            )
        return carry

    lax.fori_loop(
        lax.div(groups * part, PARTS), lax.div(groups * (part + 1), PARTS), one_group, 0
    )


def near_part(prepared, before, after, part):
    left, right, dd, plan = prepared
    return pl.pallas_call(
        functools.partial(near_kernel, part),
        out_shape=jax.ShapeDtypeStruct(left.shape, F32),
        in_specs=[SMEM] + [VMEM] * (3 + len(before)) + [ANY],
        out_specs=VMEM,
        input_output_aliases={4: 0} if before else {},
        compiler_params=PARAMS,
        name="near_part",
    )(plan, left, right, dd, *before, after)


def down_kernel(
    leaf_count,
    levels,
    sizes_ref,
    noise_ref,
    scale_ref,
    d_ref,
    r_ref,
    basis_ref,
    nt_ref,
    nc_ref,
    ut_ref,
    uc_ref,
    local_ref,
    *rest,
):
    side_refs = rest[:levels]
    near_ref, a_ref, sums_ref = rest[levels:]
    probes, points = d_ref.shape
    down = None
    for level in range(levels - 1, -1, -1):
        coupling = nc_ref[0, 0] if level == 0 else uc_ref[0, level - 1]
        side = side_refs[level][...]
        if down is None:
            down = times_transposed(side, coupling)
        else:
            transfer = nt_ref[0, 0] if level == 0 else ut_ref[0, level - 1]
            down = times_transposed(
                jnp.concatenate([down, side], axis=1),
                jnp.concatenate([transfer, coupling], axis=1),
            )
    current = [down]
    while len(current) < leaf_count:
        count = len(current)
        following = []
        for index in range(2 * count):
            node = 2 * count - 1 + index
            parent = index // 2
            following.append(
                times_transposed(
                    jnp.concatenate([current[parent], local_ref[count - 1 + parent]], axis=1),
                    jnp.concatenate([nt_ref[0, node], nc_ref[0, node]], axis=1),
                )
            )
        current = following
    stacked = jnp.concatenate([halves(term) for term in current], axis=0)
    ends = leaf_ends(sizes_ref, leaf_count)
    noise = noise_ref[...].reshape(1, 1)
    near_scale = scale_ref[...].reshape(1, 1) * POLY
    width = 512
    peak = jnp.zeros((probes, 128), F32)
    old = jnp.zeros((probes, 128), F32)
    curve = jnp.zeros((probes, 128), F32)

    def lanes(x):
        return sum(x[:, 128 * i : 128 * i + 128] for i in range(width // 128))

    for first in range(0, points, width):
        far_all = jnp.dot(
            stacked, basis_ref[:, first : first + width], preferred_element_type=F32
        )
        leaf = leaf_row(ends, first, (probes, width))
        far = folded(far_all[: 2 * probes])
        for index in range(1, leaf_count):
            term = folded(far_all[2 * probes * index : 2 * probes * (index + 1)])
            far = jnp.where(leaf == index, term, far)
        d = d_ref[:, first : first + width]
        r = r_ref[:, first : first + width]
        near = folded(near_ref[first : first + width, :].T[: 2 * probes])
        applied = noise * d + near_scale * near + far
        a_ref[:, first : first + width] = applied
        size = jnp.abs(applied)
        for i in range(width // 128):
            peak = jnp.maximum(peak, size[:, 128 * i : 128 * i + 128])
        old = old + lanes(r * r)
        curve = curve + lanes(d * applied)
    top = jnp.maximum(jnp.max(peak, axis=1, keepdims=True), 1e-30)
    inverse = 1.0 / top
    cross = jnp.zeros((probes, 128), F32)
    square = jnp.zeros((probes, 128), F32)
    for first in range(0, points, width):
        unit = a_ref[:, first : first + width] * inverse
        cross = cross + lanes(r_ref[:, first : first + width] * unit)
        square = square + lanes(unit * unit)
    columns = [jnp.sum(x, axis=1, keepdims=True) for x in (old, curve, cross, square)]
    lane = lax.broadcasted_iota(jnp.int32, (probes, 128), 1)
    quantity = lax.div(lane, probes)
    own = lax.rem(lane, probes) == lax.broadcasted_iota(jnp.int32, (probes, 128), 0)
    picked = columns[0]
    for index in range(1, 4):
        picked = jnp.where(quantity == index, columns[index], picked)
    row = jnp.concatenate(
        [
            jnp.sum(jnp.where(own, picked, 0.0), axis=0, keepdims=True),
            jnp.sum(jnp.where(own, top, 0.0), axis=0, keepdims=True),
        ],
        axis=1,
    )
    sums_ref[...] = jnp.broadcast_to(row[None], sums_ref.shape)


def descend(
    sizes, noise, scale, direction, residual, basis, node_transfer, node_coupling,
    upper_transfer, upper_coupling, local, sides, near,
):
    leaf_count = sizes.shape[1]
    probes, points = direction.shape
    return pl.pallas_call(
        functools.partial(down_kernel, leaf_count, len(sides)),
        out_shape=(
            jax.ShapeDtypeStruct((probes, points), F32),
            jax.ShapeDtypeStruct((2 ** len(sides), 1, 256), F32),
        ),
        in_specs=[SMEM] + [VMEM] * (11 + len(sides)),
        out_specs=(VMEM, VMEM),
        compiler_params=PARAMS,
        name="descend",
    )(
        sizes, noise, scale, direction, residual, basis,
        node_transfer, node_coupling, upper_transfer, upper_coupling, local, *sides, near,
    )


def merged(sums, probes):
    values, tops = sums[:, :, :128], sums[:, :, 128:]
    top = jnp.max(tops, axis=0)
    ratio = tops / top
    quantity = lax.div(lax.broadcasted_iota(jnp.int32, (1, 1, 128), 2), probes)
    factor = jnp.where(quantity < 2, 1.0, jnp.where(quantity == 2, ratio, ratio * ratio))
    return jnp.sum(values * factor, axis=0), top


def step_kernel(sums_ref, x_ref, r_ref, d_ref, a_ref, nx_ref, nr_ref, nd_ref):
    probes = d_ref.shape[0]
    total, top = merged(sums_ref[...], probes)
    lane = lax.broadcasted_iota(jnp.int32, (probes, 128), 1)
    probe = lax.broadcasted_iota(jnp.int32, (probes, 128), 0)

    def column(row, index):
        return jnp.sum(
            jnp.where(lane == index * probes + probe, row, 0.0), axis=1, keepdims=True
        )

    old, curve, cross, square = (column(total, index) for index in range(4))
    step = old / curve
    reach = step * column(top, 0)
    fresh = old - 2.0 * (reach * cross) + (reach * reach) * square
    beta = fresh / old
    d = d_ref[...]
    nx_ref[...] = x_ref[...] + step * d
    remaining = r_ref[...] - step * a_ref[...]
    nr_ref[...] = remaining
    nd_ref[...] = remaining + beta * d


def finish(sums, solution_block, residual, direction, applied):
    shape = jax.ShapeDtypeStruct(direction.shape, F32)
    return pl.pallas_call(
        step_kernel,
        out_shape=(shape, shape, shape),
        in_specs=[VMEM] * 5,
        out_specs=(VMEM, VMEM, VMEM),
        compiler_params=PARAMS,
        name="finish",
    )(sums, solution_block, residual, direction, applied)


def from_partner(array, stride):
    count = lax.axis_size("leaf")
    return lax.ppermute(array, "leaf", [(i, i ^ stride) for i in range(count)])


def shards(
    solution,
    residual,
    direction,
    coordinates,
    cluster_order,
    leaf_sizes,
    leaf_basis,
    node_transfer,
    node_coupling,
    upper_transfer,
    upper_coupling,
    lengthscale,
    outputscale,
    noise_variance,
):
    levels = lax.axis_size("leaf").bit_length() - 1
    probes, points = direction.shape
    up, local = climb(
        leaf_sizes,
        (direction, leaf_basis, node_transfer, node_coupling, upper_transfer, upper_coupling),
        levels,
    )
    sides = []
    near = ()
    current = up
    for level in range(max(levels, PARTS + 2)):
        if level < levels:
            incoming = from_partner(current, 2**level)
        if level == 1:
            prepared = features(
                leaf_sizes, lengthscale, coordinates, cluster_order, direction, current
            )
        if 2 <= level < PARTS + 2:
            near = (near_part(prepared, near, current, level - 2),)
        if level < levels:
            current = current + incoming
            sides.append(current[0])
            current = current[1:] if level + 1 < levels else current
            if level == 1:
                current, *prepared = lax.optimization_barrier((current, *prepared))
            elif near and level < PARTS + 2:
                current, *near = lax.optimization_barrier((current, *near))
    near = near[0]
    applied, sums = descend(
        leaf_sizes, noise_variance, outputscale, direction, residual, leaf_basis,
        node_transfer, node_coupling, upper_transfer, upper_coupling, local, sides, near,
    )
    gathered = lax.all_to_all(sums, "leaf", 0, 0, tiled=True)
    return finish(gathered, solution, residual, direction, applied)


def solution(mesh):
    in_specs = (
        P(None, "leaf"),
        P(None, "leaf"),
        P(None, "leaf"),
        P(None, "leaf"),
        P("leaf"),
        P("leaf", None),
        P(None, "leaf"),
        P("leaf", None, None, None),
        P("leaf", None, None, None),
        P("leaf", None, None, None),
        P("leaf", None, None, None),
        P(),
        P(),
        P(),
    )
    out_specs = (P(None, "leaf"), P(None, "leaf"), P(None, "leaf"))
    return jax.shard_map(shards, mesh=mesh, in_specs=in_specs, out_specs=out_specs, check_vma=False)
```

```python
import functools
import math

import jax
import jax.numpy as jnp
from jax import lax
from jax.experimental import pallas as pl
from jax.experimental.pallas import tpu as pltpu
from jax.sharding import PartitionSpec as P

F32 = jnp.float32
BF16 = jnp.bfloat16
TILE = 256
FAR_AWAY = 32768.0
LOG2E = 1.0 / math.log(2.0)
POLY = math.log(2.0) ** 2 / 3.0
LINEAR = 3.0 * LOG2E
CONSTANT = 3.0 * LOG2E * LOG2E

VMEM = pl.BlockSpec(memory_space=pltpu.VMEM)
SMEM = pl.BlockSpec(memory_space=pltpu.SMEM)
ANY = pl.BlockSpec(memory_space=pl.ANY)
HBM = pl.BlockSpec(memory_space=pltpu.HBM)
STRIP = 384
GROUP = 4
PARTS = 3
BLOCKS = 3
PARAMS = pltpu.CompilerParams(vmem_limit_bytes=48 * 1024 * 1024)


def halves(x):
    high = x.astype(BF16)
    low = (x - high.astype(F32)).astype(BF16)
    return jnp.concatenate([high, low], axis=0)


def folded(x):
    rows = x.shape[0] // 2
    return x[:rows] + x[rows:]


def times(x, generator):
    return folded(jnp.dot(halves(x), generator, preferred_element_type=F32))


def times_transposed(x, generator):
    return folded(
        lax.dot_general(
            halves(x), generator, (((1,), (1,)), ((), ())), preferred_element_type=F32
        )
    )


def leaf_ends(sizes_ref, leaf_count):
    ends = []
    total = 0
    for leaf in range(leaf_count):
        total = total + sizes_ref[0, leaf]
        ends.append(total)
    return ends


def leaf_row(ends, first, shape):
    positions = lax.broadcasted_iota(jnp.int32, shape, 1) + first
    leaf = jnp.zeros(shape, jnp.int32)
    for end in ends[:-1]:
        leaf = leaf + (positions >= end).astype(jnp.int32)
    return leaf


def up_kernel(leaf_count, levels, *refs):
    sources, (up_ref, local_ref) = refs[:7], refs[7:9]
    held, semaphores = refs[9:16], refs[16]
    sizes_ref, d_ref, basis_ref, nt_ref, nc_ref, ut_ref, uc_ref = held
    probes, points = d_ref.shape
    block = points // BLOCKS

    def copy(index, place, window=None):
        source, target = sources[index], held[index]
        if window is not None:
            source, target = source.at[:, window], target.at[:, window]
        return pltpu.make_async_copy(source, target, semaphores.at[place])

    windows = [pl.ds(block * number, block) for number in range(BLOCKS)]
    first = [copy(0, 0)]
    blocks = [
        [copy(1, 1 + 2 * number, window), copy(2, 2 + 2 * number, window)]
        for number, window in enumerate(windows)
    ]
    others = [copy(index, 2 * BLOCKS + index - 2) for index in range(3, 7)]
    for pending in first + sum(blocks, []) + others:
        pending.start()
    first[0].wait()
    ends = leaf_ends(sizes_ref, leaf_count)
    raw = jnp.zeros((2 * probes * leaf_count, basis_ref.shape[0]), F32)
    for number, window in enumerate(windows):
        for pending in blocks[number]:
            pending.wait()
        split = halves(d_ref[:, window])
        leaf = leaf_row(ends, block * number, split.shape)
        zero = jnp.zeros_like(split)
        masked = jnp.concatenate(
            [jnp.where(leaf == index, split, zero) for index in range(leaf_count)], axis=0
        )
        raw = raw + lax.dot_general(
            masked, basis_ref[:, window], (((1,), (1,)), ((), ())), preferred_element_type=F32
        )
    for pending in others:
        pending.wait()
    current = [
        folded(raw[2 * probes * index : 2 * probes * (index + 1)]) for index in range(leaf_count)
    ]
    rank = basis_ref.shape[0]
    while len(current) > 1:
        count = len(current)
        raised, sided = [], []
        for index in range(count):
            node = count - 1 + index
            both = jnp.concatenate([nt_ref[0, node], nc_ref[0, node]], axis=1)
            image = times(current[index], both)
            raised.append(image[:, :rank])
            sided.append(image[:, rank:])
        current = [raised[2 * i] + raised[2 * i + 1] for i in range(count // 2)]
        for i in range(count // 2):
            local_ref[count // 2 - 1 + i] = sided[2 * i] + sided[2 * i + 1]
    coefficient = current[0]
    for level in range(levels):
        coupling = nc_ref[0, 0] if level == 0 else uc_ref[0, level - 1]
        if level + 1 < levels:
            transfer = nt_ref[0, 0] if level == 0 else ut_ref[0, level - 1]
            image = times(coefficient, jnp.concatenate([transfer, coupling], axis=1))
            coefficient = image[:, :rank]
            up_ref[level] = image[:, rank:]
        else:
            up_ref[level] = times(coefficient, coupling)


def climb(sizes, vectors, levels):
    leaf_count = sizes.shape[1]
    probes, rank = vectors[0].shape[0], vectors[1].shape[0]
    arrays = (sizes, *vectors)
    return pl.pallas_call(
        functools.partial(up_kernel, leaf_count, levels),
        out_shape=(
            jax.ShapeDtypeStruct((levels, probes, rank), F32),
            jax.ShapeDtypeStruct((leaf_count - 1, probes, rank), F32),
        ),
        in_specs=[HBM] * len(arrays),
        out_specs=(VMEM, VMEM),
        scratch_shapes=[pltpu.SMEM(sizes.shape, sizes.dtype)]
        + [pltpu.VMEM(array.shape, array.dtype) for array in vectors]
        + [pltpu.SemaphoreType.DMA((2 * BLOCKS + 5,))],
        compiler_params=PARAMS,
        name="climb",
    )(*(pltpu.with_memory_space_constraint(array, pltpu.HBM) for array in arrays))


def features_kernel(
    leaf_count,
    sizes_ref,
    scalars_ref,
    coords_ref,
    order_ref,
    d_ref,
    after_ref,
    left_ref,
    right_ref,
    dd_ref,
    plan_ref,
    ordered_ref,
):
    points = coords_ref.shape[1]
    chunks = points // 128
    ordered_ref[...] = jnp.zeros_like(ordered_ref)
    for group in range(chunks // 8):
        order = order_ref[8 * group : 8 * group + 8, :]
        chunk_of = lax.shift_right_logical(order, 7)
        lane_of = lax.bitwise_and(order, 127)
        for axis in range(3):
            found = jnp.zeros((8, 128), F32)
            for chunk in range(chunks):
                source = jnp.broadcast_to(
                    coords_ref[axis : axis + 1, 128 * chunk : 128 * chunk + 128], (8, 128)
                )
                picked = jnp.take_along_axis(source, lane_of, axis=1)
                found = jnp.where(chunk_of == chunk, picked, found)
            for row in range(8):
                place = 128 * (8 * group + row)
                ordered_ref[axis : axis + 1, place : place + 128] = found[row : row + 1, :]
    row8 = lax.broadcasted_iota(jnp.int32, (8, points), 0)
    scale = (math.sqrt(5.0) * LOG2E) / scalars_ref[0:1, 0:1]
    scaled = jnp.where(row8 < 3, (ordered_ref[...] - 0.5) * scale, 0.0)
    z1 = scaled.astype(BF16).astype(F32)
    z2 = (scaled - z1).astype(BF16).astype(F32)
    kept = z1 + z2
    norm = jnp.broadcast_to(jnp.sum(kept * kept, axis=0, keepdims=True), (8, points))
    n1 = norm.astype(BF16).astype(F32)
    n2 = (norm - n1).astype(BF16).astype(F32)
    n3 = norm - n1 - n2
    ends = leaf_ends(sizes_ref, leaf_count)
    plan_ref[...] = near_plan(ends, points // TILE)
    leaf = leaf_row(ends, 0, (8, points))
    parts = jnp.where(row8 % 3 == 0, n1, jnp.where(row8 % 3 == 1, n2, n3))
    norm_left = jnp.where(row8 < 3, parts, jnp.where(row8 < 6, 1.0, 0.0))
    norm_right = jnp.where(row8 < 3, 1.0, jnp.where(row8 < 6, parts, 0.0))
    same = leaf == row8
    leaf_left = jnp.where(same, 1.0, 0.0)
    leaf_right = jnp.where(same, 0.0, FAR_AWAY)
    left = jnp.concatenate(
        [-2.0 * z1, -2.0 * z1, -2.0 * z2, -2.0 * z2, norm_left, leaf_left]
        + [jnp.zeros((80, points), F32)],
        axis=0,
    )
    right = jnp.concatenate(
        [z1, z2, z1, z2, norm_right, leaf_right], axis=0
    )
    right_ref[...] = right.astype(BF16)
    left_ref[:points, :] = left.T.astype(BF16)
    left_ref[points:, :] = jnp.zeros((STRIP, 128), BF16)
    split = halves(d_ref[...]).astype(F32)
    split = jnp.concatenate([split, jnp.zeros((128 - split.shape[0], points), F32)], axis=0)
    dd_ref[:points, :] = split.T.astype(BF16)
    dd_ref[points:, :] = jnp.zeros((TILE, 128), BF16)


def scalars_kernel(length_ref, scale_ref, noise_ref, after_ref, out_ref):
    row = lax.broadcasted_iota(jnp.int32, out_ref.shape, 0)
    out_ref[...] = jnp.where(
        row == 0, length_ref[0], jnp.where(row == 1, scale_ref[0], noise_ref[0])
    )


def spread_scalars(lengthscale, outputscale, noise_variance, after):
    return pl.pallas_call(
        scalars_kernel,
        out_shape=jax.ShapeDtypeStruct((8, 128), F32),
        in_specs=[SMEM, SMEM, SMEM, ANY],
        out_specs=VMEM,
        compiler_params=PARAMS,
        name="spread_scalars",
    )(lengthscale, outputscale, noise_variance, after)


def features(sizes, scalars, coordinates, order, direction, after):
    leaf_count = sizes.shape[1]
    points = direction.shape[1]
    return pl.pallas_call(
        functools.partial(features_kernel, leaf_count),
        out_shape=(
            jax.ShapeDtypeStruct((points + STRIP, 128), BF16),
            jax.ShapeDtypeStruct((48, points), BF16),
            jax.ShapeDtypeStruct((points + TILE, 128), BF16),
            jax.ShapeDtypeStruct((8, 128), jnp.int32),
        ),
        in_specs=[SMEM, VMEM, VMEM, VMEM, VMEM, ANY],
        out_specs=(VMEM,) * 4,
        scratch_shapes=[pltpu.VMEM((8, points), F32)],
        compiler_params=PARAMS,
        name="features",
    )(sizes, scalars, coordinates, order.reshape(-1, 128), direction, after)


def strip_spans(ends, tiles):
    begins, counts = [], []
    for tile in range(tiles):
        first = tile * TILE
        last = first + TILE - 1
        low = 0
        high = ends[-1]
        for end in ends:
            low = jnp.where(end <= first, end, low)
        for end in ends[::-1]:
            high = jnp.where(end > last, end, high)
        low = lax.div(low, 128) * 128
        begins.append(low)
        counts.append(lax.div(high - low + (STRIP - 1), STRIP))
    return begins, counts


def near_plan(ends, tiles):
    begins, counts = strip_spans(ends, tiles)
    item = lax.broadcasted_iota(jnp.int32, (8, 128), 1)
    first = 0
    begin = jnp.zeros((8, 128), jnp.int32)
    column = jnp.full((8, 128), tiles * TILE, jnp.int32)
    for tile, (low, count) in enumerate(zip(begins, counts)):
        inside = (item >= first) & (item < first + count)
        begin = jnp.where(inside, low + (item - first) * STRIP, begin)
        column = jnp.where(inside, tile * TILE, column)
        first = first + count
    groups = jnp.full((8, 128), lax.div(first + (GROUP - 1), GROUP), jnp.int32)
    row = lax.broadcasted_iota(jnp.int32, (8, 128), 0)
    return jnp.where(row == 0, begin, jnp.where(row == 1, column, groups))


def near_kernel(part, plan_ref, left_ref, right_ref, dd_ref, *refs):
    out_ref = refs[-1]
    depth, points = right_ref.shape
    groups = plan_ref[2, 0]
    if part == 0:
        out_ref[...] = jnp.zeros_like(out_ref)

    def one_group(group, carry):
        for unit in range(GROUP):
            item = group * GROUP + unit
            begin = plan_ref[0, item]
            column = plan_ref[1, item]
            rows = pl.ds(pl.multiple_of(begin, 128), STRIP)
            source = pl.ds(pl.multiple_of(column, TILE), TILE)
            columns = pl.ds(pl.multiple_of(jnp.minimum(column, points - TILE), TILE), TILE)
            squared = jnp.dot(
                left_ref[rows, :depth], right_ref[:, columns], preferred_element_type=F32
            )
            squared = jnp.maximum(squared, 1e-12)
            root = squared * lax.rsqrt(squared)
            kernel = (squared + LINEAR * root + CONSTANT) * jnp.exp2(-root)
            high_part = kernel.astype(BF16)
            low_part = (kernel - high_part.astype(F32)).astype(BF16)
            both = jnp.dot(
                jnp.concatenate([high_part, low_part], axis=0),
                dd_ref[source, :],
                preferred_element_type=F32,
            )
            out_ref[rows, :] += folded(both)
        return carry

    lax.fori_loop(
        lax.div(groups * part, PARTS), lax.div(groups * (part + 1), PARTS), one_group, 0
    )


def near_part(prepared, before, after, part):
    left, right, dd, plan = prepared
    return pl.pallas_call(
        functools.partial(near_kernel, part),
        out_shape=jax.ShapeDtypeStruct(left.shape, F32),
        in_specs=[SMEM] + [VMEM] * (3 + len(before)) + [ANY],
        out_specs=VMEM,
        input_output_aliases={4: 0} if before else {},
        compiler_params=PARAMS,
        name="near_part",
    )(plan, left, right, dd, *before, after)


def down_kernel(
    leaf_count,
    levels,
    sizes_ref,
    scalars_ref,
    d_ref,
    r_ref,
    basis_ref,
    nt_ref,
    nc_ref,
    ut_ref,
    uc_ref,
    local_ref,
    *rest,
):
    side_refs = rest[:levels]
    near_ref, a_ref, sums_ref = rest[levels:]
    probes, points = d_ref.shape
    down = None
    for level in range(levels - 1, -1, -1):
        coupling = nc_ref[0, 0] if level == 0 else uc_ref[0, level - 1]
        side = side_refs[level][...]
        if down is None:
            down = times_transposed(side, coupling)
        else:
            transfer = nt_ref[0, 0] if level == 0 else ut_ref[0, level - 1]
            down = times_transposed(
                jnp.concatenate([down, side], axis=1),
                jnp.concatenate([transfer, coupling], axis=1),
            )
    current = [down]
    while len(current) < leaf_count:
        count = len(current)
        following = []
        for index in range(2 * count):
            node = 2 * count - 1 + index
            parent = index // 2
            following.append(
                times_transposed(
                    jnp.concatenate([current[parent], local_ref[count - 1 + parent]], axis=1),
                    jnp.concatenate([nt_ref[0, node], nc_ref[0, node]], axis=1),
                )
            )
        current = following
    stacked = jnp.concatenate([halves(term) for term in current], axis=0)
    ends = leaf_ends(sizes_ref, leaf_count)
    noise = scalars_ref[2:3, 0:1]
    near_scale = scalars_ref[1:2, 0:1] * POLY
    width = 512
    peak = jnp.zeros((probes, 128), F32)
    old = jnp.zeros((probes, 128), F32)
    curve = jnp.zeros((probes, 128), F32)

    def lanes(x):
        return sum(x[:, 128 * i : 128 * i + 128] for i in range(width // 128))

    for first in range(0, points, width):
        far_all = jnp.dot(
            stacked, basis_ref[:, first : first + width], preferred_element_type=F32
        )
        leaf = leaf_row(ends, first, (probes, width))
        far = folded(far_all[: 2 * probes])
        for index in range(1, leaf_count):
            term = folded(far_all[2 * probes * index : 2 * probes * (index + 1)])
            far = jnp.where(leaf == index, term, far)
        d = d_ref[:, first : first + width]
        r = r_ref[:, first : first + width]
        near = folded(near_ref[first : first + width, :].T[: 2 * probes])
        applied = noise * d + near_scale * near + far
        a_ref[:, first : first + width] = applied
        size = jnp.abs(applied)
        for i in range(width // 128):
            peak = jnp.maximum(peak, size[:, 128 * i : 128 * i + 128])
        old = old + lanes(r * r)
        curve = curve + lanes(d * applied)
    top = jnp.maximum(jnp.max(peak, axis=1, keepdims=True), 1e-30)
    inverse = 1.0 / top
    cross = jnp.zeros((probes, 128), F32)
    square = jnp.zeros((probes, 128), F32)
    for first in range(0, points, width):
        unit = a_ref[:, first : first + width] * inverse
        cross = cross + lanes(r_ref[:, first : first + width] * unit)
        square = square + lanes(unit * unit)
    columns = [jnp.sum(x, axis=1, keepdims=True) for x in (old, curve, cross, square)]
    lane = lax.broadcasted_iota(jnp.int32, (probes, 128), 1)
    quantity = lax.div(lane, probes)
    own = lax.rem(lane, probes) == lax.broadcasted_iota(jnp.int32, (probes, 128), 0)
    picked = columns[0]
    for index in range(1, 4):
        picked = jnp.where(quantity == index, columns[index], picked)
    row = jnp.concatenate(
        [
            jnp.sum(jnp.where(own, picked, 0.0), axis=0, keepdims=True),
            jnp.sum(jnp.where(own, top, 0.0), axis=0, keepdims=True),
        ],
        axis=1,
    )
    sums_ref[...] = jnp.broadcast_to(row[None], sums_ref.shape)


def descend(
    sizes, scalars, direction, residual, basis, node_transfer, node_coupling,
    upper_transfer, upper_coupling, local, sides, near,
):
    leaf_count = sizes.shape[1]
    probes, points = direction.shape
    return pl.pallas_call(
        functools.partial(down_kernel, leaf_count, len(sides)),
        out_shape=(
            jax.ShapeDtypeStruct((probes, points), F32),
            jax.ShapeDtypeStruct((2 ** len(sides), 1, 256), F32),
        ),
        in_specs=[SMEM] + [VMEM] * (10 + len(sides)),
        out_specs=(VMEM, VMEM),
        compiler_params=PARAMS,
        name="descend",
    )(
        sizes, scalars, direction, residual, basis,
        node_transfer, node_coupling, upper_transfer, upper_coupling, local, *sides, near,
    )


def merged(sums, probes):
    values, tops = sums[:, :, :128], sums[:, :, 128:]
    top = jnp.max(tops, axis=0)
    ratio = tops / top
    quantity = lax.div(lax.broadcasted_iota(jnp.int32, (1, 1, 128), 2), probes)
    factor = jnp.where(quantity < 2, 1.0, jnp.where(quantity == 2, ratio, ratio * ratio))
    return jnp.sum(values * factor, axis=0), top


def step_kernel(sums_ref, x_ref, r_ref, d_ref, a_ref, nx_ref, nr_ref, nd_ref):
    probes = d_ref.shape[0]
    total, top = merged(sums_ref[...], probes)
    lane = lax.broadcasted_iota(jnp.int32, (probes, 128), 1)
    probe = lax.broadcasted_iota(jnp.int32, (probes, 128), 0)

    def column(row, index):
        return jnp.sum(
            jnp.where(lane == index * probes + probe, row, 0.0), axis=1, keepdims=True
        )

    old, curve, cross, square = (column(total, index) for index in range(4))
    step = old / curve
    reach = step * column(top, 0)
    fresh = old - 2.0 * (reach * cross) + (reach * reach) * square
    beta = fresh / old
    d = d_ref[...]
    nx_ref[...] = x_ref[...] + step * d
    remaining = r_ref[...] - step * a_ref[...]
    nr_ref[...] = remaining
    nd_ref[...] = remaining + beta * d


def finish(sums, solution_block, residual, direction, applied):
    shape = jax.ShapeDtypeStruct(direction.shape, F32)
    return pl.pallas_call(
        step_kernel,
        out_shape=(shape, shape, shape),
        in_specs=[VMEM] * 5,
        out_specs=(VMEM, VMEM, VMEM),
        compiler_params=PARAMS,
        name="finish",
    )(sums, solution_block, residual, direction, applied)


def from_partner(array, stride):
    count = lax.axis_size("leaf")
    return lax.ppermute(array, "leaf", [(i, i ^ stride) for i in range(count)])


def shards(
    solution,
    residual,
    direction,
    coordinates,
    cluster_order,
    leaf_sizes,
    leaf_basis,
    node_transfer,
    node_coupling,
    upper_transfer,
    upper_coupling,
    lengthscale,
    outputscale,
    noise_variance,
):
    levels = lax.axis_size("leaf").bit_length() - 1
    probes, points = direction.shape
    up, local = climb(
        leaf_sizes,
        (direction, leaf_basis, node_transfer, node_coupling, upper_transfer, upper_coupling),
        levels,
    )
    sides = []
    near = ()
    current = up
    for level in range(max(levels, PARTS + 2)):
        if level < levels:
            incoming = from_partner(current, 2**level)
        if level == 0:
            scalars = spread_scalars(lengthscale, outputscale, noise_variance, current)
        if level == 1:
            prepared = features(
                leaf_sizes, scalars, coordinates, cluster_order, direction, current
            )
        if 2 <= level < PARTS + 2:
            near = (near_part(prepared, near, current, level - 2),)
        if level < levels:
            current = current + incoming
            sides.append(current[0])
            current = current[1:] if level + 1 < levels else current
            if level == 0:
                current, scalars = lax.optimization_barrier((current, scalars))
            elif level == 1:
                current, *prepared = lax.optimization_barrier((current, *prepared))
            elif near and level < PARTS + 2:
                current, *near = lax.optimization_barrier((current, *near))
    near = near[0]
    applied, sums = descend(
        leaf_sizes, scalars, direction, residual, leaf_basis,
        node_transfer, node_coupling, upper_transfer, upper_coupling, local, sides, near,
    )
    gathered = lax.all_to_all(sums, "leaf", 0, 0, tiled=True)
    return finish(gathered, solution, residual, direction, applied)


def solution(mesh):
    in_specs = (
        P(None, "leaf"),
        P(None, "leaf"),
        P(None, "leaf"),
        P(None, "leaf"),
        P("leaf"),
        P("leaf", None),
        P(None, "leaf"),
        P("leaf", None, None, None),
        P("leaf", None, None, None),
        P("leaf", None, None, None),
        P("leaf", None, None, None),
        P(),
        P(),
        P(),
    )
    out_specs = (P(None, "leaf"), P(None, "leaf"), P(None, "leaf"))
    return jax.shard_map(shards, mesh=mesh, in_specs=in_specs, out_specs=out_specs, check_vma=False)
```

```python
import functools
import math

import jax
import jax.numpy as jnp
from jax import lax
from jax.experimental import pallas as pl
from jax.experimental.pallas import tpu as pltpu
from jax.sharding import PartitionSpec as P

F32 = jnp.float32
BF16 = jnp.bfloat16
TILE = 256
FAR_AWAY = 32768.0
THIRD = 1.0 / 3.0
DECAY = -3.0 / math.log(2.0)

VMEM = pl.BlockSpec(memory_space=pltpu.VMEM)
SMEM = pl.BlockSpec(memory_space=pltpu.SMEM)
ANY = pl.BlockSpec(memory_space=pl.ANY)
HBM = pl.BlockSpec(memory_space=pltpu.HBM)
STRIP = 384
GROUP = 4
PARTS = 3
BLOCKS = 3
PARAMS = pltpu.CompilerParams(vmem_limit_bytes=48 * 1024 * 1024)


def halves(x):
    high = x.astype(BF16)
    low = (x - high.astype(F32)).astype(BF16)
    return jnp.concatenate([high, low], axis=0)


def folded(x):
    rows = x.shape[0] // 2
    return x[:rows] + x[rows:]


def times(x, generator):
    return folded(jnp.dot(halves(x), generator, preferred_element_type=F32))


def times_transposed(x, generator):
    return folded(
        lax.dot_general(
            halves(x), generator, (((1,), (1,)), ((), ())), preferred_element_type=F32
        )
    )


def lane_sums(x):
    return sum(x[:, first : first + 128] for first in range(0, x.shape[1], 128))


def leaf_ends(sizes_ref, leaf_count):
    ends = []
    total = 0
    for leaf in range(leaf_count):
        total = total + sizes_ref[0, leaf]
        ends.append(total)
    return ends


def leaf_row(ends, first, shape):
    positions = lax.broadcasted_iota(jnp.int32, shape, 1) + first
    leaf = jnp.zeros(shape, jnp.int32)
    for end in ends[:-1]:
        leaf = leaf + (positions >= end).astype(jnp.int32)
    return leaf


def up_kernel(leaf_count, levels, *refs):
    sources, (up_ref, local_ref) = refs[:7], refs[7:9]
    held, semaphores = refs[9:16], refs[16]
    sizes_ref, d_ref, basis_ref, nt_ref, nc_ref, ut_ref, uc_ref = held
    probes, points = d_ref.shape
    block = points // BLOCKS

    def copy(index, place, window=None):
        source, target = sources[index], held[index]
        if window is not None:
            source, target = source.at[:, window], target.at[:, window]
        return pltpu.make_async_copy(source, target, semaphores.at[place])

    windows = [pl.ds(block * number, block) for number in range(BLOCKS)]
    first = [copy(0, 0)]
    blocks = [
        [copy(1, 1 + 2 * number, window), copy(2, 2 + 2 * number, window)]
        for number, window in enumerate(windows)
    ]
    others = [copy(index, 2 * BLOCKS + index - 2) for index in range(3, 7)]
    for pending in first + sum(blocks, []) + others:
        pending.start()
    first[0].wait()
    ends = leaf_ends(sizes_ref, leaf_count)
    raw = jnp.zeros((2 * probes * leaf_count, basis_ref.shape[0]), F32)
    for number, window in enumerate(windows):
        for pending in blocks[number]:
            pending.wait()
        split = halves(d_ref[:, window])
        leaf = leaf_row(ends, block * number, split.shape)
        zero = jnp.zeros_like(split)
        masked = jnp.concatenate(
            [jnp.where(leaf == index, split, zero) for index in range(leaf_count)], axis=0
        )
        raw = raw + lax.dot_general(
            masked, basis_ref[:, window], (((1,), (1,)), ((), ())), preferred_element_type=F32
        )
    for pending in others:
        pending.wait()
    current = [
        folded(raw[2 * probes * index : 2 * probes * (index + 1)]) for index in range(leaf_count)
    ]
    rank = basis_ref.shape[0]
    while len(current) > 1:
        count = len(current)
        raised, sided = [], []
        for index in range(count):
            node = count - 1 + index
            both = jnp.concatenate([nt_ref[0, node], nc_ref[0, node]], axis=1)
            image = times(current[index], both)
            raised.append(image[:, :rank])
            sided.append(image[:, rank:])
        current = [raised[2 * i] + raised[2 * i + 1] for i in range(count // 2)]
        for i in range(count // 2):
            local_ref[count // 2 - 1 + i] = sided[2 * i] + sided[2 * i + 1]
    coefficient = current[0]
    for level in range(levels):
        coupling = nc_ref[0, 0] if level == 0 else uc_ref[0, level - 1]
        if level + 1 < levels:
            transfer = nt_ref[0, 0] if level == 0 else ut_ref[0, level - 1]
            image = times(coefficient, jnp.concatenate([transfer, coupling], axis=1))
            coefficient = image[:, :rank]
            up_ref[level] = image[:, rank:]
        else:
            up_ref[level] = times(coefficient, coupling)


def climb(sizes, vectors, levels):
    leaf_count = sizes.shape[1]
    probes, rank = vectors[0].shape[0], vectors[1].shape[0]
    arrays = (sizes, *vectors)
    return pl.pallas_call(
        functools.partial(up_kernel, leaf_count, levels),
        out_shape=(
            jax.ShapeDtypeStruct((levels, probes, rank), F32),
            jax.ShapeDtypeStruct((leaf_count - 1, probes, rank), F32),
        ),
        in_specs=[HBM] * len(arrays),
        out_specs=(VMEM, VMEM),
        scratch_shapes=[pltpu.SMEM(sizes.shape, sizes.dtype)]
        + [pltpu.VMEM(array.shape, array.dtype) for array in vectors]
        + [pltpu.SemaphoreType.DMA((2 * BLOCKS + 5,))],
        compiler_params=PARAMS,
        name="climb",
    )(*(pltpu.with_memory_space_constraint(array, pltpu.HBM) for array in arrays))


def features_kernel(
    leaf_count,
    sizes_ref,
    scalars_ref,
    coords_ref,
    order_ref,
    d_ref,
    after_ref,
    left_ref,
    right_ref,
    dd_ref,
    plan_ref,
    ordered_ref,
):
    points = coords_ref.shape[1]
    chunks = points // 128
    ordered_ref[...] = jnp.zeros_like(ordered_ref)
    for group in range(chunks // 8):
        order = order_ref[8 * group : 8 * group + 8, :]
        chunk_of = lax.shift_right_logical(order, 7)
        lane_of = lax.bitwise_and(order, 127)
        for axis in range(3):
            found = jnp.zeros((8, 128), F32)
            for chunk in range(chunks):
                source = jnp.broadcast_to(
                    coords_ref[axis : axis + 1, 128 * chunk : 128 * chunk + 128], (8, 128)
                )
                picked = jnp.take_along_axis(source, lane_of, axis=1)
                found = jnp.where(chunk_of == chunk, picked, found)
            for row in range(8):
                place = 128 * (8 * group + row)
                ordered_ref[axis : axis + 1, place : place + 128] = found[row : row + 1, :]
    row8 = lax.broadcasted_iota(jnp.int32, (8, points), 0)
    scale = (math.sqrt(5.0) / 3.0) / scalars_ref[0:1, 0:1]
    scaled = jnp.where(row8 < 3, (ordered_ref[...] - 0.5) * scale, 0.0)
    z1 = scaled.astype(BF16).astype(F32)
    z2 = (scaled - z1).astype(BF16).astype(F32)
    kept = z1 + z2
    norm = jnp.broadcast_to(jnp.sum(kept * kept, axis=0, keepdims=True), (8, points))
    n1 = norm.astype(BF16).astype(F32)
    n2 = (norm - n1).astype(BF16).astype(F32)
    n3 = norm - n1 - n2
    ends = leaf_ends(sizes_ref, leaf_count)
    plan_ref[...] = near_plan(ends, points // TILE)
    leaf = leaf_row(ends, 0, (8, points))
    parts = jnp.where(row8 % 3 == 0, n1, jnp.where(row8 % 3 == 1, n2, n3))
    norm_left = jnp.where(row8 < 3, parts, jnp.where(row8 < 6, 1.0, 0.0))
    norm_right = jnp.where(row8 < 3, 1.0, jnp.where(row8 < 6, parts, 0.0))
    same = leaf == row8
    leaf_left = jnp.where(same, 1.0, 0.0)
    leaf_right = jnp.where(same, 0.0, FAR_AWAY)
    left = jnp.concatenate(
        [-2.0 * z1, -2.0 * z1, -2.0 * z2, -2.0 * z2, norm_left, leaf_left]
        + [jnp.zeros((80, points), F32)],
        axis=0,
    )
    right = jnp.concatenate(
        [z1, z2, z1, z2, norm_right, leaf_right], axis=0
    )
    right_ref[...] = right.astype(BF16)
    left_ref[:points, :] = left.T.astype(BF16)
    left_ref[points:, :] = jnp.zeros((STRIP, 128), BF16)
    split = halves(d_ref[...]).astype(F32)
    split = jnp.concatenate([split, jnp.zeros((128 - split.shape[0], points), F32)], axis=0)
    dd_ref[:points, :] = split.T.astype(BF16)
    dd_ref[points:, :] = jnp.zeros((TILE, 128), BF16)


def scalars_kernel(length_ref, scale_ref, noise_ref, after_ref, out_ref):
    row = lax.broadcasted_iota(jnp.int32, out_ref.shape, 0)
    out_ref[...] = jnp.where(
        row == 0, length_ref[0], jnp.where(row == 1, scale_ref[0], noise_ref[0])
    )


def spread_scalars(lengthscale, outputscale, noise_variance, after):
    return pl.pallas_call(
        scalars_kernel,
        out_shape=jax.ShapeDtypeStruct((8, 128), F32),
        in_specs=[SMEM, SMEM, SMEM, ANY],
        out_specs=VMEM,
        compiler_params=PARAMS,
        name="spread_scalars",
    )(lengthscale, outputscale, noise_variance, after)


def features(sizes, scalars, coordinates, order, direction, after):
    leaf_count = sizes.shape[1]
    points = direction.shape[1]
    return pl.pallas_call(
        functools.partial(features_kernel, leaf_count),
        out_shape=(
            jax.ShapeDtypeStruct((points + STRIP, 128), BF16),
            jax.ShapeDtypeStruct((48, points), BF16),
            jax.ShapeDtypeStruct((points + TILE, 128), BF16),
            jax.ShapeDtypeStruct((8, 128), jnp.int32),
        ),
        in_specs=[SMEM, VMEM, VMEM, VMEM, VMEM, ANY],
        out_specs=(VMEM,) * 4,
        scratch_shapes=[pltpu.VMEM((8, points), F32)],
        compiler_params=PARAMS,
        name="features",
    )(sizes, scalars, coordinates, order.reshape(-1, 128), direction, after)


def strip_spans(ends, tiles):
    begins, counts = [], []
    for tile in range(tiles):
        first = tile * TILE
        last = first + TILE - 1
        low = 0
        high = ends[-1]
        for end in ends:
            low = jnp.where(end <= first, end, low)
        for end in ends[::-1]:
            high = jnp.where(end > last, end, high)
        low = lax.div(low, 128) * 128
        begins.append(low)
        counts.append(lax.div(high - low + (STRIP - 1), STRIP))
    return begins, counts


def near_plan(ends, tiles):
    begins, counts = strip_spans(ends, tiles)
    item = lax.broadcasted_iota(jnp.int32, (8, 128), 1)
    first = 0
    begin = jnp.zeros((8, 128), jnp.int32)
    column = jnp.full((8, 128), tiles * TILE, jnp.int32)
    for tile, (low, count) in enumerate(zip(begins, counts)):
        inside = (item >= first) & (item < first + count)
        begin = jnp.where(inside, low + (item - first) * STRIP, begin)
        column = jnp.where(inside, tile * TILE, column)
        first = first + count
    groups = jnp.full((8, 128), lax.div(first + (GROUP - 1), GROUP), jnp.int32)
    row = lax.broadcasted_iota(jnp.int32, (8, 128), 0)
    return jnp.where(row == 0, begin, jnp.where(row == 1, column, groups))


def near_kernel(part, plan_ref, left_ref, right_ref, dd_ref, *refs):
    out_ref = refs[-1]
    depth, points = right_ref.shape
    groups = plan_ref[2, 0]
    if part == 0:
        out_ref[...] = jnp.zeros_like(out_ref)

    def one_group(group, carry):
        for unit in range(GROUP):
            item = group * GROUP + unit
            begin = plan_ref[0, item]
            column = plan_ref[1, item]
            rows = pl.ds(pl.multiple_of(begin, 128), STRIP)
            source = pl.ds(pl.multiple_of(column, TILE), TILE)
            columns = pl.ds(pl.multiple_of(jnp.minimum(column, points - TILE), TILE), TILE)
            squared = jnp.dot(
                left_ref[rows, :depth], right_ref[:, columns], preferred_element_type=F32
            )
            squared = jnp.maximum(squared, 1e-12)
            root = squared * lax.rsqrt(squared)
            kernel = (squared + root + THIRD) * jnp.exp2(root * DECAY)
            high_part = kernel.astype(BF16)
            low_part = (kernel - high_part.astype(F32)).astype(BF16)
            both = jnp.dot(
                jnp.concatenate([high_part, low_part], axis=0),
                dd_ref[source, :],
                preferred_element_type=F32,
            )
            out_ref[rows, :] += folded(both)
        return carry

    lax.fori_loop(
        lax.div(groups * part, PARTS), lax.div(groups * (part + 1), PARTS), one_group, 0
    )


def near_part(prepared, before, after, part):
    left, right, dd, plan = prepared
    return pl.pallas_call(
        functools.partial(near_kernel, part),
        out_shape=jax.ShapeDtypeStruct(left.shape, F32),
        in_specs=[SMEM] + [VMEM] * (3 + len(before)) + [ANY],
        out_specs=VMEM,
        input_output_aliases={4: 0} if before else {},
        compiler_params=PARAMS,
        name="near_part",
    )(plan, left, right, dd, *before, after)


def assemble_kernel(scalars_ref, near_ref, d_ref, r_ref, after_ref, base_ref, old_ref):
    probes, points = d_ref.shape
    noise = scalars_ref[2:3, 0:1]
    near_scale = scalars_ref[1:2, 0:1] * 3.0
    old = jnp.zeros((probes, 128), F32)
    for first in range(0, points, 512):
        window = slice(first, first + 512)
        near = folded(near_ref[window, :].T[: 2 * probes])
        base_ref[:, window] = noise * d_ref[:, window] + near_scale * near
        r = r_ref[:, window]
        old = old + lane_sums(r * r)
    old_ref[...] = old


def assemble(scalars, near, direction, residual, after):
    return pl.pallas_call(
        assemble_kernel,
        out_shape=(
            jax.ShapeDtypeStruct(direction.shape, F32),
            jax.ShapeDtypeStruct((direction.shape[0], 128), F32),
        ),
        in_specs=[VMEM] * 4 + [ANY],
        out_specs=(VMEM, VMEM),
        compiler_params=PARAMS,
        name="assemble",
    )(scalars, near, direction, residual, after)


def down_kernel(
    leaf_count,
    levels,
    sizes_ref,
    base_ref,
    old_ref,
    d_ref,
    r_ref,
    basis_ref,
    nt_ref,
    nc_ref,
    ut_ref,
    uc_ref,
    local_ref,
    *rest,
):
    side_refs = rest[:levels]
    a_ref, sums_ref = rest[levels:]
    probes, points = d_ref.shape
    down = None
    for level in range(levels - 1, -1, -1):
        coupling = nc_ref[0, 0] if level == 0 else uc_ref[0, level - 1]
        side = side_refs[level][...]
        if down is None:
            down = times_transposed(side, coupling)
        else:
            transfer = nt_ref[0, 0] if level == 0 else ut_ref[0, level - 1]
            down = times_transposed(
                jnp.concatenate([down, side], axis=1),
                jnp.concatenate([transfer, coupling], axis=1),
            )
    current = [down]
    while len(current) < leaf_count:
        count = len(current)
        following = []
        for index in range(2 * count):
            node = 2 * count - 1 + index
            parent = index // 2
            following.append(
                times_transposed(
                    jnp.concatenate([current[parent], local_ref[count - 1 + parent]], axis=1),
                    jnp.concatenate([nt_ref[0, node], nc_ref[0, node]], axis=1),
                )
            )
        current = following
    stacked = jnp.concatenate([halves(term) for term in current], axis=0)
    ends = leaf_ends(sizes_ref, leaf_count)
    width = 512
    peak = jnp.zeros((probes, 128), F32)
    curve = jnp.zeros((probes, 128), F32)

    for first in range(0, points, width):
        far_all = jnp.dot(
            stacked, basis_ref[:, first : first + width], preferred_element_type=F32
        )
        leaf = leaf_row(ends, first, (probes, width))
        far = folded(far_all[: 2 * probes])
        for index in range(1, leaf_count):
            term = folded(far_all[2 * probes * index : 2 * probes * (index + 1)])
            far = jnp.where(leaf == index, term, far)
        d = d_ref[:, first : first + width]
        applied = base_ref[:, first : first + width] + far
        a_ref[:, first : first + width] = applied
        size = jnp.abs(applied)
        for i in range(width // 128):
            peak = jnp.maximum(peak, size[:, 128 * i : 128 * i + 128])
        curve = curve + lane_sums(d * applied)
    top = jnp.maximum(jnp.max(peak, axis=1, keepdims=True), 1e-30)
    inverse = 1.0 / top
    cross = jnp.zeros((probes, 128), F32)
    square = jnp.zeros((probes, 128), F32)
    for first in range(0, points, width):
        unit = a_ref[:, first : first + width] * inverse
        cross = cross + lane_sums(r_ref[:, first : first + width] * unit)
        square = square + lane_sums(unit * unit)
    columns = [jnp.sum(x, axis=1, keepdims=True) for x in (old_ref[...], curve, cross, square)]
    lane = lax.broadcasted_iota(jnp.int32, (probes, 128), 1)
    quantity = lax.div(lane, probes)
    own = lax.rem(lane, probes) == lax.broadcasted_iota(jnp.int32, (probes, 128), 0)
    picked = columns[0]
    for index in range(1, 4):
        picked = jnp.where(quantity == index, columns[index], picked)
    row = jnp.concatenate(
        [
            jnp.sum(jnp.where(own, picked, 0.0), axis=0, keepdims=True),
            jnp.sum(jnp.where(own, top, 0.0), axis=0, keepdims=True),
        ],
        axis=1,
    )
    sums_ref[...] = jnp.broadcast_to(row[None], sums_ref.shape)


def descend(
    sizes, base, old, direction, residual, basis, node_transfer, node_coupling,
    upper_transfer, upper_coupling, local, sides,
):
    leaf_count = sizes.shape[1]
    probes, points = direction.shape
    return pl.pallas_call(
        functools.partial(down_kernel, leaf_count, len(sides)),
        out_shape=(
            jax.ShapeDtypeStruct((probes, points), F32),
            jax.ShapeDtypeStruct((2 ** len(sides), 1, 256), F32),
        ),
        in_specs=[SMEM] + [VMEM] * (10 + len(sides)),
        out_specs=(VMEM, VMEM),
        compiler_params=PARAMS,
        name="descend",
    )(
        sizes, base, old, direction, residual, basis,
        node_transfer, node_coupling, upper_transfer, upper_coupling, local, *sides,
    )


def merged(sums, probes):
    values, tops = sums[:, :, :128], sums[:, :, 128:]
    top = jnp.max(tops, axis=0)
    ratio = tops / top
    quantity = lax.div(lax.broadcasted_iota(jnp.int32, (1, 1, 128), 2), probes)
    factor = jnp.where(quantity < 2, 1.0, jnp.where(quantity == 2, ratio, ratio * ratio))
    return jnp.sum(values * factor, axis=0), top


def step_kernel(sums_ref, x_ref, r_ref, d_ref, a_ref, nx_ref, nr_ref, nd_ref):
    probes = d_ref.shape[0]
    total, top = merged(sums_ref[...], probes)
    lane = lax.broadcasted_iota(jnp.int32, (probes, 128), 1)
    probe = lax.broadcasted_iota(jnp.int32, (probes, 128), 0)

    def column(row, index):
        return jnp.sum(
            jnp.where(lane == index * probes + probe, row, 0.0), axis=1, keepdims=True
        )

    old, curve, cross, square = (column(total, index) for index in range(4))
    step = old / curve
    reach = step * column(top, 0)
    fresh = old - 2.0 * (reach * cross) + (reach * reach) * square
    beta = fresh / old
    d = d_ref[...]
    nx_ref[...] = x_ref[...] + step * d
    remaining = r_ref[...] - step * a_ref[...]
    nr_ref[...] = remaining
    nd_ref[...] = remaining + beta * d


def finish(sums, solution_block, residual, direction, applied):
    shape = jax.ShapeDtypeStruct(direction.shape, F32)
    return pl.pallas_call(
        step_kernel,
        out_shape=(shape, shape, shape),
        in_specs=[VMEM] * 5,
        out_specs=(VMEM, VMEM, VMEM),
        compiler_params=PARAMS,
        name="finish",
    )(sums, solution_block, residual, direction, applied)


def from_partner(array, stride):
    count = lax.axis_size("leaf")
    return lax.ppermute(array, "leaf", [(i, i ^ stride) for i in range(count)])


def shards(
    solution,
    residual,
    direction,
    coordinates,
    cluster_order,
    leaf_sizes,
    leaf_basis,
    node_transfer,
    node_coupling,
    upper_transfer,
    upper_coupling,
    lengthscale,
    outputscale,
    noise_variance,
):
    levels = lax.axis_size("leaf").bit_length() - 1
    probes, points = direction.shape
    up, local = climb(
        leaf_sizes,
        (direction, leaf_basis, node_transfer, node_coupling, upper_transfer, upper_coupling),
        levels,
    )
    sides = []
    near = ()
    current = up
    for level in range(max(levels, PARTS + 2)):
        if level < levels:
            incoming = from_partner(current, 2**level)
        if level == 0:
            scalars = spread_scalars(lengthscale, outputscale, noise_variance, current)
        if level == 1:
            prepared = features(
                leaf_sizes, scalars, coordinates, cluster_order, direction, current
            )
        if 1 <= level <= PARTS:
            near = (near_part(prepared, near, current, level - 1),)
        if level == PARTS + 1:
            base, old = assemble(scalars, near[0], direction, residual, current)
        if level < levels:
            current = current + incoming
            sides.append(current[0])
            current = current[1:] if level + 1 < levels else current
            if level == 0:
                current, scalars = lax.optimization_barrier((current, scalars))
            elif level <= PARTS:
                current, *near = lax.optimization_barrier((current, *near))
            elif level == PARTS + 1:
                current, base, old = lax.optimization_barrier((current, base, old))
    applied, sums = descend(
        leaf_sizes, base, old, direction, residual, leaf_basis,
        node_transfer, node_coupling, upper_transfer, upper_coupling, local, sides,
    )
    gathered = lax.all_to_all(sums, "leaf", 0, 0, tiled=True)
    return finish(gathered, solution, residual, direction, applied)


def solution(mesh):
    in_specs = (
        P(None, "leaf"),
        P(None, "leaf"),
        P(None, "leaf"),
        P(None, "leaf"),
        P("leaf"),
        P("leaf", None),
        P(None, "leaf"),
        P("leaf", None, None, None),
        P("leaf", None, None, None),
        P("leaf", None, None, None),
        P("leaf", None, None, None),
        P(),
        P(),
        P(),
    )
    out_specs = (P(None, "leaf"), P(None, "leaf"), P(None, "leaf"))
    return jax.shard_map(shards, mesh=mesh, in_specs=in_specs, out_specs=out_specs, check_vma=False)
```

```python
import functools
import math

import jax
import jax.numpy as jnp
from jax import lax
from jax.experimental import pallas as pl
from jax.experimental.pallas import tpu as pltpu
from jax.sharding import PartitionSpec as P

F32 = jnp.float32
BF16 = jnp.bfloat16
TILE = 256
FAR_AWAY = 32768.0
THIRD = 1.0 / 3.0
DECAY = -3.0 / math.log(2.0)

VMEM = pl.BlockSpec(memory_space=pltpu.VMEM)
SMEM = pl.BlockSpec(memory_space=pltpu.SMEM)
ANY = pl.BlockSpec(memory_space=pl.ANY)
HBM = pl.BlockSpec(memory_space=pltpu.HBM)
STRIP = 384
GROUP = 4
PARTS = 4
BLOCKS = 3
PARAMS = pltpu.CompilerParams(vmem_limit_bytes=48 * 1024 * 1024)


def halves(x):
    high = x.astype(BF16)
    low = (x - high.astype(F32)).astype(BF16)
    return jnp.concatenate([high, low], axis=0)


def folded(x):
    rows = x.shape[0] // 2
    return x[:rows] + x[rows:]


def times(x, generator):
    return folded(jnp.dot(halves(x), generator, preferred_element_type=F32))


def times_transposed(x, generator):
    return folded(
        lax.dot_general(
            halves(x), generator, (((1,), (1,)), ((), ())), preferred_element_type=F32
        )
    )


def lane_sums(x):
    return sum(x[:, first : first + 128] for first in range(0, x.shape[1], 128))


def leaf_ends(sizes_ref, leaf_count):
    ends = []
    total = 0
    for leaf in range(leaf_count):
        total = total + sizes_ref[0, leaf]
        ends.append(total)
    return ends


def leaf_row(ends, first, shape):
    positions = lax.broadcasted_iota(jnp.int32, shape, 1) + first
    leaf = jnp.zeros(shape, jnp.int32)
    for end in ends[:-1]:
        leaf = leaf + (positions >= end).astype(jnp.int32)
    return leaf


def up_kernel(leaf_count, levels, *refs):
    sources, (up_ref, local_ref, high_ref, low_ref) = refs[:7], refs[7:11]
    held, semaphores = refs[11:18], refs[18]
    sizes_ref, d_ref, basis_ref, nt_ref, nc_ref, ut_ref, uc_ref = held
    probes, points = d_ref.shape
    block = points // BLOCKS

    def copy(index, place, window=None):
        source, target = sources[index], held[index]
        if window is not None:
            source, target = source.at[:, window], target.at[:, window]
        return pltpu.make_async_copy(source, target, semaphores.at[place])

    windows = [pl.ds(block * number, block) for number in range(BLOCKS)]
    first = [copy(0, 0)]
    blocks = [
        [copy(1, 1 + 2 * number, window), copy(2, 2 + 2 * number, window)]
        for number, window in enumerate(windows)
    ]
    others = [copy(index, 2 * BLOCKS + index - 2) for index in range(3, 7)]
    for pending in others + first + sum(blocks, []):
        pending.start()
    for pending in others:
        pending.wait()
    rank = basis_ref.shape[0]
    images = [nc_ref[0, 0].astype(F32)]
    path = nt_ref[0, 0].astype(F32)
    for level in range(1, levels):
        if level + 1 < levels:
            both = jnp.concatenate([ut_ref[0, level - 1], uc_ref[0, level - 1]], axis=1)
            image = times(path, both)
            path = image[:, :rank]
            images.append(image[:, rank:])
        else:
            images.append(times(path, uc_ref[0, level - 1]))
    images = jnp.concatenate(images, axis=1)
    high = images.astype(BF16)
    low = (images - high.astype(F32)).astype(BF16)
    high_ref[...] = high
    low_ref[...] = low
    first[0].wait()
    ends = leaf_ends(sizes_ref, leaf_count)
    raw = jnp.zeros((2 * probes * leaf_count, basis_ref.shape[0]), F32)
    for number, window in enumerate(windows):
        for pending in blocks[number]:
            pending.wait()
        split = halves(d_ref[:, window])
        leaf = leaf_row(ends, block * number, split.shape)
        zero = jnp.zeros_like(split)
        masked = jnp.concatenate(
            [jnp.where(leaf == index, split, zero) for index in range(leaf_count)], axis=0
        )
        raw = raw + lax.dot_general(
            masked, basis_ref[:, window], (((1,), (1,)), ((), ())), preferred_element_type=F32
        )
    current = [
        folded(raw[2 * probes * index : 2 * probes * (index + 1)]) for index in range(leaf_count)
    ]
    while len(current) > 1:
        count = len(current)
        raised, sided = [], []
        for index in range(count):
            node = count - 1 + index
            both = jnp.concatenate([nt_ref[0, node], nc_ref[0, node]], axis=1)
            image = times(current[index], both)
            raised.append(image[:, :rank])
            sided.append(image[:, rank:])
        current = [raised[2 * i] + raised[2 * i + 1] for i in range(count // 2)]
        for i in range(count // 2):
            local_ref[count // 2 - 1 + i] = sided[2 * i] + sided[2 * i + 1]
    image = times(current[0], high) + times(current[0], low)
    for level in range(levels):
        up_ref[level] = image[:, rank * level : rank * (level + 1)]


def climb(sizes, vectors, levels):
    leaf_count = sizes.shape[1]
    probes, rank = vectors[0].shape[0], vectors[1].shape[0]
    arrays = (sizes, *vectors)
    return pl.pallas_call(
        functools.partial(up_kernel, leaf_count, levels),
        out_shape=(
            jax.ShapeDtypeStruct((levels, probes, rank), F32),
            jax.ShapeDtypeStruct((leaf_count - 1, probes, rank), F32),
            jax.ShapeDtypeStruct((rank, rank * levels), BF16),
            jax.ShapeDtypeStruct((rank, rank * levels), BF16),
        ),
        in_specs=[HBM] * len(arrays),
        out_specs=(VMEM,) * 4,
        scratch_shapes=[pltpu.SMEM(sizes.shape, sizes.dtype)]
        + [pltpu.VMEM(array.shape, array.dtype) for array in vectors]
        + [pltpu.SemaphoreType.DMA((2 * BLOCKS + 5,))],
        compiler_params=PARAMS,
        name="climb",
    )(*(pltpu.with_memory_space_constraint(array, pltpu.HBM) for array in arrays))


def features_kernel(
    leaf_count,
    sizes_ref,
    scalars_ref,
    coords_ref,
    order_ref,
    d_ref,
    after_ref,
    left_ref,
    right_ref,
    dd_ref,
    plan_ref,
    ordered_ref,
    list_ref,
    semaphore,
):
    points = coords_ref.shape[1]
    chunks = points // 128
    ordered_ref[...] = jnp.zeros_like(ordered_ref)
    for group in range(chunks // 8):
        order = order_ref[8 * group : 8 * group + 8, :]
        chunk_of = lax.shift_right_logical(order, 7)
        lane_of = lax.bitwise_and(order, 127)
        for axis in range(3):
            found = jnp.zeros((8, 128), F32)
            for chunk in range(chunks):
                source = jnp.broadcast_to(
                    coords_ref[axis : axis + 1, 128 * chunk : 128 * chunk + 128], (8, 128)
                )
                picked = jnp.take_along_axis(source, lane_of, axis=1)
                found = jnp.where(chunk_of == chunk, picked, found)
            for row in range(8):
                place = 128 * (8 * group + row)
                ordered_ref[axis : axis + 1, place : place + 128] = found[row : row + 1, :]
    row8 = lax.broadcasted_iota(jnp.int32, (8, points), 0)
    scale = (math.sqrt(5.0) / 3.0) / scalars_ref[0:1, 0:1]
    scaled = jnp.where(row8 < 3, (ordered_ref[...] - 0.5) * scale, 0.0)
    z1 = scaled.astype(BF16).astype(F32)
    z2 = (scaled - z1).astype(BF16).astype(F32)
    kept = z1 + z2
    norm = jnp.broadcast_to(jnp.sum(kept * kept, axis=0, keepdims=True), (8, points))
    n1 = norm.astype(BF16).astype(F32)
    n2 = (norm - n1).astype(BF16).astype(F32)
    n3 = norm - n1 - n2
    ends = leaf_ends(sizes_ref, leaf_count)
    list_ref[...] = near_plan(ends, points // TILE)
    handed = pltpu.make_async_copy(list_ref, plan_ref, semaphore.at[0])
    handed.start()
    leaf = leaf_row(ends, 0, (8, points))
    parts = jnp.where(row8 % 3 == 0, n1, jnp.where(row8 % 3 == 1, n2, n3))
    norm_left = jnp.where(row8 < 3, parts, jnp.where(row8 < 6, 1.0, 0.0))
    norm_right = jnp.where(row8 < 3, 1.0, jnp.where(row8 < 6, parts, 0.0))
    same = leaf == row8
    leaf_left = jnp.where(same, 1.0, 0.0)
    leaf_right = jnp.where(same, 0.0, FAR_AWAY)
    left = jnp.concatenate(
        [-2.0 * z1, -2.0 * z1, -2.0 * z2, -2.0 * z2, norm_left, leaf_left]
        + [jnp.zeros((80, points), F32)],
        axis=0,
    )
    right = jnp.concatenate(
        [z1, z2, z1, z2, norm_right, leaf_right], axis=0
    )
    right_ref[...] = right.astype(BF16)
    left_ref[:points, :] = left.T.astype(BF16)
    left_ref[points:, :] = jnp.zeros((STRIP, 128), BF16)
    split = halves(d_ref[...]).astype(F32)
    split = jnp.concatenate([split, jnp.zeros((128 - split.shape[0], points), F32)], axis=0)
    dd_ref[:points, :] = split.T.astype(BF16)
    dd_ref[points:, :] = jnp.zeros((TILE, 128), BF16)
    handed.wait()


def scalars_kernel(length_ref, scale_ref, noise_ref, after_ref, out_ref):
    row = lax.broadcasted_iota(jnp.int32, out_ref.shape, 0)
    out_ref[...] = jnp.where(
        row == 0, length_ref[0], jnp.where(row == 1, scale_ref[0], noise_ref[0])
    )


def spread_scalars(lengthscale, outputscale, noise_variance, after):
    return pl.pallas_call(
        scalars_kernel,
        out_shape=jax.ShapeDtypeStruct((8, 128), F32),
        in_specs=[SMEM, SMEM, SMEM, ANY],
        out_specs=VMEM,
        compiler_params=PARAMS,
        name="spread_scalars",
    )(lengthscale, outputscale, noise_variance, after)


def features(sizes, scalars, coordinates, order, direction, after):
    leaf_count = sizes.shape[1]
    points = direction.shape[1]
    return pl.pallas_call(
        functools.partial(features_kernel, leaf_count),
        out_shape=(
            jax.ShapeDtypeStruct((points + STRIP, 128), BF16),
            jax.ShapeDtypeStruct((48, points), BF16),
            jax.ShapeDtypeStruct((points + TILE, 128), BF16),
            pltpu.SMEM((8, 128), jnp.int32),
        ),
        in_specs=[SMEM, VMEM, VMEM, VMEM, VMEM, ANY],
        out_specs=(VMEM, VMEM, VMEM, SMEM),
        scratch_shapes=[
            pltpu.VMEM((8, points), F32),
            pltpu.VMEM((8, 128), jnp.int32),
            pltpu.SemaphoreType.DMA((1,)),
        ],
        compiler_params=PARAMS,
        name="features",
    )(sizes, scalars, coordinates, order.reshape(-1, 128), direction, after)


def strip_spans(ends, tiles):
    begins, counts = [], []
    for tile in range(tiles):
        first = tile * TILE
        last = first + TILE - 1
        low = 0
        high = ends[-1]
        for end in ends:
            low = jnp.where(end <= first, end, low)
        for end in ends[::-1]:
            high = jnp.where(end > last, end, high)
        low = lax.div(low, 128) * 128
        begins.append(low)
        counts.append(lax.div(high - low + (STRIP - 1), STRIP))
    return begins, counts


def near_plan(ends, tiles):
    begins, counts = strip_spans(ends, tiles)
    item = lax.broadcasted_iota(jnp.int32, (8, 128), 1)
    first = 0
    begin = jnp.zeros((8, 128), jnp.int32)
    column = jnp.full((8, 128), tiles * TILE, jnp.int32)
    for tile, (low, count) in enumerate(zip(begins, counts)):
        inside = (item >= first) & (item < first + count)
        begin = jnp.where(inside, low + (item - first) * STRIP, begin)
        column = jnp.where(inside, tile * TILE, column)
        first = first + count
    groups = jnp.full((8, 128), lax.div(first + (GROUP - 1), GROUP), jnp.int32)
    row = lax.broadcasted_iota(jnp.int32, (8, 128), 0)
    return jnp.where(row == 0, begin, jnp.where(row == 1, column, groups))


def near_kernel(part, plan_ref, left_ref, right_ref, dd_ref, *refs):
    out_ref = refs[-1]
    depth, points = right_ref.shape
    groups = plan_ref[2, 0]
    if part == 0:
        out_ref[...] = jnp.zeros_like(out_ref)

    def one_group(group, carry):
        for unit in range(GROUP):
            item = group * GROUP + unit
            begin = plan_ref[0, item]
            column = plan_ref[1, item]
            rows = pl.ds(pl.multiple_of(begin, 128), STRIP)
            source = pl.ds(pl.multiple_of(column, TILE), TILE)
            columns = pl.ds(pl.multiple_of(jnp.minimum(column, points - TILE), TILE), TILE)
            squared = jnp.dot(
                left_ref[rows, :depth], right_ref[:, columns], preferred_element_type=F32
            )
            squared = jnp.maximum(squared, 1e-12)
            root = squared * lax.rsqrt(squared)
            kernel = (squared + root + THIRD) * jnp.exp2(root * DECAY)
            high_part = kernel.astype(BF16)
            low_part = (kernel - high_part.astype(F32)).astype(BF16)
            both = jnp.dot(
                jnp.concatenate([high_part, low_part], axis=0),
                dd_ref[source, :],
                preferred_element_type=F32,
            )
            out_ref[rows, :] += folded(both)
        return carry

    lax.fori_loop(
        lax.div(groups * part, PARTS), lax.div(groups * (part + 1), PARTS), one_group, 0
    )


def near_part(prepared, before, after, part):
    left, right, dd, plan = prepared
    plan = pltpu.with_memory_space_constraint(plan, pltpu.SMEM)
    return pl.pallas_call(
        functools.partial(near_kernel, part),
        out_shape=jax.ShapeDtypeStruct(left.shape, F32),
        in_specs=[SMEM] + [VMEM] * (3 + len(before)) + [ANY],
        out_specs=VMEM,
        input_output_aliases={4: 0} if before else {},
        compiler_params=PARAMS,
        name="near_part",
    )(plan, left, right, dd, *before, after)


def assemble_kernel(scalars_ref, near_ref, d_ref, r_ref, after_ref, base_ref, old_ref):
    probes, points = d_ref.shape
    noise = scalars_ref[2:3, 0:1]
    near_scale = scalars_ref[1:2, 0:1] * 3.0
    old = jnp.zeros((probes, 128), F32)
    for first in range(0, points, 512):
        window = slice(first, first + 512)
        near = folded(near_ref[window, :].T[: 2 * probes])
        base_ref[:, window] = noise * d_ref[:, window] + near_scale * near
        r = r_ref[:, window]
        old = old + lane_sums(r * r)
    old_ref[...] = old


def assemble(scalars, near, direction, residual, after):
    return pl.pallas_call(
        assemble_kernel,
        out_shape=(
            jax.ShapeDtypeStruct(direction.shape, F32),
            jax.ShapeDtypeStruct((direction.shape[0], 128), F32),
        ),
        in_specs=[VMEM] * 4 + [ANY],
        out_specs=(VMEM, VMEM),
        compiler_params=PARAMS,
        name="assemble",
    )(scalars, near, direction, residual, after)


def down_kernel(
    leaf_count,
    levels,
    sizes_ref,
    base_ref,
    old_ref,
    d_ref,
    r_ref,
    basis_ref,
    nt_ref,
    nc_ref,
    high_ref,
    low_ref,
    local_ref,
    *rest,
):
    side_refs = rest[:levels]
    a_ref, sums_ref = rest[levels:]
    probes, points = d_ref.shape
    wide = jnp.concatenate([side_ref[...] for side_ref in side_refs], axis=1)
    down = times_transposed(wide, high_ref[...]) + times_transposed(wide, low_ref[...])
    current = [down]
    while len(current) < leaf_count:
        count = len(current)
        following = []
        for index in range(2 * count):
            node = 2 * count - 1 + index
            parent = index // 2
            following.append(
                times_transposed(
                    jnp.concatenate([current[parent], local_ref[count - 1 + parent]], axis=1),
                    jnp.concatenate([nt_ref[0, node], nc_ref[0, node]], axis=1),
                )
            )
        current = following
    stacked = jnp.concatenate([halves(term) for term in current], axis=0)
    ends = leaf_ends(sizes_ref, leaf_count)
    width = 512
    peak = jnp.zeros((probes, 128), F32)
    curve = jnp.zeros((probes, 128), F32)

    for first in range(0, points, width):
        far_all = jnp.dot(
            stacked, basis_ref[:, first : first + width], preferred_element_type=F32
        )
        leaf = leaf_row(ends, first, (probes, width))
        far = folded(far_all[: 2 * probes])
        for index in range(1, leaf_count):
            term = folded(far_all[2 * probes * index : 2 * probes * (index + 1)])
            far = jnp.where(leaf == index, term, far)
        d = d_ref[:, first : first + width]
        applied = base_ref[:, first : first + width] + far
        a_ref[:, first : first + width] = applied
        size = jnp.abs(applied)
        for i in range(width // 128):
            peak = jnp.maximum(peak, size[:, 128 * i : 128 * i + 128])
        curve = curve + lane_sums(d * applied)
    top = jnp.maximum(jnp.max(peak, axis=1, keepdims=True), 1e-30)
    inverse = 1.0 / top
    cross = jnp.zeros((probes, 128), F32)
    square = jnp.zeros((probes, 128), F32)
    for first in range(0, points, width):
        unit = a_ref[:, first : first + width] * inverse
        cross = cross + lane_sums(r_ref[:, first : first + width] * unit)
        square = square + lane_sums(unit * unit)
    columns = [jnp.sum(x, axis=1, keepdims=True) for x in (old_ref[...], curve, cross, square)]
    lane = lax.broadcasted_iota(jnp.int32, (probes, 128), 1)
    quantity = lax.div(lane, probes)
    own = lax.rem(lane, probes) == lax.broadcasted_iota(jnp.int32, (probes, 128), 0)
    picked = columns[0]
    for index in range(1, 4):
        picked = jnp.where(quantity == index, columns[index], picked)
    row = jnp.concatenate(
        [
            jnp.sum(jnp.where(own, picked, 0.0), axis=0, keepdims=True),
            jnp.sum(jnp.where(own, top, 0.0), axis=0, keepdims=True),
        ],
        axis=1,
    )
    sums_ref[...] = jnp.broadcast_to(row[None], sums_ref.shape)


def descend(
    sizes, base, old, direction, residual, basis, node_transfer, node_coupling,
    images, local, sides,
):
    leaf_count = sizes.shape[1]
    probes, points = direction.shape
    return pl.pallas_call(
        functools.partial(down_kernel, leaf_count, len(sides)),
        out_shape=(
            jax.ShapeDtypeStruct((probes, points), F32),
            jax.ShapeDtypeStruct((2 ** len(sides), 1, 256), F32),
        ),
        in_specs=[SMEM] + [VMEM] * (10 + len(sides)),
        out_specs=(VMEM, VMEM),
        compiler_params=PARAMS,
        name="descend",
    )(
        sizes, base, old, direction, residual, basis,
        node_transfer, node_coupling, *images, local, *sides,
    )


def merged(sums, probes):
    values, tops = sums[:, :, :128], sums[:, :, 128:]
    top = jnp.max(tops, axis=0)
    ratio = tops / top
    quantity = lax.div(lax.broadcasted_iota(jnp.int32, (1, 1, 128), 2), probes)
    factor = jnp.where(quantity < 2, 1.0, jnp.where(quantity == 2, ratio, ratio * ratio))
    return jnp.sum(values * factor, axis=0), top


def step_kernel(sums_ref, x_ref, r_ref, d_ref, a_ref, nx_ref, nr_ref, nd_ref):
    probes = d_ref.shape[0]
    total, top = merged(sums_ref[...], probes)
    lane = lax.broadcasted_iota(jnp.int32, (probes, 128), 1)
    probe = lax.broadcasted_iota(jnp.int32, (probes, 128), 0)

    def column(row, index):
        return jnp.sum(
            jnp.where(lane == index * probes + probe, row, 0.0), axis=1, keepdims=True
        )

    old, curve, cross, square = (column(total, index) for index in range(4))
    step = old / curve
    reach = step * column(top, 0)
    fresh = old - 2.0 * (reach * cross) + (reach * reach) * square
    beta = fresh / old
    d = d_ref[...]
    nx_ref[...] = x_ref[...] + step * d
    remaining = r_ref[...] - step * a_ref[...]
    nr_ref[...] = remaining
    nd_ref[...] = remaining + beta * d


def finish(sums, solution_block, residual, direction, applied):
    shape = jax.ShapeDtypeStruct(direction.shape, F32)
    return pl.pallas_call(
        step_kernel,
        out_shape=(shape, shape, shape),
        in_specs=[VMEM] * 5,
        out_specs=(VMEM, VMEM, VMEM),
        compiler_params=PARAMS,
        name="finish",
    )(sums, solution_block, residual, direction, applied)


def from_partner(array, stride):
    count = lax.axis_size("leaf")
    return lax.ppermute(array, "leaf", [(i, i ^ stride) for i in range(count)])


def shards(
    solution,
    residual,
    direction,
    coordinates,
    cluster_order,
    leaf_sizes,
    leaf_basis,
    node_transfer,
    node_coupling,
    upper_transfer,
    upper_coupling,
    lengthscale,
    outputscale,
    noise_variance,
):
    levels = lax.axis_size("leaf").bit_length() - 1
    probes, points = direction.shape
    up, local, *images = climb(
        leaf_sizes,
        (direction, leaf_basis, node_transfer, node_coupling, upper_transfer, upper_coupling),
        levels,
    )
    sides = []
    near = ()
    current = up
    for level in range(max(levels, PARTS + 1)):
        if level < levels:
            incoming = from_partner(current, 2**level)
        if level == 0:
            scalars = spread_scalars(lengthscale, outputscale, noise_variance, current)
        if level == 1:
            prepared = features(
                leaf_sizes, scalars, coordinates, cluster_order, direction, current
            )
        if 1 <= level <= PARTS:
            near = (near_part(prepared, near, current, level - 1),)
        if level < levels:
            current = current + incoming
            sides.append(current[0])
            current = current[1:] if level + 1 < levels else current
            if level == 0:
                current, scalars = lax.optimization_barrier((current, scalars))
            elif level <= PARTS:
                current, *near = lax.optimization_barrier((current, *near))
    base, old = assemble(scalars, near[0], direction, residual, near[0])
    applied, sums = descend(
        leaf_sizes, base, old, direction, residual, leaf_basis,
        node_transfer, node_coupling, images, local, sides,
    )
    gathered = lax.all_to_all(sums, "leaf", 0, 0, tiled=True)
    return finish(gathered, solution, residual, direction, applied)


def solution(mesh):
    in_specs = (
        P(None, "leaf"),
        P(None, "leaf"),
        P(None, "leaf"),
        P(None, "leaf"),
        P("leaf"),
        P("leaf", None),
        P(None, "leaf"),
        P("leaf", None, None, None),
        P("leaf", None, None, None),
        P("leaf", None, None, None),
        P("leaf", None, None, None),
        P(),
        P(),
        P(),
    )
    out_specs = (P(None, "leaf"), P(None, "leaf"), P(None, "leaf"))
    return jax.shard_map(shards, mesh=mesh, in_specs=in_specs, out_specs=out_specs, check_vma=False)
```

```python
import functools
import math

import jax
import jax.numpy as jnp
from jax import lax
from jax.experimental import pallas as pl
from jax.experimental.pallas import tpu as pltpu
from jax.sharding import PartitionSpec as P

F32 = jnp.float32
BF16 = jnp.bfloat16
TILE = 256
FAR_AWAY = 32768.0
THIRD = 1.0 / 3.0
DECAY = -3.0 / math.log(2.0)

VMEM = pl.BlockSpec(memory_space=pltpu.VMEM)
SMEM = pl.BlockSpec(memory_space=pltpu.SMEM)
ANY = pl.BlockSpec(memory_space=pl.ANY)
HBM = pl.BlockSpec(memory_space=pltpu.HBM)
STRIP = 384
GROUP = 4
PARTS = 4
SENDS = 6
PARAMS = pltpu.CompilerParams(vmem_limit_bytes=48 * 1024 * 1024)


def halves(x):
    high = x.astype(BF16)
    low = (x - high.astype(F32)).astype(BF16)
    return jnp.concatenate([high, low], axis=0)


def folded(x):
    rows = x.shape[0] // 2
    return x[:rows] + x[rows:]


def times(x, generator):
    return folded(jnp.dot(halves(x), generator, preferred_element_type=F32))


def times_transposed(x, generator):
    return folded(
        lax.dot_general(
            halves(x), generator, (((1,), (1,)), ((), ())), preferred_element_type=F32
        )
    )


def lane_sums(x):
    return sum(x[:, first : first + 128] for first in range(0, x.shape[1], 128))


def leaf_ends(sizes_ref, leaf_count):
    ends = []
    total = 0
    for leaf in range(leaf_count):
        total = total + sizes_ref[0, leaf]
        ends.append(total)
    return ends


def leaf_row(ends, first, shape):
    positions = lax.broadcasted_iota(jnp.int32, shape, 1) + first
    leaf = jnp.zeros(shape, jnp.int32)
    for end in ends[:-1]:
        leaf = leaf + (positions >= end).astype(jnp.int32)
    return leaf


def up_kernel(leaf_count, levels, *refs):
    sources, (up_ref, local_ref, high_ref, low_ref) = refs[:7], refs[7:11]
    d_ref, basis_ref, nt_ref, nc_ref = refs[11:15]
    sizes_ref, ut_ref, uc_ref, semaphores = refs[15:]
    probes, points = d_ref.shape
    copies = [
        pltpu.make_async_copy(source, target, semaphores.at[index])
        for index, (source, target) in enumerate(
            zip(sources, (sizes_ref, d_ref, basis_ref, nt_ref, nc_ref, ut_ref, uc_ref))
        )
    ]
    for copy in copies:
        copy.start()
    for copy in copies:
        copy.wait()
    rank = basis_ref.shape[0]
    images = [nc_ref[0, 0].astype(F32)]
    path = nt_ref[0, 0].astype(F32)
    for level in range(1, levels):
        if level + 1 < levels:
            both = jnp.concatenate([ut_ref[0, level - 1], uc_ref[0, level - 1]], axis=1)
            image = times(path, both)
            path = image[:, :rank]
            images.append(image[:, rank:])
        else:
            images.append(times(path, uc_ref[0, level - 1]))
    images = jnp.concatenate(images, axis=1)
    high = images.astype(BF16)
    low = (images - high.astype(F32)).astype(BF16)
    high_ref[...] = high
    low_ref[...] = low
    ends = leaf_ends(sizes_ref, leaf_count)
    split = halves(d_ref[...])
    leaf = leaf_row(ends, 0, split.shape)
    zero = jnp.zeros_like(split)
    masked = jnp.concatenate(
        [jnp.where(leaf == index, split, zero) for index in range(leaf_count)], axis=0
    )
    raw = lax.dot_general(
        masked, basis_ref[...], (((1,), (1,)), ((), ())), preferred_element_type=F32
    )
    current = [
        folded(raw[2 * probes * index : 2 * probes * (index + 1)]) for index in range(leaf_count)
    ]
    while len(current) > 1:
        count = len(current)
        raised, sided = [], []
        for index in range(count):
            node = count - 1 + index
            both = jnp.concatenate([nt_ref[0, node], nc_ref[0, node]], axis=1)
            image = times(current[index], both)
            raised.append(image[:, :rank])
            sided.append(image[:, rank:])
        current = [raised[2 * i] + raised[2 * i + 1] for i in range(count // 2)]
        for i in range(count // 2):
            local_ref[count // 2 - 1 + i] = sided[2 * i] + sided[2 * i + 1]
    image = times(current[0], high) + times(current[0], low)
    for level in range(levels):
        up_ref[level] = image[:, rank * level : rank * (level + 1)]


def climb(sizes, vectors, levels):
    leaf_count = sizes.shape[1]
    probes, rank = vectors[0].shape[0], vectors[1].shape[0]
    arrays = (sizes, *vectors)
    return pl.pallas_call(
        functools.partial(up_kernel, leaf_count, levels),
        out_shape=(
            jax.ShapeDtypeStruct((levels, probes, rank), F32),
            jax.ShapeDtypeStruct((leaf_count - 1, probes, rank), F32),
            jax.ShapeDtypeStruct((rank, rank * levels), BF16),
            jax.ShapeDtypeStruct((rank, rank * levels), BF16),
            *(jax.ShapeDtypeStruct(array.shape, array.dtype) for array in vectors[:4]),
        ),
        in_specs=[HBM] * len(arrays),
        out_specs=(VMEM,) * 8,
        scratch_shapes=[
            pltpu.SMEM(sizes.shape, sizes.dtype),
            *(pltpu.VMEM(array.shape, array.dtype) for array in vectors[4:]),
            pltpu.SemaphoreType.DMA((len(arrays),)),
        ],
        compiler_params=PARAMS,
        name="climb",
    )(*(pltpu.with_memory_space_constraint(array, pltpu.HBM) for array in arrays))


def features_kernel(
    leaf_count,
    sizes_ref,
    scalars_ref,
    coords_ref,
    order_ref,
    d_ref,
    after_ref,
    left_ref,
    right_ref,
    dd_ref,
    plan_ref,
    ordered_ref,
    list_ref,
    semaphore,
):
    points = coords_ref.shape[1]
    chunks = points // 128
    ends = leaf_ends(sizes_ref, leaf_count)
    list_ref[...] = near_plan(ends, points // TILE)
    handed = pltpu.make_async_copy(list_ref, plan_ref, semaphore.at[0])
    handed.start()
    ordered_ref[...] = jnp.zeros_like(ordered_ref)
    for group in range(chunks // 8):
        order = order_ref[8 * group : 8 * group + 8, :]
        chunk_of = lax.shift_right_logical(order, 7)
        lane_of = lax.bitwise_and(order, 127)
        for axis in range(3):
            found = jnp.zeros((8, 128), F32)
            for chunk in range(chunks):
                source = jnp.broadcast_to(
                    coords_ref[axis : axis + 1, 128 * chunk : 128 * chunk + 128], (8, 128)
                )
                picked = jnp.take_along_axis(source, lane_of, axis=1)
                found = jnp.where(chunk_of == chunk, picked, found)
            for row in range(8):
                place = 128 * (8 * group + row)
                ordered_ref[axis : axis + 1, place : place + 128] = found[row : row + 1, :]
    row8 = lax.broadcasted_iota(jnp.int32, (8, points), 0)
    scale = (math.sqrt(5.0) / 3.0) / scalars_ref[0:1, 0:1]
    scaled = jnp.where(row8 < 3, (ordered_ref[...] - 0.5) * scale, 0.0)
    z1 = scaled.astype(BF16).astype(F32)
    z2 = (scaled - z1).astype(BF16).astype(F32)
    kept = z1 + z2
    norm = jnp.broadcast_to(jnp.sum(kept * kept, axis=0, keepdims=True), (8, points))
    n1 = norm.astype(BF16).astype(F32)
    n2 = (norm - n1).astype(BF16).astype(F32)
    n3 = norm - n1 - n2
    leaf = leaf_row(ends, 0, (8, points))
    parts = jnp.where(row8 % 3 == 0, n1, jnp.where(row8 % 3 == 1, n2, n3))
    norm_left = jnp.where(row8 < 3, parts, jnp.where(row8 < 6, 1.0, 0.0))
    norm_right = jnp.where(row8 < 3, 1.0, jnp.where(row8 < 6, parts, 0.0))
    same = leaf == row8
    leaf_left = jnp.where(same, 1.0, 0.0)
    leaf_right = jnp.where(same, 0.0, FAR_AWAY)
    left = jnp.concatenate(
        [-2.0 * z1, -2.0 * z1, -2.0 * z2, -2.0 * z2, norm_left, leaf_left]
        + [jnp.zeros((80, points), F32)],
        axis=0,
    )
    right = jnp.concatenate(
        [z1, z2, z1, z2, norm_right, leaf_right], axis=0
    )
    right_ref[...] = right.astype(BF16)
    left_ref[:points, :] = left.T.astype(BF16)
    left_ref[points:, :] = jnp.zeros((STRIP, 128), BF16)
    split = halves(d_ref[...]).astype(F32)
    split = jnp.concatenate([split, jnp.zeros((128 - split.shape[0], points), F32)], axis=0)
    dd_ref[:points, :] = split.T.astype(BF16)
    dd_ref[points:, :] = jnp.zeros((TILE, 128), BF16)
    handed.wait()


def scalars_kernel(length_ref, scale_ref, noise_ref, after_ref, out_ref):
    row = lax.broadcasted_iota(jnp.int32, out_ref.shape, 0)
    out_ref[...] = jnp.where(
        row == 0, length_ref[0], jnp.where(row == 1, scale_ref[0], noise_ref[0])
    )


def spread_scalars(lengthscale, outputscale, noise_variance, after):
    return pl.pallas_call(
        scalars_kernel,
        out_shape=jax.ShapeDtypeStruct((8, 128), F32),
        in_specs=[SMEM, SMEM, SMEM, ANY],
        out_specs=VMEM,
        compiler_params=PARAMS,
        name="spread_scalars",
    )(lengthscale, outputscale, noise_variance, after)


def features(sizes, scalars, coordinates, order, direction, after):
    leaf_count = sizes.shape[1]
    points = direction.shape[1]
    return pl.pallas_call(
        functools.partial(features_kernel, leaf_count),
        out_shape=(
            jax.ShapeDtypeStruct((points + STRIP, 128), BF16),
            jax.ShapeDtypeStruct((48, points), BF16),
            jax.ShapeDtypeStruct((points + TILE, 128), BF16),
            pltpu.SMEM((8, 128), jnp.int32),
        ),
        in_specs=[SMEM, VMEM, VMEM, VMEM, VMEM, ANY],
        out_specs=(VMEM, VMEM, VMEM, SMEM),
        scratch_shapes=[
            pltpu.VMEM((8, points), F32),
            pltpu.VMEM((8, 128), jnp.int32),
            pltpu.SemaphoreType.DMA((1,)),
        ],
        compiler_params=PARAMS,
        name="features",
    )(sizes, scalars, coordinates, order.reshape(-1, 128), direction, after)


def strip_spans(ends, tiles):
    begins, counts = [], []
    for tile in range(tiles):
        first = tile * TILE
        last = first + TILE - 1
        low = 0
        high = ends[-1]
        for end in ends:
            low = jnp.where(end <= first, end, low)
        for end in ends[::-1]:
            high = jnp.where(end > last, end, high)
        low = lax.div(low, 128) * 128
        begins.append(low)
        counts.append(lax.div(high - low + (STRIP - 1), STRIP))
    return begins, counts


def near_plan(ends, tiles):
    begins, counts = strip_spans(ends, tiles)
    item = lax.broadcasted_iota(jnp.int32, (8, 128), 1)
    first = 0
    begin = jnp.zeros((8, 128), jnp.int32)
    column = jnp.full((8, 128), tiles * TILE, jnp.int32)
    for tile, (low, count) in enumerate(zip(begins, counts)):
        inside = (item >= first) & (item < first + count)
        begin = jnp.where(inside, low + (item - first) * STRIP, begin)
        column = jnp.where(inside, tile * TILE, column)
        first = first + count
    groups = jnp.full((8, 128), lax.div(first + (GROUP - 1), GROUP), jnp.int32)
    row = lax.broadcasted_iota(jnp.int32, (8, 128), 0)
    return jnp.where(row == 0, begin, jnp.where(row == 1, column, groups))


def near_kernel(part, plan_ref, left_ref, right_ref, dd_ref, *refs):
    out_ref = refs[-1]
    depth, points = right_ref.shape
    groups = plan_ref[2, 0]
    if part == 0:
        out_ref[...] = jnp.zeros_like(out_ref)

    def one_group(group, carry):
        for unit in range(GROUP):
            item = group * GROUP + unit
            begin = plan_ref[0, item]
            column = plan_ref[1, item]
            rows = pl.ds(pl.multiple_of(begin, 128), STRIP)
            source = pl.ds(pl.multiple_of(column, TILE), TILE)
            columns = pl.ds(pl.multiple_of(jnp.minimum(column, points - TILE), TILE), TILE)
            squared = jnp.dot(
                left_ref[rows, :depth], right_ref[:, columns], preferred_element_type=F32
            )
            squared = jnp.maximum(squared, 1e-12)
            root = squared * lax.rsqrt(squared)
            kernel = (squared + root + THIRD) * jnp.exp2(root * DECAY)
            high_part = kernel.astype(BF16)
            low_part = (kernel - high_part.astype(F32)).astype(BF16)
            both = jnp.dot(
                jnp.concatenate([high_part, low_part], axis=0),
                dd_ref[source, :],
                preferred_element_type=F32,
            )
            out_ref[rows, :] += folded(both)
        return carry

    lax.fori_loop(
        lax.div(groups * part, PARTS), lax.div(groups * (part + 1), PARTS), one_group, 0
    )


def near_part(prepared, before, after, part):
    left, right, dd, plan = prepared
    plan = pltpu.with_memory_space_constraint(plan, pltpu.SMEM)
    return pl.pallas_call(
        functools.partial(near_kernel, part),
        out_shape=jax.ShapeDtypeStruct(left.shape, F32),
        in_specs=[SMEM] + [VMEM] * (3 + len(before)) + [ANY],
        out_specs=VMEM,
        input_output_aliases={4: 0} if before else {},
        compiler_params=PARAMS,
        name="near_part",
    )(plan, left, right, dd, *before, after)


def assemble_kernel(scalars_ref, near_ref, d_ref, r_ref, after_ref, base_ref, old_ref):
    probes, points = d_ref.shape
    noise = scalars_ref[2:3, 0:1]
    near_scale = scalars_ref[1:2, 0:1] * 3.0
    old = jnp.zeros((probes, 128), F32)
    for first in range(0, points, 512):
        window = slice(first, first + 512)
        near = folded(near_ref[window, :].T[: 2 * probes])
        base_ref[:, window] = noise * d_ref[:, window] + near_scale * near
        r = r_ref[:, window]
        old = old + lane_sums(r * r)
    old_ref[...] = old


def assemble(scalars, near, direction, residual, after):
    return pl.pallas_call(
        assemble_kernel,
        out_shape=(
            jax.ShapeDtypeStruct(direction.shape, F32),
            jax.ShapeDtypeStruct((direction.shape[0], 128), F32),
        ),
        in_specs=[VMEM] * 4 + [ANY],
        out_specs=(VMEM, VMEM),
        compiler_params=PARAMS,
        name="assemble",
    )(scalars, near, direction, residual, after)


def down_kernel(
    leaf_count,
    levels,
    sizes_ref,
    base_ref,
    old_ref,
    d_ref,
    r_ref,
    basis_ref,
    nt_ref,
    nc_ref,
    high_ref,
    low_ref,
    local_ref,
    *rest,
):
    side_refs = rest[:levels]
    a_ref, sums_ref = rest[levels:]
    probes, points = d_ref.shape
    wide = jnp.concatenate([side_ref[...] for side_ref in side_refs], axis=1)
    down = times_transposed(wide, high_ref[...]) + times_transposed(wide, low_ref[...])
    current = [down]
    while len(current) < leaf_count:
        count = len(current)
        following = []
        for index in range(2 * count):
            node = 2 * count - 1 + index
            parent = index // 2
            following.append(
                times_transposed(
                    jnp.concatenate([current[parent], local_ref[count - 1 + parent]], axis=1),
                    jnp.concatenate([nt_ref[0, node], nc_ref[0, node]], axis=1),
                )
            )
        current = following
    stacked = jnp.concatenate([halves(term) for term in current], axis=0)
    ends = leaf_ends(sizes_ref, leaf_count)
    width = 512
    peak = jnp.zeros((probes, 128), F32)
    curve = jnp.zeros((probes, 128), F32)

    for first in range(0, points, width):
        far_all = jnp.dot(
            stacked, basis_ref[:, first : first + width], preferred_element_type=F32
        )
        leaf = leaf_row(ends, first, (probes, width))
        far = folded(far_all[: 2 * probes])
        for index in range(1, leaf_count):
            term = folded(far_all[2 * probes * index : 2 * probes * (index + 1)])
            far = jnp.where(leaf == index, term, far)
        d = d_ref[:, first : first + width]
        applied = base_ref[:, first : first + width] + far
        a_ref[:, first : first + width] = applied
        size = jnp.abs(applied)
        for i in range(width // 128):
            peak = jnp.maximum(peak, size[:, 128 * i : 128 * i + 128])
        curve = curve + lane_sums(d * applied)
    top = jnp.maximum(jnp.max(peak, axis=1, keepdims=True), 1e-30)
    inverse = 1.0 / top
    cross = jnp.zeros((probes, 128), F32)
    square = jnp.zeros((probes, 128), F32)
    for first in range(0, points, width):
        unit = a_ref[:, first : first + width] * inverse
        cross = cross + lane_sums(r_ref[:, first : first + width] * unit)
        square = square + lane_sums(unit * unit)
    columns = [jnp.sum(x, axis=1, keepdims=True) for x in (old_ref[...], curve, cross, square)]
    lane = lax.broadcasted_iota(jnp.int32, (probes, 128), 1)
    quantity = lax.div(lane, probes)
    own = lax.rem(lane, probes) == lax.broadcasted_iota(jnp.int32, (probes, 128), 0)
    picked = columns[0]
    for index in range(1, 4):
        picked = jnp.where(quantity == index, columns[index], picked)
    row = jnp.concatenate(
        [
            jnp.sum(jnp.where(own, picked, 0.0), axis=0, keepdims=True),
            jnp.sum(jnp.where(own, top, 0.0), axis=0, keepdims=True),
        ],
        axis=1,
    )
    sums_ref[...] = jnp.broadcast_to(row[None], sums_ref.shape)


def descend(
    sizes, base, old, direction, residual, basis, node_transfer, node_coupling,
    images, local, sides,
):
    leaf_count = sizes.shape[1]
    probes, points = direction.shape
    return pl.pallas_call(
        functools.partial(down_kernel, leaf_count, len(sides)),
        out_shape=(
            jax.ShapeDtypeStruct((probes, points), F32),
            jax.ShapeDtypeStruct((2 ** len(sides), 1, 256), F32),
        ),
        in_specs=[SMEM] + [VMEM] * (10 + len(sides)),
        out_specs=(VMEM, VMEM),
        compiler_params=PARAMS,
        name="descend",
    )(
        sizes, base, old, direction, residual, basis,
        node_transfer, node_coupling, *images, local, *sides,
    )


def merged(sums, probes):
    values, tops = sums[:, :, :128], sums[:, :, 128:]
    top = jnp.max(tops, axis=0)
    ratio = tops / top
    quantity = lax.div(lax.broadcasted_iota(jnp.int32, (1, 1, 128), 2), probes)
    factor = jnp.where(quantity < 2, 1.0, jnp.where(quantity == 2, ratio, ratio * ratio))
    return jnp.sum(values * factor, axis=0), top


def step_kernel(sums_ref, x_ref, r_ref, d_ref, a_ref, *refs):
    targets, held, semaphores = refs[:3], refs[3:6], refs[6]
    probes = d_ref.shape[0]
    total, top = merged(sums_ref[...], probes)
    lane = lax.broadcasted_iota(jnp.int32, (probes, 128), 1)
    probe = lax.broadcasted_iota(jnp.int32, (probes, 128), 0)

    def column(row, index):
        return jnp.sum(
            jnp.where(lane == index * probes + probe, row, 0.0), axis=1, keepdims=True
        )

    old, curve, cross, square = (column(total, index) for index in range(4))
    step = old / curve
    reach = step * column(top, 0)
    fresh = old - 2.0 * (reach * cross) + (reach * reach) * square
    beta = fresh / old
    points = d_ref.shape[1]
    width = points // SENDS
    copies = []
    for number in range(SENDS):
        window = pl.ds(width * number, width)
        d = d_ref[:, window]
        remaining = r_ref[:, window] - step * a_ref[:, window]
        held[0][:, window] = x_ref[:, window] + step * d
        held[1][:, window] = remaining
        held[2][:, window] = remaining + beta * d
        for index in range(3):
            copy = pltpu.make_async_copy(
                held[index].at[:, window],
                targets[index].at[:, window],
                semaphores.at[3 * number + index],
            )
            copy.start()
            copies.append(copy)
    for copy in copies:
        copy.wait()


def finish(sums, solution_block, residual, direction, applied):
    shape = jax.ShapeDtypeStruct(direction.shape, F32)
    return pl.pallas_call(
        step_kernel,
        out_shape=(shape, shape, shape),
        in_specs=[VMEM] * 5,
        out_specs=(HBM, HBM, HBM),
        scratch_shapes=[pltpu.VMEM(direction.shape, F32)] * 3
        + [pltpu.SemaphoreType.DMA((3 * SENDS,))],
        compiler_params=PARAMS,
        name="finish",
    )(sums, solution_block, residual, direction, applied)


def from_partner(array, stride):
    count = lax.axis_size("leaf")
    return lax.ppermute(array, "leaf", [(i, i ^ stride) for i in range(count)])


def shards(
    solution,
    residual,
    direction,
    coordinates,
    cluster_order,
    leaf_sizes,
    leaf_basis,
    node_transfer,
    node_coupling,
    upper_transfer,
    upper_coupling,
    lengthscale,
    outputscale,
    noise_variance,
):
    levels = lax.axis_size("leaf").bit_length() - 1
    probes, points = direction.shape
    up, local, high, low, direction, leaf_basis, node_transfer, node_coupling = climb(
        leaf_sizes,
        (direction, leaf_basis, node_transfer, node_coupling, upper_transfer, upper_coupling),
        levels,
    )
    sides = []
    near = ()
    current = up
    for level in range(max(levels, PARTS + 1)):
        if level < levels:
            incoming = from_partner(current, 2**level)
        if level == 0:
            scalars = spread_scalars(lengthscale, outputscale, noise_variance, current)
        if level == 1:
            prepared = features(
                leaf_sizes, scalars, coordinates, cluster_order, direction, current
            )
        if 1 <= level <= PARTS:
            near = (near_part(prepared, near, current, level - 1),)
        if level == PARTS:
            base, old = assemble(scalars, near[0], direction, residual, near[0])
            current, base, old = lax.optimization_barrier((current, base, old))
        if level < levels:
            current = current + incoming
            sides.append(current[0])
            current = current[1:] if level + 1 < levels else current
            if level == 0:
                current, scalars = lax.optimization_barrier((current, scalars))
            elif level < PARTS:
                current, *near = lax.optimization_barrier((current, *near))
    applied, sums = descend(
        leaf_sizes, base, old, direction, residual, leaf_basis,
        node_transfer, node_coupling, (high, low), local, sides,
    )
    gathered = lax.all_to_all(sums, "leaf", 0, 0, tiled=True)
    return finish(gathered, solution, residual, direction, applied)


def solution(mesh):
    in_specs = (
        P(None, "leaf"),
        P(None, "leaf"),
        P(None, "leaf"),
        P(None, "leaf"),
        P("leaf"),
        P("leaf", None),
        P(None, "leaf"),
        P("leaf", None, None, None),
        P("leaf", None, None, None),
        P("leaf", None, None, None),
        P("leaf", None, None, None),
        P(),
        P(),
        P(),
    )
    out_specs = (P(None, "leaf"), P(None, "leaf"), P(None, "leaf"))
    return jax.shard_map(shards, mesh=mesh, in_specs=in_specs, out_specs=out_specs, check_vma=False)
```

```python
import functools
import math

import jax
import jax.numpy as jnp
from jax import lax
from jax.experimental import pallas as pl
from jax.experimental.pallas import tpu as pltpu
from jax.sharding import PartitionSpec as P

F32 = jnp.float32
BF16 = jnp.bfloat16
TILE = 256
FAR_AWAY = 32768.0
THIRD = 1.0 / 3.0
DECAY = -3.0 / math.log(2.0)

VMEM = pl.BlockSpec(memory_space=pltpu.VMEM)
SMEM = pl.BlockSpec(memory_space=pltpu.SMEM)
ANY = pl.BlockSpec(memory_space=pl.ANY)
HBM = pl.BlockSpec(memory_space=pltpu.HBM)
STRIP = 384
GROUP = 4
PARTS = 4
SENDS = 6
PARAMS = pltpu.CompilerParams(vmem_limit_bytes=48 * 1024 * 1024)


def halves(x):
    high = x.astype(BF16)
    low = (x - high.astype(F32)).astype(BF16)
    return jnp.concatenate([high, low], axis=0)


def folded(x):
    rows = x.shape[0] // 2
    return x[:rows] + x[rows:]


def times(x, generator):
    return folded(jnp.dot(halves(x), generator, preferred_element_type=F32))


def times_transposed(x, generator):
    return folded(
        lax.dot_general(
            halves(x), generator, (((1,), (1,)), ((), ())), preferred_element_type=F32
        )
    )


def lane_sums(x):
    return sum(x[:, first : first + 128] for first in range(0, x.shape[1], 128))


def leaf_ends(sizes_ref, leaf_count):
    ends = []
    total = 0
    for leaf in range(leaf_count):
        total = total + sizes_ref[0, leaf]
        ends.append(total)
    return ends


def leaf_row(ends, first, shape):
    positions = lax.broadcasted_iota(jnp.int32, shape, 1) + first
    leaf = jnp.zeros(shape, jnp.int32)
    for end in ends[:-1]:
        leaf = leaf + (positions >= end).astype(jnp.int32)
    return leaf


def up_kernel(leaf_count, levels, *refs):
    sources, (up_ref, local_ref, high_ref, low_ref) = refs[:7], refs[7:11]
    d_ref, basis_ref, nt_ref, nc_ref, plan_ref = refs[11:16]
    sizes_ref, ut_ref, uc_ref, list_ref, semaphores = refs[16:]
    probes, points = d_ref.shape
    copies = [
        pltpu.make_async_copy(source, target, semaphores.at[index])
        for index, (source, target) in enumerate(
            zip(sources, (sizes_ref, d_ref, basis_ref, nt_ref, nc_ref, ut_ref, uc_ref))
        )
    ]
    for copy in copies:
        copy.start()
    copies[0].wait()
    ends = leaf_ends(sizes_ref, leaf_count)
    list_ref[...] = near_plan(ends, points // TILE)
    handed = pltpu.make_async_copy(list_ref, plan_ref, semaphores.at[len(copies)])
    handed.start()
    for copy in copies[1:]:
        copy.wait()
    rank = basis_ref.shape[0]
    images = [nc_ref[0, 0].astype(F32)]
    path = nt_ref[0, 0].astype(F32)
    for level in range(1, levels):
        if level + 1 < levels:
            both = jnp.concatenate([ut_ref[0, level - 1], uc_ref[0, level - 1]], axis=1)
            image = times(path, both)
            path = image[:, :rank]
            images.append(image[:, rank:])
        else:
            images.append(times(path, uc_ref[0, level - 1]))
    images = jnp.concatenate(images, axis=1)
    high = images.astype(BF16)
    low = (images - high.astype(F32)).astype(BF16)
    high_ref[...] = high
    low_ref[...] = low
    split = halves(d_ref[...])
    leaf = leaf_row(ends, 0, split.shape)
    zero = jnp.zeros_like(split)
    masked = jnp.concatenate(
        [jnp.where(leaf == index, split, zero) for index in range(leaf_count)], axis=0
    )
    raw = lax.dot_general(
        masked, basis_ref[...], (((1,), (1,)), ((), ())), preferred_element_type=F32
    )
    current = [
        folded(raw[2 * probes * index : 2 * probes * (index + 1)]) for index in range(leaf_count)
    ]
    while len(current) > 1:
        count = len(current)
        raised, sided = [], []
        for index in range(count):
            node = count - 1 + index
            both = jnp.concatenate([nt_ref[0, node], nc_ref[0, node]], axis=1)
            image = times(current[index], both)
            raised.append(image[:, :rank])
            sided.append(image[:, rank:])
        current = [raised[2 * i] + raised[2 * i + 1] for i in range(count // 2)]
        for i in range(count // 2):
            local_ref[count // 2 - 1 + i] = sided[2 * i] + sided[2 * i + 1]
    image = times(current[0], high) + times(current[0], low)
    for level in range(levels):
        up_ref[level] = image[:, rank * level : rank * (level + 1)]
    handed.wait()


def climb(sizes, vectors, levels):
    leaf_count = sizes.shape[1]
    probes, rank = vectors[0].shape[0], vectors[1].shape[0]
    arrays = (sizes, *vectors)
    return pl.pallas_call(
        functools.partial(up_kernel, leaf_count, levels),
        out_shape=(
            jax.ShapeDtypeStruct((levels, probes, rank), F32),
            jax.ShapeDtypeStruct((leaf_count - 1, probes, rank), F32),
            jax.ShapeDtypeStruct((rank, rank * levels), BF16),
            jax.ShapeDtypeStruct((rank, rank * levels), BF16),
            *(jax.ShapeDtypeStruct(array.shape, array.dtype) for array in vectors[:4]),
            pltpu.SMEM((8, 128), jnp.int32),
        ),
        in_specs=[HBM] * len(arrays),
        out_specs=(VMEM,) * 8 + (SMEM,),
        scratch_shapes=[
            pltpu.SMEM(sizes.shape, sizes.dtype),
            *(pltpu.VMEM(array.shape, array.dtype) for array in vectors[4:]),
            pltpu.VMEM((8, 128), jnp.int32),
            pltpu.SemaphoreType.DMA((len(arrays) + 1,)),
        ],
        compiler_params=PARAMS,
        name="climb",
    )(*(pltpu.with_memory_space_constraint(array, pltpu.HBM) for array in arrays))


def features_kernel(
    leaf_count,
    sizes_ref,
    scalars_ref,
    coords_ref,
    order_ref,
    d_ref,
    after_ref,
    left_ref,
    right_ref,
    dd_ref,
    ordered_ref,
):
    points = coords_ref.shape[1]
    chunks = points // 128
    ends = leaf_ends(sizes_ref, leaf_count)
    ordered_ref[...] = jnp.zeros_like(ordered_ref)
    for group in range(chunks // 8):
        order = order_ref[8 * group : 8 * group + 8, :]
        chunk_of = lax.shift_right_logical(order, 7)
        lane_of = lax.bitwise_and(order, 127)
        for axis in range(3):
            found = jnp.zeros((8, 128), F32)
            for chunk in range(chunks):
                source = jnp.broadcast_to(
                    coords_ref[axis : axis + 1, 128 * chunk : 128 * chunk + 128], (8, 128)
                )
                picked = jnp.take_along_axis(source, lane_of, axis=1)
                found = jnp.where(chunk_of == chunk, picked, found)
            for row in range(8):
                place = 128 * (8 * group + row)
                ordered_ref[axis : axis + 1, place : place + 128] = found[row : row + 1, :]
    row8 = lax.broadcasted_iota(jnp.int32, (8, points), 0)
    scale = (math.sqrt(5.0) / 3.0) / scalars_ref[0:1, 0:1]
    scaled = jnp.where(row8 < 3, (ordered_ref[...] - 0.5) * scale, 0.0)
    z1 = scaled.astype(BF16).astype(F32)
    z2 = (scaled - z1).astype(BF16).astype(F32)
    kept = z1 + z2
    norm = jnp.broadcast_to(jnp.sum(kept * kept, axis=0, keepdims=True), (8, points))
    n1 = norm.astype(BF16).astype(F32)
    n2 = (norm - n1).astype(BF16).astype(F32)
    n3 = norm - n1 - n2
    leaf = leaf_row(ends, 0, (8, points))
    parts = jnp.where(row8 % 3 == 0, n1, jnp.where(row8 % 3 == 1, n2, n3))
    norm_left = jnp.where(row8 < 3, parts, jnp.where(row8 < 6, 1.0, 0.0))
    norm_right = jnp.where(row8 < 3, 1.0, jnp.where(row8 < 6, parts, 0.0))
    same = leaf == row8
    leaf_left = jnp.where(same, 1.0, 0.0)
    leaf_right = jnp.where(same, 0.0, FAR_AWAY)
    left = jnp.concatenate(
        [-2.0 * z1, -2.0 * z1, -2.0 * z2, -2.0 * z2, norm_left, leaf_left]
        + [jnp.zeros((80, points), F32)],
        axis=0,
    )
    right = jnp.concatenate(
        [z1, z2, z1, z2, norm_right, leaf_right], axis=0
    )
    right_ref[...] = right.astype(BF16)
    left_ref[:points, :] = left.T.astype(BF16)
    left_ref[points:, :] = jnp.zeros((STRIP, 128), BF16)
    split = halves(d_ref[...]).astype(F32)
    split = jnp.concatenate([split, jnp.zeros((128 - split.shape[0], points), F32)], axis=0)
    dd_ref[:points, :] = split.T.astype(BF16)
    dd_ref[points:, :] = jnp.zeros((TILE, 128), BF16)


def scalars_kernel(*refs):
    out_ref = refs[-1]
    row = lax.broadcasted_iota(jnp.int32, out_ref.shape, 0)
    spread = jnp.full(out_ref.shape, refs[0][0])
    for index, ref in enumerate(refs[1:-2]):
        spread = jnp.where(row == index + 1, ref[0], spread)
    out_ref[...] = spread


def spread_scalars(scalars, after):
    return pl.pallas_call(
        scalars_kernel,
        out_shape=jax.ShapeDtypeStruct((8, 128), F32),
        in_specs=[SMEM] * len(scalars) + [ANY],
        out_specs=VMEM,
        compiler_params=PARAMS,
        name="spread_scalars",
    )(*scalars, after)


def features(sizes, scalars, coordinates, order, direction, after):
    leaf_count = sizes.shape[1]
    points = direction.shape[1]
    return pl.pallas_call(
        functools.partial(features_kernel, leaf_count),
        out_shape=(
            jax.ShapeDtypeStruct((points + STRIP, 128), BF16),
            jax.ShapeDtypeStruct((48, points), BF16),
            jax.ShapeDtypeStruct((points + TILE, 128), BF16),
        ),
        in_specs=[SMEM, VMEM, VMEM, VMEM, VMEM, ANY],
        out_specs=(VMEM, VMEM, VMEM),
        scratch_shapes=[pltpu.VMEM((8, points), F32)],
        compiler_params=PARAMS,
        name="features",
    )(sizes, scalars, coordinates, order.reshape(-1, 128), direction, after)


def strip_spans(ends, tiles):
    begins, counts = [], []
    for tile in range(tiles):
        first = tile * TILE
        last = first + TILE - 1
        low = 0
        high = ends[-1]
        for end in ends:
            low = jnp.where(end <= first, end, low)
        for end in ends[::-1]:
            high = jnp.where(end > last, end, high)
        low = lax.div(low, 128) * 128
        begins.append(low)
        counts.append(lax.div(high - low + (STRIP - 1), STRIP))
    return begins, counts


def near_plan(ends, tiles):
    begins, counts = strip_spans(ends, tiles)
    item = lax.broadcasted_iota(jnp.int32, (8, 128), 1)
    first = 0
    begin = jnp.zeros((8, 128), jnp.int32)
    column = jnp.full((8, 128), tiles * TILE, jnp.int32)
    for tile, (low, count) in enumerate(zip(begins, counts)):
        inside = (item >= first) & (item < first + count)
        begin = jnp.where(inside, low + (item - first) * STRIP, begin)
        column = jnp.where(inside, tile * TILE, column)
        first = first + count
    groups = jnp.full((8, 128), lax.div(first + (GROUP - 1), GROUP), jnp.int32)
    row = lax.broadcasted_iota(jnp.int32, (8, 128), 0)
    return jnp.where(row == 0, begin, jnp.where(row == 1, column, groups))


def near_kernel(part, plan_ref, left_ref, right_ref, dd_ref, *refs):
    out_ref = refs[-1]
    depth, points = right_ref.shape
    groups = plan_ref[2, 0]
    if part == 0:
        out_ref[...] = jnp.zeros_like(out_ref)

    def one_group(group, carry):
        for unit in range(GROUP):
            item = group * GROUP + unit
            begin = plan_ref[0, item]
            column = plan_ref[1, item]
            rows = pl.ds(pl.multiple_of(begin, 128), STRIP)
            source = pl.ds(pl.multiple_of(column, TILE), TILE)
            columns = pl.ds(pl.multiple_of(jnp.minimum(column, points - TILE), TILE), TILE)
            squared = jnp.dot(
                left_ref[rows, :depth], right_ref[:, columns], preferred_element_type=F32
            )
            squared = jnp.maximum(squared, 1e-12)
            root = squared * lax.rsqrt(squared)
            kernel = (squared + root + THIRD) * jnp.exp2(root * DECAY)
            high_part = kernel.astype(BF16)
            low_part = (kernel - high_part.astype(F32)).astype(BF16)
            both = jnp.dot(
                jnp.concatenate([high_part, low_part], axis=0),
                dd_ref[source, :],
                preferred_element_type=F32,
            )
            out_ref[rows, :] += folded(both)
        return carry

    lax.fori_loop(
        lax.div(groups * part, PARTS), lax.div(groups * (part + 1), PARTS), one_group, 0
    )


def near_part(plan, prepared, before, after, part):
    left, right, dd = prepared
    plan = pltpu.with_memory_space_constraint(plan, pltpu.SMEM)
    return pl.pallas_call(
        functools.partial(near_kernel, part),
        out_shape=jax.ShapeDtypeStruct(left.shape, F32),
        in_specs=[SMEM] + [VMEM] * (3 + len(before)) + [ANY],
        out_specs=VMEM,
        input_output_aliases={4: 0} if before else {},
        compiler_params=PARAMS,
        name="near_part",
    )(plan, left, right, dd, *before, after)


def assemble_kernel(scalars_ref, noise_ref, near_ref, d_ref, r_ref, after_ref, base_ref, old_ref):
    probes, points = d_ref.shape
    noise = noise_ref[0:1, 0:1]
    near_scale = scalars_ref[1:2, 0:1] * 3.0
    old = jnp.zeros((probes, 128), F32)
    for first in range(0, points, 512):
        window = slice(first, first + 512)
        near = folded(near_ref[window, :].T[: 2 * probes])
        base_ref[:, window] = noise * d_ref[:, window] + near_scale * near
        r = r_ref[:, window]
        old = old + lane_sums(r * r)
    old_ref[...] = old


def assemble(scalars, noise, near, direction, residual, after):
    return pl.pallas_call(
        assemble_kernel,
        out_shape=(
            jax.ShapeDtypeStruct(direction.shape, F32),
            jax.ShapeDtypeStruct((direction.shape[0], 128), F32),
        ),
        in_specs=[VMEM] * 5 + [ANY],
        out_specs=(VMEM, VMEM),
        compiler_params=PARAMS,
        name="assemble",
    )(scalars, noise, near, direction, residual, after)


def down_kernel(
    leaf_count,
    levels,
    sizes_ref,
    base_ref,
    old_ref,
    d_ref,
    r_ref,
    basis_ref,
    nt_ref,
    nc_ref,
    high_ref,
    low_ref,
    local_ref,
    *rest,
):
    side_refs = rest[:levels]
    a_ref, sums_ref = rest[levels:]
    probes, points = d_ref.shape
    wide = jnp.concatenate([side_ref[...] for side_ref in side_refs], axis=1)
    down = times_transposed(wide, high_ref[...]) + times_transposed(wide, low_ref[...])
    current = [down]
    while len(current) < leaf_count:
        count = len(current)
        following = []
        for index in range(2 * count):
            node = 2 * count - 1 + index
            parent = index // 2
            following.append(
                times_transposed(
                    jnp.concatenate([current[parent], local_ref[count - 1 + parent]], axis=1),
                    jnp.concatenate([nt_ref[0, node], nc_ref[0, node]], axis=1),
                )
            )
        current = following
    stacked = jnp.concatenate([halves(term) for term in current], axis=0)
    ends = leaf_ends(sizes_ref, leaf_count)
    width = 512
    peak = jnp.zeros((probes, 128), F32)
    curve = jnp.zeros((probes, 128), F32)

    for first in range(0, points, width):
        far_all = jnp.dot(
            stacked, basis_ref[:, first : first + width], preferred_element_type=F32
        )
        leaf = leaf_row(ends, first, (probes, width))
        far = folded(far_all[: 2 * probes])
        for index in range(1, leaf_count):
            term = folded(far_all[2 * probes * index : 2 * probes * (index + 1)])
            far = jnp.where(leaf == index, term, far)
        d = d_ref[:, first : first + width]
        applied = base_ref[:, first : first + width] + far
        a_ref[:, first : first + width] = applied
        size = jnp.abs(applied)
        for i in range(width // 128):
            peak = jnp.maximum(peak, size[:, 128 * i : 128 * i + 128])
        curve = curve + lane_sums(d * applied)
    top = jnp.maximum(jnp.max(peak, axis=1, keepdims=True), 1e-30)
    inverse = 1.0 / top
    cross = jnp.zeros((probes, 128), F32)
    square = jnp.zeros((probes, 128), F32)
    for first in range(0, points, width):
        unit = a_ref[:, first : first + width] * inverse
        cross = cross + lane_sums(r_ref[:, first : first + width] * unit)
        square = square + lane_sums(unit * unit)
    columns = [jnp.sum(x, axis=1, keepdims=True) for x in (old_ref[...], curve, cross, square)]
    lane = lax.broadcasted_iota(jnp.int32, (probes, 128), 1)
    quantity = lax.div(lane, probes)
    own = lax.rem(lane, probes) == lax.broadcasted_iota(jnp.int32, (probes, 128), 0)
    picked = columns[0]
    for index in range(1, 4):
        picked = jnp.where(quantity == index, columns[index], picked)
    row = jnp.concatenate(
        [
            jnp.sum(jnp.where(own, picked, 0.0), axis=0, keepdims=True),
            jnp.sum(jnp.where(own, top, 0.0), axis=0, keepdims=True),
        ],
        axis=1,
    )
    sums_ref[...] = jnp.broadcast_to(row[None], sums_ref.shape)


def descend(
    sizes, base, old, direction, residual, basis, node_transfer, node_coupling,
    images, local, sides,
):
    leaf_count = sizes.shape[1]
    probes, points = direction.shape
    return pl.pallas_call(
        functools.partial(down_kernel, leaf_count, len(sides)),
        out_shape=(
            jax.ShapeDtypeStruct((probes, points), F32),
            jax.ShapeDtypeStruct((2 ** len(sides), 1, 256), F32),
        ),
        in_specs=[SMEM] + [VMEM] * (10 + len(sides)),
        out_specs=(VMEM, VMEM),
        compiler_params=PARAMS,
        name="descend",
    )(
        sizes, base, old, direction, residual, basis,
        node_transfer, node_coupling, *images, local, *sides,
    )


def merged(sums, probes):
    values, tops = sums[:, :, :128], sums[:, :, 128:]
    top = jnp.max(tops, axis=0)
    ratio = tops / top
    quantity = lax.div(lax.broadcasted_iota(jnp.int32, (1, 1, 128), 2), probes)
    factor = jnp.where(quantity < 2, 1.0, jnp.where(quantity == 2, ratio, ratio * ratio))
    return jnp.sum(values * factor, axis=0), top


def step_kernel(sums_ref, x_ref, r_ref, d_ref, a_ref, *refs):
    targets, held, semaphores = refs[:3], refs[3:6], refs[6]
    probes = d_ref.shape[0]
    total, top = merged(sums_ref[...], probes)
    lane = lax.broadcasted_iota(jnp.int32, (probes, 128), 1)
    probe = lax.broadcasted_iota(jnp.int32, (probes, 128), 0)

    def column(row, index):
        return jnp.sum(
            jnp.where(lane == index * probes + probe, row, 0.0), axis=1, keepdims=True
        )

    old, curve, cross, square = (column(total, index) for index in range(4))
    step = old / curve
    reach = step * column(top, 0)
    fresh = old - 2.0 * (reach * cross) + (reach * reach) * square
    beta = fresh / old
    points = d_ref.shape[1]
    width = points // SENDS
    copies = []
    for number in range(SENDS):
        window = pl.ds(width * number, width)
        d = d_ref[:, window]
        remaining = r_ref[:, window] - step * a_ref[:, window]
        held[0][:, window] = x_ref[:, window] + step * d
        held[1][:, window] = remaining
        held[2][:, window] = remaining + beta * d
        for index in range(3):
            copy = pltpu.make_async_copy(
                held[index].at[:, window],
                targets[index].at[:, window],
                semaphores.at[3 * number + index],
            )
            copy.start()
            copies.append(copy)
    for copy in copies:
        copy.wait()


def finish(sums, solution_block, residual, direction, applied):
    shape = jax.ShapeDtypeStruct(direction.shape, F32)
    return pl.pallas_call(
        step_kernel,
        out_shape=(shape, shape, shape),
        in_specs=[VMEM] * 5,
        out_specs=(HBM, HBM, HBM),
        scratch_shapes=[pltpu.VMEM(direction.shape, F32)] * 3
        + [pltpu.SemaphoreType.DMA((3 * SENDS,))],
        compiler_params=PARAMS,
        name="finish",
    )(sums, solution_block, residual, direction, applied)


def from_partner(array, stride):
    count = lax.axis_size("leaf")
    return lax.ppermute(array, "leaf", [(i, i ^ stride) for i in range(count)])


def shards(
    solution,
    residual,
    direction,
    coordinates,
    cluster_order,
    leaf_sizes,
    leaf_basis,
    node_transfer,
    node_coupling,
    upper_transfer,
    upper_coupling,
    lengthscale,
    outputscale,
    noise_variance,
):
    levels = lax.axis_size("leaf").bit_length() - 1
    probes, points = direction.shape
    up, local, high, low, direction, leaf_basis, node_transfer, node_coupling, plan = climb(
        leaf_sizes,
        (direction, leaf_basis, node_transfer, node_coupling, upper_transfer, upper_coupling),
        levels,
    )
    sides = []
    near = ()
    current = up
    for level in range(max(levels, PARTS + 1)):
        if level < levels:
            incoming = from_partner(current, 2**level)
        if level == 0:
            scalars = spread_scalars((lengthscale, outputscale), current)
        if level == 1:
            noise = spread_scalars((noise_variance,), current)
            prepared = features(
                leaf_sizes, scalars, coordinates, cluster_order, direction, current
            )
        if 1 <= level <= PARTS:
            near = (near_part(plan, prepared, near, current, level - 1),)
        if level == PARTS:
            base, old = assemble(scalars, noise, near[0], direction, residual, near[0])
            current, base, old = lax.optimization_barrier((current, base, old))
        if level < levels:
            current = current + incoming
            sides.append(current[0])
            current = current[1:] if level + 1 < levels else current
            if level == 0:
                current, scalars = lax.optimization_barrier((current, scalars))
            elif level == 1:
                current, noise, *near = lax.optimization_barrier((current, noise, *near))
            elif level < PARTS:
                current, *near = lax.optimization_barrier((current, *near))
    applied, sums = descend(
        leaf_sizes, base, old, direction, residual, leaf_basis,
        node_transfer, node_coupling, (high, low), local, sides,
    )
    gathered = lax.all_to_all(sums, "leaf", 0, 0, tiled=True)
    return finish(gathered, solution, residual, direction, applied)


def solution(mesh):
    in_specs = (
        P(None, "leaf"),
        P(None, "leaf"),
        P(None, "leaf"),
        P(None, "leaf"),
        P("leaf"),
        P("leaf", None),
        P(None, "leaf"),
        P("leaf", None, None, None),
        P("leaf", None, None, None),
        P("leaf", None, None, None),
        P("leaf", None, None, None),
        P(),
        P(),
        P(),
    )
    out_specs = (P(None, "leaf"), P(None, "leaf"), P(None, "leaf"))
    return jax.shard_map(shards, mesh=mesh, in_specs=in_specs, out_specs=out_specs, check_vma=False)
```
